32 devices in a mesh: groups: 2 (over x), node: 16 (over z, y, core).
Axes of the slice: x: 2, y: 2, z: 4, core: 2. Of those that a mesh axis runs over, the one named last changes fastest.
Arguments:
- hidden: bfloat16 [4096, 4096], P(('groups', 'node')), parts along dimension 0, may hold values from -6 to 6
- queries: bfloat16 [4096, 4096], P(('groups', 'node')), parts along dimension 0, may hold values from -64 to 64
- kv_weight: bfloat16 [4096, 1024], P(None, 'node'), may hold values from -0.09375 to 0.09375
- doc_ids: int32 [4096], P('groups'), parts along dimension 0, may hold values from 0 to 2, never falling along the last dimension, each value on 1 to 1536 neighbouring positions
Outputs:
- attended: bfloat16 [4096, 4096], P(('groups', 'node')), parts along dimension 0
The draws below stay inside these ranges and needn't reach their ends.
There are 2 independent parts, one for each index of `groups`. The reference program is written for one: setup_inputs(seed, part) draws one part's arguments, and reference() takes and returns one part's arrays. A program takes and returns all parts, laid end to end along the dimension named above; an argument that names none is the same for every part. Nothing has to cross between parts.
All inputs are finite; a program needn't handle non-finite values.
Results may differ from the reference program's by a relative error of at most 0.0035.
The reference program's roundings to bfloat16 on the way (of `keys`, `values` and `weight`) count: a program that leaves them out, or rounds other values in their place, can miss the bound.
Values may be sent and summed in bfloat16 or wider, within the bound.
No kernel may reach another device: no remote copies, remote signals or barrier semaphores. Data moves between devices by JAX's collectives and lax.ppermute only.
A program may use at most 128 MiB of HBM per device.

```python
import math
import jax
import jax.numpy as jnp
import numpy as np
from jax import lax

DW = 4096
KVH = 4
QPK = 8
HD = 128
DOCS = 3
TOKENS = 2048


def draw_queries(key, part):
    key = jax.random.fold_in(key, 11)
    values = jnp.clip(jax.random.normal(key, (TOKENS, KVH * QPK * HD), jnp.float32), -6.0, 6.0)
    return values.astype(jnp.bfloat16)


def block_levels(rng, dims, cuts, low, high):
    def one(axis_at, blocks):
        heights = jax.random.uniform(jax.random.fold_in(jax.random.fold_in(rng, 6), axis_at), (blocks,), jnp.float32, low / len(cuts), high / len(cuts))
        return jnp.repeat(jnp.exp(heights), dims[axis_at] // blocks).reshape((-1,) + (1,) * (len(dims) - axis_at - 1))

    loudness = one(*cuts[0])
    for cut in cuts[1:]:
        loudness = loudness * one(*cut)
    return loudness


def split_up(amount, total, most, skew):
    portions = [(1 << 20) // math.isqrt(grade ** skew) + 1 for grade in range(2, amount + 1)]
    rest, counts = total - most - (amount - 1), [1] * (amount - 1)
    while rest > 0:
        candidates = [i for i in range(amount - 1) if counts[i] < most]
        whole, left = sum([portions[i] for i in candidates]), rest
        for i in candidates:
            more = min(most - counts[i], max(1, left * portions[i] // whole), rest)
            counts[i] = counts[i] + more
            rest = rest - more
    return np.array([most] + counts)


def ragged_sizes(own_key, amount, total, bound, lean):
    if amount == 2:
        one = jax.random.randint(own_key, (), max(1, total - bound), min(bound, total - 1) + 1)
        return jnp.stack([one, total - one])
    sizes = jnp.asarray(split_up(amount, total, bound, lean), jnp.int32)
    twos = (amount - 1) // 2
    giver, sink = sizes[1:1 + 2 * twos:2], sizes[2:2 + 2 * twos:2]
    slack = jnp.minimum(giver - 1, bound - sink)
    moved = jax.random.randint(jax.random.fold_in(own_key, 1), (twos,), 0, 1 << 20) % (slack + 1)
    sizes = sizes.at[1:1 + 2 * twos:2].set(giver - moved).at[2:2 + 2 * twos:2].set(sink + moved)
    return sizes[jax.random.permutation(jax.random.fold_in(own_key, 2), amount)]


def gaussian(rng, shape, width, most, cuts=(), kind=jnp.bfloat16):
    array = jax.random.normal(rng, shape, jnp.float32) * width
    if len(cuts) > 0:
        array = block_levels(rng, shape, cuts, -0.22, 0.18) * array
    return jnp.clip(array, min=-most, max=most).astype(kind)


def setup_inputs(seed: int = 0, part: int = 0) -> dict:
    key_list = jax.random.split(jax.random.key(seed), 5)
    own_keys = jax.random.split(jax.random.fold_in(key_list[4], part), 5)
    return {
        "hidden": gaussian(own_keys[0], (TOKENS, DW), 1.0, 6.0, ((0, 16),)),
        "queries": draw_queries(jax.random.fold_in(jax.random.fold_in(key_list[4], part), 71), part),
        "kv_weight": gaussian(key_list[2], (DW, 2 * KVH * HD), DW ** -0.5, 0.09375, ((1, 16),)),
        "doc_ids": jnp.searchsorted(jnp.cumsum(ragged_sizes(own_keys[3], DOCS, TOKENS, 3 * TOKENS // 4, 0)), jnp.arange(TOKENS), side="right").astype(jnp.int32),
    }


def rotate_keys(keys, positions):
    half = keys.shape[-1] // 2
    freqs = 500000.0 ** (-(jnp.arange(half).astype(jnp.float32) * 2.0) / keys.shape[-1])
    angle = positions[:, None] * freqs[None, :]
    cosine = jnp.cos(angle)[:, None, :]
    sine = jnp.sin(angle)[:, None, :]
    first = keys[..., :half]
    second = keys[..., half:]
    return jnp.concatenate([first * cosine - second * sine, second * cosine + first * sine], axis=-1)


def reference(hidden, queries, kv_weight, doc_ids):
    projected = jnp.dot(hidden, kv_weight, preferred_element_type=jnp.float32)
    split = KVH * HD
    positions = jnp.arange(TOKENS).astype(jnp.float32)
    keys = rotate_keys(projected[:, :split].reshape(TOKENS, KVH, HD), positions).astype(jnp.bfloat16)
    values = projected[:, split:].reshape(TOKENS, KVH, HD).astype(jnp.bfloat16)
    keys_f = keys.astype(jnp.float32)
    values_f = values.astype(jnp.float32)
    block = math.gcd(TOKENS, 128)
    nblocks = TOKENS // block
    query_blocks = queries.reshape(nblocks, block, KVH, QPK, HD)
    key_pos = jnp.arange(TOKENS).astype(jnp.int32)
    scale = HD ** -0.5

    def one_block(item):
        index, qblock = item
        qpos = (index * block + jnp.arange(block)).astype(jnp.int32)
        qdoc = lax.dynamic_slice_in_dim(doc_ids, (index * block).astype(jnp.int32), block)
        score = jnp.einsum('qgph,kgh->qgpk', qblock.astype(jnp.float32), keys_f) * scale
        mask = (qdoc[:, None] == doc_ids[None, :]) & (key_pos[None, :] <= qpos[:, None])
        score = jnp.where(mask[:, None, None, :], score, -1e30)
        top = jnp.max(score, axis=-1, keepdims=True)
        expo = jnp.where(mask[:, None, None, :], jnp.exp(score - top), 0.0)
        total = jnp.sum(expo, axis=-1)
        weight = expo.astype(jnp.bfloat16).astype(jnp.float32)
        out = jnp.einsum('qgpk,kgh->qgph', weight, values_f) / total[..., None]
        return out.reshape(block, KVH * QPK * HD).astype(jnp.bfloat16)

    result = lax.map(one_block, (jnp.arange(nblocks).astype(jnp.int32), query_blocks))
    return result.reshape(TOKENS, KVH * QPK * HD)
```

```python
import math

import jax
import jax.numpy as jnp
from jax import lax
from jax.experimental import pallas as pl
from jax.experimental.pallas import tpu as pltpu
from jax.sharding import PartitionSpec as P

KVH = 4
QPK = 8
HD = 128
AXES = ("groups", "node")
MASKED = -1e30
EXP2_SCALE = HD ** (-0.5) * math.log2(math.e)
VMEM_LIMIT = 56 * 1024 * 1024

ANY = pl.BlockSpec(memory_space=pl.ANY)
IN_SMEM = pl.BlockSpec(memory_space=pltpu.SMEM)
IN_VMEM = pl.BlockSpec(memory_space=pltpu.VMEM)


def rope_tables(positions):
    half = HD // 2
    freqs = 500000.0 ** (-(jnp.arange(half).astype(jnp.float32) * 2.0) / HD)
    angle = positions.astype(jnp.float32)[:, None] * freqs[None, :]
    return jnp.cos(angle), jnp.sin(angle)


def attend_kernel(rows, chunk, n_arrays, place_ref, qdoc_ref, kdoc_ref, *refs):
    q_ref = refs[0]
    arrays = refs[1 : 1 + n_arrays]
    out_ref = refs[1 + n_arrays]
    kv, qv, acc, stat_m, stat_l, bias, sem, qsem = refs[2 + n_arrays :]
    first_chunk, end_chunk, stride = place_ref[0], place_ref[1], place_ref[2]
    me = place_ref[3]
    blocks = arrays[0].shape[1]

    q_copy = pltpu.make_async_copy(q_ref, qv, qsem)
    q_copy.start()

    def copies(a):
        base = 4 + 3 * a
        out = []
        for b in range(blocks):
            at = place_ref[base + 2] + b * stride
            out.append(
                pltpu.make_async_copy(
                    arrays[a].at[:, b],
                    kv.at[
                        place_ref[base + 1],
                        :,
                        pl.ds(pl.multiple_of(at * rows, rows), rows),
                    ],
                    sem.at[a, b],
                )
            )
        return out

    for a in range(n_arrays):

        @pl.when(place_ref[4 + 3 * a] == 1)
        def _():
            for c in copies(a):
                c.start()

    stat_m[...] = jnp.full_like(stat_m, MASKED)
    stat_l[...] = jnp.zeros_like(stat_l)
    acc[...] = jnp.zeros_like(acc)
    q_copy.wait()
    for a in range(n_arrays):

        @pl.when(place_ref[4 + 3 * a] == 1)
        def _():
            for c in copies(a):
                c.wait()

    qdoc = qdoc_ref[...]
    q_pos = me * rows + lax.broadcasted_iota(jnp.int32, (chunk, rows), 1)

    @pl.loop(first_chunk, end_chunk)
    def _(t):
        begin = pl.multiple_of(t * chunk, chunk)
        k_pos = begin + lax.broadcasted_iota(jnp.int32, (chunk, rows), 0)
        kdoc = kdoc_ref[pl.ds(begin, chunk), :]
        seen = (k_pos <= q_pos) & (kdoc == qdoc)
        bias[...] = jnp.where(seen, 0.0, MASKED)
        for g in range(KVH):
            keys = kv[g % 2, g // 2, pl.ds(begin, chunk), :]
            values_t = kv[g % 2, 2 + g // 2, pl.ds(begin, chunk), :].T
            for p in range(QPK):
                h = g * QPK + p
                query = qv[:, h * HD : (h + 1) * HD]
                score = lax.dot_general(
                    keys, query, (((1,), (1,)), ((), ())), preferred_element_type=jnp.float32
                )
                score = score + bias[...]
                old = stat_m[h : h + 1, :]
                top = jnp.maximum(old, jnp.max(score, axis=0, keepdims=True))
                expo = jnp.exp2((score - top) * EXP2_SCALE)
                factor = jnp.exp2((old - top) * EXP2_SCALE)
                stat_m[h : h + 1, :] = top
                stat_l[h : h + 1, :] = stat_l[h : h + 1, :] * factor + jnp.sum(
                    expo, axis=0, keepdims=True
                )
                part = jnp.dot(
                    values_t, expo.astype(jnp.bfloat16), preferred_element_type=jnp.float32
                )
                acc[h] = acc[h] * factor + part

    for h in range(KVH * QPK):
        whole = acc[h] / stat_l[h : h + 1, :]
        out_ref[:, h * HD : (h + 1) * HD] = whole.T.astype(jnp.bfloat16)


def attend(queries, doc_ids, me, arrays, places, stride):
    rows = queries.shape[0]
    tokens = doc_ids.shape[0]
    chunk = math.gcd(tokens, 512)
    my_docs = lax.dynamic_slice_in_dim(doc_ids, me * rows, rows)
    first_key = jnp.sum((doc_ids < my_docs[0]).astype(jnp.int32))
    heads = [first_key // chunk, (me * rows + rows + chunk - 1) // chunk, stride, me]
    for used, kind, at in places:
        heads += [used, kind, at]
    place = jnp.stack([jnp.asarray(v).astype(jnp.int32) for v in heads])
    n = len(arrays)
    qdoc = my_docs.reshape(1, rows)
    kdoc = jnp.broadcast_to(doc_ids.reshape(tokens, 1), (tokens, HD))
    return pl.pallas_call(
        lambda *refs: attend_kernel(rows, chunk, n, *refs),
        out_shape=jax.ShapeDtypeStruct(queries.shape, jnp.bfloat16),
        in_specs=[IN_SMEM, IN_VMEM, IN_VMEM, ANY] + [ANY] * n,
        out_specs=IN_VMEM,
        scratch_shapes=[
            pltpu.VMEM((2, KVH, tokens, HD), jnp.bfloat16),
            pltpu.VMEM(queries.shape, jnp.bfloat16),
            pltpu.VMEM((KVH * QPK, HD, rows), jnp.float32),
            pltpu.VMEM((KVH * QPK, rows), jnp.float32),
            pltpu.VMEM((KVH * QPK, rows), jnp.float32),
            pltpu.VMEM((chunk, rows), jnp.float32),
            pltpu.SemaphoreType.DMA((n, arrays[0].shape[1])),
            pltpu.SemaphoreType.DMA,
        ],
        compiler_params=pltpu.CompilerParams(vmem_limit_bytes=VMEM_LIMIT),
        cost_estimate=pl.CostEstimate(
            flops=2 * rows * tokens * HD * KVH * QPK * 2,
            bytes_accessed=8 * 1024 * 1024,
            transcendentals=rows * tokens * KVH * QPK,
        ),
        name="attend",
    )(place, qdoc, kdoc, queries, *arrays)


def project_kernel(rows, n_pieces, place_ref, cos_ref, sin_ref, *refs):
    hidden = refs[:2]
    pieces = refs[2 : 2 + n_pieces]
    out_ref = refs[2 + n_pieces]
    hbuf, wbuf, hsem, wsem = refs[3 + n_pieces :]
    half = HD // 2
    started = []
    for i in range(2):
        at = place_ref[0] if i == 0 else rows - place_ref[0]
        started.append(
            pltpu.make_async_copy(
                hidden[i], hbuf.at[pl.ds(pl.multiple_of(at, rows), rows)], hsem.at[i]
            )
        )
    for i in range(n_pieces):
        size = pieces[i].shape[0]
        started.append(
            pltpu.make_async_copy(
                pieces[i],
                wbuf.at[pl.ds(pl.multiple_of(place_ref[5 + i], size), size)],
                wsem.at[i],
            )
        )
    for c in started:
        c.start()
    for c in started:
        c.wait()
    for pair in range(2):
        both = lax.dot_general(
            hbuf[...],
            wbuf[pair * 2 * HD : (pair + 1) * 2 * HD, :],
            (((1,), (1,)), ((), ())),
            preferred_element_type=jnp.float32,
        )
        for s in range(2):
            head = place_ref[1 + pair * 2 + s]
            a = both[:, s * HD : s * HD + half]
            b = both[:, s * HD + half : (s + 1) * HD]
            kind = head // 2
            cosine = cos_ref[kind]
            sine = sin_ref[kind]
            turned = jnp.concatenate([a * cosine - b * sine, b * cosine + a * sine], axis=-1)
            out_ref[head] = turned.astype(jnp.bfloat16).reshape(2, rows, HD)


def project(hidden, other, row, slots, pieces, cos, sin):
    rows, depth = hidden.shape
    place = [row] + list(slots) + [at for _, at in pieces]
    place = jnp.stack([jnp.asarray(v).astype(jnp.int32) for v in place])
    n = len(pieces)
    return pl.pallas_call(
        lambda *refs: project_kernel(rows, n, *refs),
        out_shape=jax.ShapeDtypeStruct((4, 2, rows, HD), jnp.bfloat16),
        in_specs=[IN_SMEM, IN_VMEM, IN_VMEM] + [ANY] * (2 + n),
        out_specs=IN_VMEM,
        scratch_shapes=[
            pltpu.VMEM((2 * rows, depth), jnp.bfloat16),
            pltpu.VMEM((4 * HD, depth), jnp.bfloat16),
            pltpu.SemaphoreType.DMA((2,)),
            pltpu.SemaphoreType.DMA((n,)),
        ],
        compiler_params=pltpu.CompilerParams(vmem_limit_bytes=VMEM_LIMIT),
        cost_estimate=pl.CostEstimate(
            flops=2 * 2 * rows * depth * 4 * HD,
            bytes_accessed=7 * 1024 * 1024,
            transcendentals=0,
        ),
        name="project",
    )(place, cos, sin, hidden, other, *[p for p, _ in pieces])


def by_planes(hidden, queries, kv_weight, doc_ids):
    rows = hidden.shape[0]
    width = kv_weight.shape[1]
    x = lax.axis_index("groups")
    node = lax.axis_index("node")
    z, y, c = node // 4, (node // 2) % 2, node % 2

    def hop(fn):
        pairs = []
        for i in range(32):
            to = fn(i // 16, (i // 4) % 4, (i // 2) % 2, i % 2)
            if to is not None:
                pairs.append((i, ((to[0] * 4 + to[1]) * 2 + to[2]) * 2 + to[3]))
        return lambda v: lax.ppermute(v, AXES, pairs)

    to_core = hop(lambda x, z, y, c: (x, z, y, 1 - c))
    to_y = hop(lambda x, z, y, c: (x, z, 1 - y, c))
    to_x = hop(lambda x, z, y, c: (1 - x, z, y, c))
    to_z = {k: hop(lambda x, z, y, c, k=k: (x, z ^ k, y, c)) for k in (1, 2, 3)}
    up = {
        k: hop(lambda x, z, y, c, k=k: (x, z + k, y, c) if z + k < 4 else None) for k in (1, 2, 3)
    }

    weight = kv_weight.T
    part = width // 2
    mine = lax.dynamic_slice_in_dim(weight, x * part, part, 0)
    from_z = {k: to_z[k](mine) for k in (3, 2, 1)}
    other_hidden = to_y(hidden)
    pieces = [(weight, c * width), (to_core(weight), (1 - c) * width)]
    for k in (3, 2, 1):
        base = k * HD
        w = from_z[k]
        w_x = to_x(w)
        pieces.append((w, base + c * width + x * part))
        pieces.append((w_x, base + c * width + (1 - x) * part))
        pieces.append((to_core(w), base + (1 - c) * width + x * part))
        pieces.append((to_core(w_x), base + (1 - c) * width + (1 - x) * part))

    token_blocks = 4 * z + 2 * jnp.arange(2) + c
    positions = (token_blocks[:, None] * rows + jnp.arange(rows)[None, :]).reshape(-1)
    cosine, sine = rope_tables(positions)
    cos = jnp.stack([cosine, jnp.ones_like(cosine)])
    sin = jnp.stack([sine, jnp.zeros_like(sine)])
    kv = project(hidden, other_hidden, y * rows, [z ^ k for k in range(4)], pieces, cos, sin)

    arrays, places = [], []
    for k in range(4):
        below = kv if k == 0 else up[k](kv)
        across = to_y(below)
        used = z - k >= 0
        at = 4 * jnp.maximum(z - k, 0)
        for array, kind, core in (
            (below, y, c),
            (to_core(below), y, 1 - c),
            (across, 1 - y, c),
            (to_core(across), 1 - y, 1 - c),
        ):
            arrays.append(array)
            places.append((used, kind, at + core))
    return attend(queries, doc_ids, node, arrays, places, 2)


def by_gathers(hidden, queries, kv_weight, doc_ids):
    rows = hidden.shape[0]
    me = lax.axis_index("node")
    whole = lax.all_gather(kv_weight, "node", axis=1, tiled=True)
    projected = jnp.dot(hidden, whole, preferred_element_type=jnp.float32)
    split = whole.shape[1] // 2
    cosine, sine = rope_tables(me * rows + jnp.arange(rows))
    keys = projected[:, :split].reshape(rows, KVH, HD)
    a, b = keys[..., : HD // 2], keys[..., HD // 2 :]
    cosine, sine = cosine[:, None, :], sine[:, None, :]
    keys = jnp.concatenate([a * cosine - b * sine, b * cosine + a * sine], axis=-1)
    both = jnp.concatenate([keys, projected[:, split:].reshape(rows, KVH, HD)], axis=1)
    both = both.astype(jnp.bfloat16).transpose(1, 0, 2)
    whole = lax.all_gather(both, "node", axis=1, tiled=True)
    tokens = whole.shape[1]
    whole = whole.reshape(2, 2, 2, tokens // rows, rows, HD)
    arrays = [whole[:, :, kind].reshape(4, tokens // rows, rows, HD) for kind in range(2)]
    return attend(queries, doc_ids, me, arrays, [(1, 0, 0), (1, 1, 0)], 1)


def solution(mesh):
    planes = mesh.shape["groups"] == 2 and mesh.shape["node"] == 16
    in_specs = (P(AXES, None), P(AXES, None), P(None, "node"), P("groups"))
    return jax.shard_map(
        by_planes if planes else by_gathers,
        mesh=mesh,
        in_specs=in_specs,
        out_specs=P(AXES, None),
        check_vma=False,
    )
```

```python
import math

import jax
import jax.numpy as jnp
from jax import lax
from jax.experimental import pallas as pl
from jax.experimental.pallas import tpu as pltpu
from jax.sharding import PartitionSpec as P

KVH = 4
QPK = 8
HD = 128
AXES = ("groups", "node")
MASKED = -1e30
EXP2_SCALE = HD ** (-0.5) * math.log2(math.e)
VMEM_LIMIT = 48 * 1024 * 1024

ANY = pl.BlockSpec(memory_space=pl.ANY)
IN_SMEM = pl.BlockSpec(memory_space=pltpu.SMEM)
IN_VMEM = pl.BlockSpec(memory_space=pltpu.VMEM)


def scalars(*values):
    return jnp.stack([jnp.asarray(v).astype(jnp.int32) for v in values])


def rope_tables(positions):
    half = HD // 2
    freqs = 500000.0 ** (-(jnp.arange(half).astype(jnp.float32) * 2.0) / HD)
    angle = positions.astype(jnp.float32)[:, None] * freqs[None, :]
    return jnp.cos(angle), jnp.sin(angle)


def attend_kernel(rows, chunk, n_q, n_kv, place_ref, start_ref, *refs):
    queries = refs[:n_q]
    arrays = refs[n_q : n_q + n_kv]
    outs = refs[n_q + n_kv : 2 * n_q + n_kv]
    kv, qv, whole, acc, stat_m, stat_l, bias, sem, qsem = refs[2 * n_q + n_kv :]
    part_rows = queries[0].shape[0]
    length = arrays[0].shape[0]

    def q_copy(i):
        column = pl.multiple_of(place_ref[4 + 2 * i], HD)
        return pltpu.make_async_copy(
            queries[i].at[:, pl.ds(column, QPK * HD)],
            qv.at[pl.ds(pl.multiple_of(place_ref[3 + 2 * i], part_rows), part_rows)],
            qsem.at[i],
        )

    def kv_copy(i):
        base = 3 + 2 * n_q + 3 * i
        return pltpu.make_async_copy(
            arrays[i],
            kv.at[place_ref[base + 1], pl.ds(pl.multiple_of(place_ref[base + 2], length), length)],
            sem.at[i],
        )

    for i in range(n_q):
        q_copy(i).start()
    for i in range(n_kv):

        @pl.when(place_ref[3 + 2 * n_q + 3 * i] == 1)
        def _():
            kv_copy(i).start()

    stat_m[...] = jnp.full_like(stat_m, MASKED)
    stat_l[...] = jnp.zeros_like(stat_l)
    acc[...] = jnp.zeros_like(acc)
    for i in range(n_q):
        q_copy(i).wait()
    for i in range(n_kv):

        @pl.when(place_ref[3 + 2 * n_q + 3 * i] == 1)
        def _():
            kv_copy(i).wait()

    starts = start_ref[...]
    q_pos = place_ref[2] + lax.broadcasted_iota(jnp.int32, (chunk, rows), 1)

    @pl.loop(place_ref[0], place_ref[1])
    def _(t):
        begin = pl.multiple_of(t * chunk, chunk)
        k_pos = begin + lax.broadcasted_iota(jnp.int32, (chunk, rows), 0)
        bias[...] = jnp.where((k_pos <= q_pos) & (k_pos >= starts), 0.0, MASKED)
        keys = kv[0, pl.ds(begin, chunk), :]
        values_t = kv[1, pl.ds(begin, chunk), :].T
        for h in range(QPK):
            score = lax.dot_general(
                keys,
                qv[:, h * HD : (h + 1) * HD],
                (((1,), (1,)), ((), ())),
                preferred_element_type=jnp.float32,
            )
            score = score + bias[...]
            old = stat_m[h : h + 1, :]
            top = jnp.maximum(old, jnp.max(score, axis=0, keepdims=True))
            expo = jnp.exp2((score - top) * EXP2_SCALE)
            factor = jnp.exp2((old - top) * EXP2_SCALE)
            stat_m[h : h + 1, :] = top
            stat_l[h : h + 1, :] = stat_l[h : h + 1, :] * factor + jnp.sum(
                expo, axis=0, keepdims=True
            )
            part = jnp.dot(
                values_t, expo.astype(jnp.bfloat16), preferred_element_type=jnp.float32
            )
            acc[h] = acc[h] * factor + part

    for h in range(QPK):
        done = acc[h] / stat_l[h : h + 1, :]
        whole[:, h * HD : (h + 1) * HD] = done.T.astype(jnp.bfloat16)
    for i in range(n_q):
        at = pl.multiple_of(place_ref[3 + 2 * i], part_rows)
        outs[i][...] = whole[pl.ds(at, part_rows), :]


def attend_plan(doc_ids, first_row, rows, chunk):
    docs = lax.dynamic_slice_in_dim(doc_ids, first_row, rows)
    starts = jnp.sum((doc_ids[None, :] < docs[:, None]).astype(jnp.int32), axis=1)
    end = (first_row + rows + chunk - 1) // chunk
    return starts.reshape(1, rows), starts[0] // chunk, end


def attend(place, starts, queries, arrays, tokens, chunk):
    rows = starts.shape[1]
    n_q, n_kv = len(queries), len(arrays)
    part_rows = queries[0].shape[0]
    return pl.pallas_call(
        lambda *refs: attend_kernel(rows, chunk, n_q, n_kv, *refs),
        out_shape=[jax.ShapeDtypeStruct((part_rows, QPK * HD), jnp.bfloat16)] * n_q,
        in_specs=[IN_SMEM, IN_VMEM] + [ANY] * (n_q + n_kv),
        out_specs=[IN_VMEM] * n_q,
        scratch_shapes=[
            pltpu.VMEM((2, tokens, HD), jnp.bfloat16),
            pltpu.VMEM((rows, QPK * HD), jnp.bfloat16),
            pltpu.VMEM((rows, QPK * HD), jnp.bfloat16),
            pltpu.VMEM((QPK, HD, rows), jnp.float32),
            pltpu.VMEM((QPK, rows), jnp.float32),
            pltpu.VMEM((QPK, rows), jnp.float32),
            pltpu.VMEM((chunk, rows), jnp.float32),
            pltpu.SemaphoreType.DMA((n_kv,)),
            pltpu.SemaphoreType.DMA((n_q,)),
        ],
        compiler_params=pltpu.CompilerParams(vmem_limit_bytes=VMEM_LIMIT),
        cost_estimate=pl.CostEstimate(
            flops=4 * rows * tokens * HD * QPK,
            bytes_accessed=4 * 1024 * 1024,
            transcendentals=rows * tokens * QPK,
        ),
        name="attend",
    )(place, starts, *queries, *arrays)


def project_kernel(rows, n_hidden, n_pieces, place_ref, cos_ref, sin_ref, *refs):
    hidden = refs[:n_hidden]
    pieces = refs[n_hidden : n_hidden + n_pieces]
    out_ref = refs[n_hidden + n_pieces]
    hbuf, wbuf, hsem, wsem = refs[n_hidden + n_pieces + 1 :]

    def w_copy(i):
        size = pieces[i].shape[0]
        at = pl.multiple_of(place_ref[2 + n_hidden + 2 * i], size)
        return pltpu.make_async_copy(pieces[i], wbuf.at[pl.ds(at, size)], wsem.at[i])

    def h_copy(i):
        return pltpu.make_async_copy(hidden[i], hbuf.at[i], hsem.at[i])

    for i in range(n_pieces):

        @pl.when(place_ref[1 + n_hidden + 2 * i] == 1)
        def _():
            w_copy(i).start()

    for i in range(n_hidden):
        h_copy(i).start()
    for i in range(n_pieces):

        @pl.when(place_ref[1 + n_hidden + 2 * i] == 1)
        def _():
            w_copy(i).wait()

    rotate = place_ref[0] == 1
    for i in range(n_hidden):
        h_copy(i).wait()
        block = place_ref[1 + i]
        head = lax.dot_general(
            hbuf[i], wbuf[...], (((1,), (1,)), ((), ())), preferred_element_type=jnp.float32
        )
        turned = head * cos_ref[block] + pltpu.roll(head, HD // 2, 1) * sin_ref[block]
        out_ref[pl.ds(pl.multiple_of(block * rows, rows), rows), :] = jnp.where(
            rotate, turned, head
        ).astype(jnp.bfloat16)


def project(place, cos, sin, hidden, pieces):
    rows, depth = hidden[0].shape
    n = len(hidden)
    return pl.pallas_call(
        lambda *refs: project_kernel(rows, n, len(pieces), *refs),
        out_shape=jax.ShapeDtypeStruct((n * rows, HD), jnp.bfloat16),
        in_specs=[IN_SMEM, IN_VMEM, IN_VMEM] + [ANY] * (n + len(pieces)),
        out_specs=IN_VMEM,
        scratch_shapes=[
            pltpu.VMEM((n, rows, depth), jnp.bfloat16),
            pltpu.VMEM((HD, depth), jnp.bfloat16),
            pltpu.SemaphoreType.DMA((n,)),
            pltpu.SemaphoreType.DMA((len(pieces),)),
        ],
        compiler_params=pltpu.CompilerParams(vmem_limit_bytes=VMEM_LIMIT),
        cost_estimate=pl.CostEstimate(
            flops=2 * n * rows * depth * HD,
            bytes_accessed=5 * 1024 * 1024,
            transcendentals=0,
        ),
        name="project",
    )(place, cos, sin, *hidden, *pieces)


def join_kernel(place_ref, *refs):
    n = len(refs) - 2
    out_ref, sem = refs[n:]
    copies = []
    for i in range(n):
        width = refs[i].shape[1]
        at = pl.multiple_of(place_ref[i], width)
        copies.append(
            pltpu.make_async_copy(refs[i], out_ref.at[:, pl.ds(at, width)], sem.at[i])
        )
    for c in copies:
        c.start()
    for c in copies:
        c.wait()


def join(place, parts, shape):
    return pl.pallas_call(
        join_kernel,
        out_shape=jax.ShapeDtypeStruct(shape, parts[0].dtype),
        in_specs=[IN_SMEM] + [ANY] * len(parts),
        out_specs=ANY,
        scratch_shapes=[pltpu.SemaphoreType.DMA((len(parts),))],
        name="join",
    )(place, *parts)


def by_planes(hidden, queries, kv_weight, doc_ids):
    rows = hidden.shape[0]
    tokens = doc_ids.shape[0]
    width = kv_weight.shape[1]
    x = lax.axis_index("groups")
    node = lax.axis_index("node")
    z, y, c = node // 4, (node // 2) % 2, node % 2
    low = z % 2

    def hop(fn):
        pairs = []
        for i in range(32):
            to = fn(i // 16, (i // 4) % 4, (i // 2) % 2, i % 2)
            if to is not None:
                pairs.append((i, ((to[0] * 4 + to[1]) * 2 + to[2]) * 2 + to[3]))
        return lambda v: lax.ppermute(v, AXES, pairs)

    to_core = hop(lambda x, z, y, c: (x, z, y, 1 - c))
    to_y = hop(lambda x, z, y, c: (x, z, 1 - y, c))
    to_x = hop(lambda x, z, y, c: (1 - x, z, y, c))
    to_x_late = hop(lambda x, z, y, c: (1 - x, z, y, c) if c != z % 2 else None)
    near = hop(lambda x, z, y, c: (x, z ^ 1, y, z % 2) if c == x else None)
    far = hop(lambda x, z, y, c: (x, z ^ (2 + c), y, z % 2))
    pair = hop(lambda x, z, y, c: (x, z ^ 1, y, c))
    up = {
        k: hop(lambda x, z, y, c, k=k: (x, z + k, y, c) if z + k < 4 else None) for k in (1, 2, 3)
    }

    weight = kv_weight.T
    part = width // 2
    far_0 = far(lax.dynamic_slice_in_dim(weight, x * part, part, 0))
    near_0 = near(weight)
    hidden_y = to_y(hidden)
    hidden_c = to_core(hidden)
    weight_c = to_core(weight)

    positions = z * 4 * rows + jnp.arange(4 * rows)
    cosine, sine = rope_tables(positions)
    cos = jnp.concatenate([cosine, cosine], axis=1).reshape(4, rows, HD)
    sin = jnp.concatenate([-sine, sine], axis=1).reshape(4, rows, HD)
    chunk = math.gcd(tokens, 256)
    first_row = (4 * z + 2 * y) * rows
    starts, first_chunk, end_chunk = attend_plan(doc_ids, first_row, 2 * rows, chunk)
    blocks = [2 * y + c, 2 * y + 1 - c, 2 * (1 - y) + c, 2 * (1 - y) + 1 - c]
    own = (c == low).astype(jnp.int32)
    place_a = scalars(
        z < 2, *blocks, own, c * width, own, (1 - c) * width,
        1 - own, x * width, 1 - own, (1 - x) * width,
    )
    side = (1 - own) * width
    place_b = scalars(
        z >= 2, *blocks, 1, side + x * part, 1, side + (1 - x) * part,
        1, width - side + x * part, 1, width - side + (1 - x) * part,
    )
    half_cols = queries.shape[1] // 2
    places_q = []
    for head in (y, 1 - y):
        at = head * QPK * HD
        values = [first_chunk, end_chunk, first_row]
        values += [c * rows, c * half_cols + at, (1 - c) * rows, at]
        for k in range(4):
            plane = z - k
            used = (plane >= 0) & ((plane + 1) * 4 * rows > first_chunk * chunk)
            plane = jnp.maximum(plane, 0)
            values += [used, plane // 2, plane * 4 * rows]
            values += [used, 1 - plane // 2, plane * 4 * rows]
        places_q.append(scalars(*values))
    place_out = scalars(
        (2 * c + y) * QPK * HD, (2 * c + 1 - y) * QPK * HD,
        (2 * (1 - c) + y) * QPK * HD, (2 * (1 - c) + 1 - y) * QPK * HD,
    )
    q_away = lax.dynamic_slice_in_dim(queries, (1 - c) * half_cols, half_cols, 1)
    (far_0, cos, sin, starts, place_a, place_b, places_q, place_out, q_away) = (
        lax.optimization_barrier(
            (far_0, cos, sin, starts, place_a, place_b, places_q, place_out, q_away)
        )
    )
    q_here = to_core(q_away)

    far_1 = pair(far_0)
    far_0x = to_x(far_0)
    near_x = to_x_late(near_0)
    far_1x = to_x(far_1)
    hidden_yc = to_core(hidden_y)
    plane_hidden = [hidden, hidden_c, hidden_y, hidden_yc]
    kv_a = project(place_a, cos, sin, plane_hidden, [weight, weight_c, near_0, near_x])
    kv_b = project(place_b, cos, sin, plane_hidden, [far_0, far_0x, far_1, far_1x])

    mine, others = [], []
    a_up = [kv_a] + [up[k](kv_a) for k in (1, 2, 3)]
    b_up = [kv_b] + [up[k](kv_b) for k in (1, 2, 3)]
    for k in range(4):
        mine += [a_up[k], b_up[k]]
        others += [to_y(a_up[k]), to_y(b_up[k])]
    keep_0, away_0 = attend(places_q[0], starts, [queries, q_here], mine, tokens, chunk)
    back_0 = to_core(away_0)
    keep_1, away_1 = attend(places_q[1], starts, [queries, q_here], others, tokens, chunk)
    back_1 = to_core(away_1)
    return join(place_out, [keep_0, keep_1, back_0, back_1], queries.shape)


def by_gathers(hidden, queries, kv_weight, doc_ids):
    rows = hidden.shape[0]
    tokens = doc_ids.shape[0]
    me = lax.axis_index("node")
    whole = lax.all_gather(kv_weight, "node", axis=1, tiled=True)
    projected = jnp.dot(hidden, whole, preferred_element_type=jnp.float32)
    split = whole.shape[1] // 2
    cosine, sine = rope_tables(me * rows + jnp.arange(rows))
    keys = projected[:, :split].reshape(rows, KVH, HD)
    a, b = keys[..., : HD // 2], keys[..., HD // 2 :]
    cosine, sine = cosine[:, None, :], sine[:, None, :]
    keys = jnp.concatenate([a * cosine - b * sine, b * cosine + a * sine], axis=-1)
    both = jnp.concatenate([keys, projected[:, split:].reshape(rows, KVH, HD)], axis=1)
    both = both.astype(jnp.bfloat16).transpose(1, 0, 2)
    whole = lax.all_gather(both, "node", axis=1, tiled=True)
    chunk = math.gcd(tokens, 256)
    starts, first_chunk, end_chunk = attend_plan(doc_ids, me * rows, rows, chunk)
    outs = []
    for g in range(KVH):
        place = scalars(
            first_chunk, end_chunk, me * rows, 0, g * QPK * HD, 1, 0, 0, 1, 1, 0
        )
        outs += attend(place, starts, [queries], [whole[g], whole[KVH + g]], tokens, chunk)
    return jnp.concatenate(outs, axis=1)


def solution(mesh):
    planes = mesh.shape["groups"] == 2 and mesh.shape["node"] == 16
    in_specs = (P(AXES, None), P(AXES, None), P(None, "node"), P("groups"))
    return jax.shard_map(
        by_planes if planes else by_gathers,
        mesh=mesh,
        in_specs=in_specs,
        out_specs=P(AXES, None),
        check_vma=False,
    )
```

```python
import math

import jax
import jax.numpy as jnp
import numpy as np
from jax import lax
from jax.experimental import pallas as pl
from jax.experimental.pallas import tpu as pltpu
from jax.sharding import PartitionSpec as P

KVH = 4
QPK = 8
HD = 128
AXES = ("groups", "node")
MASKED = -1e30
EXP2_SCALE = HD ** (-0.5) * math.log2(math.e)
VMEM_LIMIT = 20 * 1024 * 1024

ANY = pl.BlockSpec(memory_space=pl.ANY)
IN_SMEM = pl.BlockSpec(memory_space=pltpu.SMEM)
IN_VMEM = pl.BlockSpec(memory_space=pltpu.VMEM)


def scalars(*values):
    return jnp.stack([jnp.asarray(v).astype(jnp.int32) for v in values])


def rope_tables(positions):
    half = HD // 2
    freqs = 500000.0 ** (-(jnp.arange(half).astype(jnp.float32) * 2.0) / HD)
    angle = positions.astype(jnp.float32)[:, None] * freqs[None, :]
    return jnp.cos(angle), jnp.sin(angle)


def attend_kernel(rows, chunk, n_q, n_kv, place_ref, start_ref, starts_ref, *refs):
    queries = refs[:n_q]
    arrays = refs[n_q : n_q + n_kv]
    outs = refs[n_q + n_kv : 2 * n_q + n_kv]
    kv, qv, whole, acc, stat_m, stat_l, bias, sem, qsem = refs[2 * n_q + n_kv :]
    part_rows = queries[0].shape[0]
    length = arrays[0].shape[0]
    first_chunk = start_ref[0, 0] // chunk

    def used(i):
        base = 2 + 2 * n_q + 3 * i
        return (place_ref[base] == 1) & (place_ref[base + 2] + length > first_chunk * chunk)

    def q_copy(i):
        column = pl.multiple_of(place_ref[3 + 2 * i], HD)
        return pltpu.make_async_copy(
            queries[i].at[:, pl.ds(column, QPK * HD)],
            qv.at[pl.ds(pl.multiple_of(place_ref[2 + 2 * i], part_rows), part_rows)],
            qsem.at[i],
        )

    def kv_copy(i):
        base = 2 + 2 * n_q + 3 * i
        return pltpu.make_async_copy(
            arrays[i],
            kv.at[place_ref[base + 1], pl.ds(pl.multiple_of(place_ref[base + 2], length), length)],
            sem.at[i],
        )

    for i in range(n_q):
        q_copy(i).start()
    for i in range(n_kv):

        @pl.when(used(i))
        def _():
            kv_copy(i).start()

    stat_m[...] = jnp.full_like(stat_m, MASKED)
    stat_l[...] = jnp.zeros_like(stat_l)
    acc[...] = jnp.zeros_like(acc)
    for i in range(n_q):
        q_copy(i).wait()
    for i in range(n_kv):

        @pl.when(used(i))
        def _():
            kv_copy(i).wait()

    starts = starts_ref[...]
    q_pos = place_ref[1] + lax.broadcasted_iota(jnp.int32, (chunk, rows), 1)

    @pl.loop(first_chunk, place_ref[0])
    def _(t):
        begin = pl.multiple_of(t * chunk, chunk)
        k_pos = begin + lax.broadcasted_iota(jnp.int32, (chunk, rows), 0)
        bias[...] = jnp.where((k_pos <= q_pos) & (k_pos >= starts), 0.0, MASKED)
        keys = kv[0, pl.ds(begin, chunk), :]
        values_t = kv[1, pl.ds(begin, chunk), :].T
        for h in range(QPK):
            score = lax.dot_general(
                keys,
                qv[:, h * HD : (h + 1) * HD],
                (((1,), (1,)), ((), ())),
                preferred_element_type=jnp.float32,
            )
            score = score + bias[...]
            old = stat_m[h : h + 1, :]
            top = jnp.maximum(old, jnp.max(score, axis=0, keepdims=True))
            expo = jnp.exp2((score - top) * EXP2_SCALE)
            factor = jnp.exp2((old - top) * EXP2_SCALE)
            stat_m[h : h + 1, :] = top
            stat_l[h : h + 1, :] = stat_l[h : h + 1, :] * factor + jnp.sum(
                expo, axis=0, keepdims=True
            )
            part = jnp.dot(
                values_t, expo.astype(jnp.bfloat16), preferred_element_type=jnp.float32
            )
            acc[h] = acc[h] * factor + part

    for h in range(QPK):
        done = acc[h] / stat_l[h : h + 1, :]
        whole[:, h * HD : (h + 1) * HD] = done.T.astype(jnp.bfloat16)
    for i in range(n_q):
        at = pl.multiple_of(place_ref[2 + 2 * i], part_rows)
        outs[i][...] = whole[pl.ds(at, part_rows), :]


def attend_starts(doc_ids, first_row, rows):
    docs = lax.dynamic_slice_in_dim(doc_ids, first_row, rows)
    starts = jnp.sum((doc_ids[None, :] < docs[:, None]).astype(jnp.int32), axis=1)
    return starts.reshape(1, rows)


def attend(place, starts, queries, arrays, tokens, chunk):
    rows = starts.shape[1]
    n_q, n_kv = len(queries), len(arrays)
    part_rows = queries[0].shape[0]
    return pl.pallas_call(
        lambda *refs: attend_kernel(rows, chunk, n_q, n_kv, *refs),
        out_shape=[jax.ShapeDtypeStruct((part_rows, QPK * HD), jnp.bfloat16)] * n_q,
        in_specs=[IN_SMEM, IN_SMEM, IN_VMEM] + [ANY] * (n_q + n_kv),
        out_specs=[IN_VMEM] * n_q,
        scratch_shapes=[
            pltpu.VMEM((2, tokens, HD), jnp.bfloat16),
            pltpu.VMEM((rows, QPK * HD), jnp.bfloat16),
            pltpu.VMEM((rows, QPK * HD), jnp.bfloat16),
            pltpu.VMEM((QPK, HD, rows), jnp.float32),
            pltpu.VMEM((QPK, rows), jnp.float32),
            pltpu.VMEM((QPK, rows), jnp.float32),
            pltpu.VMEM((chunk, rows), jnp.float32),
            pltpu.SemaphoreType.DMA((n_kv,)),
            pltpu.SemaphoreType.DMA((n_q,)),
        ],
        compiler_params=pltpu.CompilerParams(vmem_limit_bytes=VMEM_LIMIT),
        cost_estimate=pl.CostEstimate(
            flops=4 * rows * tokens * HD * QPK,
            bytes_accessed=4 * 1024 * 1024,
            transcendentals=rows * tokens * QPK,
        ),
        name="attend",
    )(place, starts, starts, *queries, *arrays)


def project_kernel(rows, n_hidden, n_pieces, place_ref, cos_ref, sin_ref, *refs):
    hidden = refs[:n_hidden]
    pieces = refs[n_hidden : n_hidden + n_pieces]
    out_ref = refs[n_hidden + n_pieces]
    hbuf, wbuf, hsem, wsem = refs[n_hidden + n_pieces + 1 :]

    def w_copy(i):
        size = pieces[i].shape[0]
        at = pl.multiple_of(place_ref[2 + n_hidden + 2 * i], size)
        return pltpu.make_async_copy(pieces[i], wbuf.at[pl.ds(at, size)], wsem.at[i])

    def h_copy(i):
        return pltpu.make_async_copy(hidden[i], hbuf.at[i], hsem.at[i])

    for i in range(n_pieces):

        @pl.when(place_ref[1 + n_hidden + 2 * i] == 1)
        def _():
            w_copy(i).start()

    for i in range(n_hidden):
        h_copy(i).start()
    for i in range(n_pieces):

        @pl.when(place_ref[1 + n_hidden + 2 * i] == 1)
        def _():
            w_copy(i).wait()

    rotate = place_ref[0] == 1
    for i in range(n_hidden):
        h_copy(i).wait()
        block = place_ref[1 + i]
        head = lax.dot_general(
            hbuf[i], wbuf[...], (((1,), (1,)), ((), ())), preferred_element_type=jnp.float32
        )
        turned = head * cos_ref[block] + pltpu.roll(head, HD // 2, 1) * sin_ref[block]
        out_ref[pl.ds(pl.multiple_of(block * rows, rows), rows), :] = jnp.where(
            rotate, turned, head
        ).astype(jnp.bfloat16)


def project(place, cos, sin, hidden, pieces):
    rows, depth = hidden[0].shape
    n = len(hidden)
    return pl.pallas_call(
        lambda *refs: project_kernel(rows, n, len(pieces), *refs),
        out_shape=jax.ShapeDtypeStruct((n * rows, HD), jnp.bfloat16),
        in_specs=[IN_SMEM, IN_VMEM, IN_VMEM] + [ANY] * (n + len(pieces)),
        out_specs=IN_VMEM,
        scratch_shapes=[
            pltpu.VMEM((n, rows, depth), jnp.bfloat16),
            pltpu.VMEM((HD, depth), jnp.bfloat16),
            pltpu.SemaphoreType.DMA((n,)),
            pltpu.SemaphoreType.DMA((len(pieces),)),
        ],
        compiler_params=pltpu.CompilerParams(vmem_limit_bytes=VMEM_LIMIT),
        cost_estimate=pl.CostEstimate(
            flops=2 * n * rows * depth * HD,
            bytes_accessed=5 * 1024 * 1024,
            transcendentals=0,
        ),
        name="project",
    )(place, cos, sin, *hidden, *pieces)


def join_kernel(place_ref, *refs):
    n = len(refs) - 2
    out_ref, sem = refs[n:]
    copies = []
    for i in range(n):
        width = refs[i].shape[1]
        at = pl.multiple_of(place_ref[i], width)
        copies.append(
            pltpu.make_async_copy(refs[i], out_ref.at[:, pl.ds(at, width)], sem.at[i])
        )
    for c in copies:
        c.start()
    for c in copies:
        c.wait()


def join(place, parts, shape):
    return pl.pallas_call(
        join_kernel,
        out_shape=jax.ShapeDtypeStruct(shape, parts[0].dtype),
        in_specs=[IN_SMEM] + [IN_VMEM] * len(parts),
        out_specs=ANY,
        scratch_shapes=[pltpu.SemaphoreType.DMA((len(parts),))],
        name="join",
    )(place, *parts)


def by_planes(hidden, queries, kv_weight, doc_ids):
    rows = hidden.shape[0]
    tokens = doc_ids.shape[0]
    width = kv_weight.shape[1]
    part = width // 2
    columns = QPK * HD
    x = lax.axis_index("groups")
    node = lax.axis_index("node")
    z, y, c = node // 4, (node // 2) % 2, node % 2

    def hop(fn):
        pairs = []
        for i in range(32):
            to = fn(i // 16, (i // 4) % 4, (i // 2) % 2, i % 2)
            if to is not None:
                pairs.append((i, ((to[0] * 4 + to[1]) * 2 + to[2]) * 2 + to[3]))
        return lambda v: lax.ppermute(v, AXES, pairs)

    to_core = hop(lambda x, z, y, c: (x, z, y, 1 - c))
    to_y = hop(lambda x, z, y, c: (x, z, 1 - y, c))
    to_both = hop(lambda x, z, y, c: (x, z, 1 - y, 1 - c))
    to_x = hop(lambda x, z, y, c: (1 - x, z, y, c))
    to_x_near = hop(lambda x, z, y, c: (1 - x, z, y, c) if c != z % 2 else None)
    near = hop(lambda x, z, y, c: (x, z ^ 1, y, z % 2) if c == x else None)
    far = hop(lambda x, z, y, c: (x, z ^ (2 + c), y, z % 2))
    far_too = hop(lambda x, z, y, c: (x, z ^ (3 - c), y, z % 2))
    up = {
        k: hop(lambda x, z, y, c, k=k: (x, z + k, y, c) if z + k < 4 else None) for k in (1, 2, 3)
    }

    chunk = math.gcd(tokens, 256)
    tables = [[] for _ in range(5)]
    for i in range(32):
        ix, iz, iy, ic = i // 16, (i // 4) % 4, (i // 2) % 2, i % 2
        blocks = [2 * iy + ic, 2 * iy + 1 - ic, 2 * (1 - iy) + ic, 2 * (1 - iy) + 1 - ic]
        own = int(ic == iz % 2)
        tables[0].append(
            [int(iz < 2), *blocks]
            + [own, ic * width, own, (1 - ic) * width]
            + [1 - own, ix * width, 1 - own, (1 - ix) * width]
        )
        side = (1 - own) * width
        tables[1].append(
            [int(iz >= 2), *blocks]
            + [1, side + ix * part, 1, side + (1 - ix) * part]
            + [1, width - side + ix * part, 1, width - side + (1 - ix) * part]
        )
        stored = []
        for k in range(4):
            plane = max(iz - k, 0)
            stored += [int(iz >= k), plane // 2, plane * 4 * rows]
            stored += [int(iz >= k), 1 - plane // 2, plane * 4 * rows]
        for t, (head, q_columns) in enumerate(((1 - iy, (0, 0)), (iy, ((iy + 2 * ic) * columns, 0)))):
            first = (4 * iz + 2 * head) * rows
            tables[2 + t].append(
                [-(-(first + 2 * rows) // chunk), first]
                + [ic * rows, q_columns[0], (1 - ic) * rows, q_columns[1]]
                + stored
            )
        heads = [iy + 2 * ic, iy + 2 * (1 - ic), 1 - iy + 2 * ic, 1 - iy + 2 * (1 - ic)]
        tables[4].append([h * columns for h in heads])
    widths = [len(t[0]) for t in tables]
    whole = np.concatenate([np.asarray(t, np.int32) for t in tables], axis=1)
    place = lax.dynamic_slice_in_dim(jnp.asarray(whole), x * 16 + node, 1, 0)[0]
    at, places = 0, []
    for w in widths:
        places.append(place[at : at + w])
        at += w

    weight = kv_weight.T
    quarter = lax.dynamic_slice_in_dim(weight, x * part, part, 0)
    far_0 = far(quarter)
    near_0 = near(weight)
    far_1 = far_too(quarter)
    hidden_y = to_y(hidden)
    hidden_c = to_core(hidden)
    weight_c = to_core(weight)

    positions = z * 4 * rows + jnp.arange(4 * rows)
    cosine, sine = rope_tables(positions)
    cos = jnp.concatenate([cosine, cosine], axis=1).reshape(4, rows, HD)
    sin = jnp.concatenate([-sine, sine], axis=1).reshape(4, rows, HD)
    starts = [attend_starts(doc_ids, (4 * z + 2 * h) * rows, 2 * rows) for h in (1 - y, y)]
    q_away = [
        lax.dynamic_slice_in_dim(queries, h * columns, columns, 1)
        for h in (y + 2 * (1 - c), 1 - y + 2 * c, 1 - y + 2 * (1 - c))
    ]
    far_0, cos, sin, starts, places, q_away = lax.optimization_barrier(
        (far_0, cos, sin, starts, places, q_away)
    )
    far_0x = to_x(far_0)
    near_x = to_x_near(near_0)
    far_1x = to_x(far_1)
    hidden_yc = to_core(hidden_y)
    q_core, q_y, q_both = to_core(q_away[0]), to_y(q_away[1]), to_both(q_away[2])

    plane_hidden = [hidden, hidden_c, hidden_y, hidden_yc]
    kv_a = project(places[0], cos, sin, plane_hidden, [weight, weight_c, near_0, near_x])
    kv_b = project(places[1], cos, sin, plane_hidden, [far_0, far_0x, far_1, far_1x])

    a_up = [kv_a] + [up[k](kv_a) for k in (1, 2, 3)]
    b_up = [kv_b] + [up[k](kv_b) for k in (1, 2, 3)]
    stored = []
    for k in range(4):
        stored += [a_up[k], b_up[k]]
    across = attend(places[2], starts[0], [q_y, q_both], stored, tokens, chunk)
    back = [to_y(across[0]), to_both(across[1])]
    here = attend(places[3], starts[1], [queries, q_core], stored, tokens, chunk)
    parts = [here[0], to_core(here[1])] + back
    return join(places[4], parts, queries.shape)


def by_gathers(hidden, queries, kv_weight, doc_ids):
    rows = hidden.shape[0]
    tokens = doc_ids.shape[0]
    me = lax.axis_index("node")
    whole = lax.all_gather(kv_weight, "node", axis=1, tiled=True)
    projected = jnp.dot(hidden, whole, preferred_element_type=jnp.float32)
    split = whole.shape[1] // 2
    cosine, sine = rope_tables(me * rows + jnp.arange(rows))
    keys = projected[:, :split].reshape(rows, KVH, HD)
    a, b = keys[..., : HD // 2], keys[..., HD // 2 :]
    cosine, sine = cosine[:, None, :], sine[:, None, :]
    keys = jnp.concatenate([a * cosine - b * sine, b * cosine + a * sine], axis=-1)
    both = jnp.concatenate([keys, projected[:, split:].reshape(rows, KVH, HD)], axis=1)
    both = both.astype(jnp.bfloat16).transpose(1, 0, 2)
    whole = lax.all_gather(both, "node", axis=1, tiled=True)
    chunk = math.gcd(tokens, 256)
    starts = attend_starts(doc_ids, me * rows, rows)
    end = (me * rows + rows + chunk - 1) // chunk
    outs = []
    for g in range(KVH):
        place = scalars(end, me * rows, 0, g * QPK * HD, 1, 0, 0, 1, 1, 0)
        outs += attend(place, starts, [queries], [whole[g], whole[KVH + g]], tokens, chunk)
    return jnp.concatenate(outs, axis=1)


def solution(mesh):
    planes = mesh.shape["groups"] == 2 and mesh.shape["node"] == 16
    in_specs = (P(AXES, None), P(AXES, None), P(None, "node"), P("groups"))
    return jax.shard_map(
        by_planes if planes else by_gathers,
        mesh=mesh,
        in_specs=in_specs,
        out_specs=P(AXES, None),
        check_vma=False,
    )
```

```python
import math

import jax
import jax.numpy as jnp
import numpy as np
from jax import lax
from jax.experimental import pallas as pl
from jax.experimental.pallas import tpu as pltpu
from jax.sharding import PartitionSpec as P

KVH = 4
QPK = 8
HD = 128
AXES = ("groups", "node")
MASKED = -1e30
EXP2_SCALE = HD ** (-0.5) * math.log2(math.e)
VMEM_LIMIT = 32 * 1024 * 1024

ANY = pl.BlockSpec(memory_space=pl.ANY)
IN_SMEM = pl.BlockSpec(memory_space=pltpu.SMEM)
IN_VMEM = pl.BlockSpec(memory_space=pltpu.VMEM)


def scalars(*values):
    return jnp.stack([jnp.asarray(v).astype(jnp.int32) for v in values])


def rope_tables(positions):
    half = HD // 2
    freqs = 500000.0 ** (-(jnp.arange(half).astype(jnp.float32) * 2.0) / HD)
    angle = positions.astype(jnp.float32)[:, None] * freqs[None, :]
    return jnp.cos(angle), jnp.sin(angle)


def attend_kernel(rows, chunk, n_q, n_kv, place_ref, start_ref, starts_ref, *refs):
    queries = refs[:n_q]
    arrays = refs[n_q : n_q + n_kv]
    outs = refs[n_q + n_kv : 2 * n_q + n_kv]
    kv, qv, stacked, acc, stat_m, stat_l, bias, sem, qsem = refs[2 * n_q + n_kv :]
    part_rows = queries[0].shape[0]
    length = arrays[0].shape[0]
    first_chunk = start_ref[0] // chunk

    def used(i):
        base = 2 + 2 * n_q + 3 * i
        return (place_ref[base] == 1) & (place_ref[base + 2] + length > first_chunk * chunk)

    def q_copy(i):
        column = pl.multiple_of(place_ref[3 + 2 * i], HD)
        return pltpu.make_async_copy(
            queries[i].at[:, pl.ds(column, QPK * HD)],
            qv.at[pl.ds(pl.multiple_of(place_ref[2 + 2 * i], part_rows), part_rows)],
            qsem.at[i],
        )

    def kv_copy(i):
        base = 2 + 2 * n_q + 3 * i
        return pltpu.make_async_copy(
            arrays[i],
            kv.at[place_ref[base + 1], pl.ds(pl.multiple_of(place_ref[base + 2], length), length)],
            sem.at[i],
        )

    for i in range(n_q):
        q_copy(i).start()
    for i in range(n_kv):

        @pl.when(used(i))
        def _():
            kv_copy(i).start()

    stat_m[...] = jnp.full_like(stat_m, MASKED)
    stat_l[...] = jnp.zeros_like(stat_l)
    acc[...] = jnp.zeros_like(acc)
    for i in range(n_q):
        q_copy(i).wait()
    for h in range(QPK):
        stacked[h * rows : (h + 1) * rows, :] = qv[:, h * HD : (h + 1) * HD]
    for i in range(n_kv):

        @pl.when(used(i))
        def _():
            kv_copy(i).wait()

    lanes = chunk // HD
    starts = jnp.concatenate([starts_ref[...]] * lanes, axis=1)
    q_pos = place_ref[1] + lax.broadcasted_iota(jnp.int32, (rows, chunk), 0)

    @pl.loop(first_chunk, place_ref[0])
    def _(t):
        begin = pl.multiple_of(t * chunk, chunk)
        k_pos = begin + lax.broadcasted_iota(jnp.int32, (rows, chunk), 1)
        bias[...] = jnp.where((k_pos <= q_pos) & (k_pos >= starts), 0.0, MASKED)
        score = lax.dot_general(
            stacked[...],
            kv[0, pl.ds(begin, chunk), :],
            (((1,), (1,)), ((), ())),
            preferred_element_type=jnp.float32,
        )
        score = (score.reshape(QPK, rows, chunk) + bias[...][None]).reshape(QPK * rows, chunk)
        old = stat_m[...]
        top = jnp.maximum(old, jnp.max(score, axis=1, keepdims=True))
        expo = jnp.exp2((score - jnp.concatenate([top] * lanes, axis=1)) * EXP2_SCALE)
        factor = jnp.exp2((old - top) * EXP2_SCALE)
        stat_m[...] = top
        sums = expo[:, :HD]
        for i in range(1, lanes):
            sums = sums + expo[:, i * HD : (i + 1) * HD]
        stat_l[...] = stat_l[...] * factor + sums
        part = jnp.dot(
            expo.astype(jnp.bfloat16),
            kv[1, pl.ds(begin, chunk), :],
            preferred_element_type=jnp.float32,
        )
        acc[...] = acc[...] * factor + part

    for h in range(QPK):
        at = slice(h * rows, (h + 1) * rows)
        done = acc[at, :] / jnp.sum(stat_l[at, :], axis=1, keepdims=True)
        qv[:, h * HD : (h + 1) * HD] = done.astype(jnp.bfloat16)
    for i in range(n_q):
        at = pl.multiple_of(place_ref[2 + 2 * i], part_rows)
        outs[i][...] = qv[pl.ds(at, part_rows), :]


def attend_starts(doc_ids, first_row, rows):
    docs = lax.dynamic_slice_in_dim(doc_ids, first_row, rows)
    starts = jnp.sum((doc_ids[None, :] < docs[:, None]).astype(jnp.int32), axis=1)
    return starts


def attend(place, starts, queries, arrays, tokens, chunk):
    rows = starts.shape[0]
    n_q, n_kv = len(queries), len(arrays)
    part_rows = queries[0].shape[0]
    return pl.pallas_call(
        lambda *refs: attend_kernel(rows, chunk, n_q, n_kv, *refs),
        out_shape=[jax.ShapeDtypeStruct((part_rows, QPK * HD), jnp.bfloat16)] * n_q,
        in_specs=[IN_SMEM, IN_SMEM, IN_VMEM] + [ANY] * (n_q + n_kv),
        out_specs=[IN_VMEM] * n_q,
        scratch_shapes=[
            pltpu.VMEM((2, tokens, HD), jnp.bfloat16),
            pltpu.VMEM((rows, QPK * HD), jnp.bfloat16),
            pltpu.VMEM((QPK * rows, HD), jnp.bfloat16),
            pltpu.VMEM((QPK * rows, HD), jnp.float32),
            pltpu.VMEM((QPK * rows, HD), jnp.float32),
            pltpu.VMEM((QPK * rows, HD), jnp.float32),
            pltpu.VMEM((rows, chunk), jnp.float32),
            pltpu.SemaphoreType.DMA((n_kv,)),
            pltpu.SemaphoreType.DMA((n_q,)),
        ],
        compiler_params=pltpu.CompilerParams(vmem_limit_bytes=VMEM_LIMIT),
        cost_estimate=pl.CostEstimate(
            flops=rows * tokens * HD,
            bytes_accessed=rows * tokens,
            transcendentals=0,
        ),
        name="attend",
    )(place, starts[:1], jnp.broadcast_to(starts[:, None], (rows, HD)), *queries, *arrays)


def project_kernel(rows, n_hidden, n_pieces, place_ref, cos_ref, sin_ref, *refs):
    hidden = refs[:n_hidden]
    pieces = refs[n_hidden : n_hidden + n_pieces]
    out_ref = refs[n_hidden + n_pieces]
    hbuf, wbuf, hsem, wsem = refs[n_hidden + n_pieces + 1 :]

    def w_copy(i):
        size = pieces[i].shape[0]
        at = pl.multiple_of(place_ref[2 + n_hidden + 2 * i], size)
        return pltpu.make_async_copy(pieces[i], wbuf.at[pl.ds(at, size)], wsem.at[i])

    def h_copy(i):
        at = pl.multiple_of(place_ref[1 + i] * rows, rows)
        return pltpu.make_async_copy(hidden[i], hbuf.at[pl.ds(at, rows)], hsem.at[i])

    for i in range(n_pieces):

        @pl.when(place_ref[1 + n_hidden + 2 * i] == 1)
        def _():
            w_copy(i).start()

    for i in range(n_hidden):
        h_copy(i).start()
    for i in range(n_pieces):

        @pl.when(place_ref[1 + n_hidden + 2 * i] == 1)
        def _():
            w_copy(i).wait()

    for i in range(n_hidden):
        h_copy(i).wait()
    head = lax.dot_general(
        hbuf[...], wbuf[...], (((1,), (1,)), ((), ())), preferred_element_type=jnp.float32
    )
    turned = head * cos_ref[...] + pltpu.roll(head, HD // 2, 1) * sin_ref[...]
    out_ref[...] = jnp.where(place_ref[0] == 1, turned, head).astype(jnp.bfloat16)


def project(place, cos, sin, hidden, pieces):
    rows, depth = hidden[0].shape
    n = len(hidden)
    return pl.pallas_call(
        lambda *refs: project_kernel(rows, n, len(pieces), *refs),
        out_shape=jax.ShapeDtypeStruct((n * rows, HD), jnp.bfloat16),
        in_specs=[IN_SMEM, IN_VMEM, IN_VMEM] + [ANY] * (n + len(pieces)),
        out_specs=IN_VMEM,
        scratch_shapes=[
            pltpu.VMEM((n * rows, depth), jnp.bfloat16),
            pltpu.VMEM((HD, depth), jnp.bfloat16),
            pltpu.SemaphoreType.DMA((n,)),
            pltpu.SemaphoreType.DMA((len(pieces),)),
        ],
        compiler_params=pltpu.CompilerParams(vmem_limit_bytes=VMEM_LIMIT),
        cost_estimate=pl.CostEstimate(
            flops=rows * depth * HD,
            bytes_accessed=rows * depth,
            transcendentals=0,
        ),
        name="project",
    )(place, cos, sin, *hidden, *pieces)


def join_kernel(place_ref, *refs):
    n = len(refs) - 4
    out_ref, whole, sem, out_sem = refs[n:]
    copies = []
    for i in range(n):
        width = refs[i].shape[1]
        at = pl.multiple_of(place_ref[i], width)
        copies.append(
            pltpu.make_async_copy(refs[i], whole.at[:, pl.ds(at, width)], sem.at[i])
        )
    for c in copies:
        c.start()
    for c in copies:
        c.wait()
    copy = pltpu.make_async_copy(whole, out_ref, out_sem)
    copy.start()
    copy.wait()


def join(place, parts, shape):
    return pl.pallas_call(
        join_kernel,
        out_shape=jax.ShapeDtypeStruct(shape, parts[0].dtype),
        in_specs=[IN_SMEM] + [ANY] * len(parts),
        out_specs=ANY,
        scratch_shapes=[
            pltpu.VMEM(shape, parts[0].dtype),
            pltpu.SemaphoreType.DMA((len(parts),)),
            pltpu.SemaphoreType.DMA,
        ],
        compiler_params=pltpu.CompilerParams(vmem_limit_bytes=VMEM_LIMIT),
        name="join",
    )(place, *parts)


def by_planes(hidden, queries, kv_weight, doc_ids):
    rows = hidden.shape[0]
    tokens = doc_ids.shape[0]
    width = kv_weight.shape[1]
    part = width // 2
    columns = QPK * HD
    x = lax.axis_index("groups")
    node = lax.axis_index("node")
    z, y, c = node // 4, (node // 2) % 2, node % 2

    def hop(fn):
        pairs = []
        for i in range(32):
            to = fn(i // 16, (i // 4) % 4, (i // 2) % 2, i % 2)
            if to is not None:
                pairs.append((i, ((to[0] * 4 + to[1]) * 2 + to[2]) * 2 + to[3]))
        return lambda v: lax.ppermute(v, AXES, pairs)

    to_core = hop(lambda x, z, y, c: (x, z, y, 1 - c))
    to_y = hop(lambda x, z, y, c: (x, z, 1 - y, c))
    to_both = hop(lambda x, z, y, c: (x, z, 1 - y, 1 - c))
    to_x = hop(lambda x, z, y, c: (1 - x, z, y, c))
    near = hop(lambda x, z, y, c: (x, z ^ 1, y, c))
    far = hop(lambda x, z, y, c: (x, z ^ (2 + c), y, z % 2))
    up = {
        k: hop(lambda x, z, y, c, k=k: (x, z + k, y, c) if z + k < 4 else None) for k in (1, 2, 3)
    }

    chunk = math.gcd(tokens, 512)
    tables = [[] for _ in range(6)]
    for i in range(32):
        ix, iz, iy, ic = i // 16, (i // 4) % 4, (i // 2) % 2, i % 2
        blocks = [2 * iy + ic, 2 * iy + 1 - ic, 2 * (1 - iy) + ic, 2 * (1 - iy) + 1 - ic]
        own = int(ic == iz % 2)
        tables[0].append(
            [int(iz < 2), *blocks]
            + [own, ic * width, 1 - own, ic * width, 1, (1 - ic) * width]
        )
        side = (1 - own) * width
        tables[1].append(
            [int(iz >= 2), *blocks]
            + [1, side + ix * part, 1, side + (1 - ix) * part]
            + [1, width - side + ix * part, 1, width - side + (1 - ix) * part]
        )
        stored = []
        for k in range(4):
            plane = max(iz - k, 0)
            stored += [int(iz >= k), plane // 2, plane * 4 * rows]
            stored += [int(iz >= k), 1 - plane // 2, plane * 4 * rows]
        for t, block in enumerate((2 * (1 - iy), 2 * iy + 1 - ic, 2 * iy + ic)):
            first = (4 * iz + block) * rows
            size = 2 * rows if t == 0 else rows
            q_rows = [ic * rows, 0, (1 - ic) * rows, 0] if t == 0 else [0, 0]
            tables[2 + t].append([-(-(first + size) // chunk), first] + q_rows + stored)
        heads = [iy + 2 * ic, iy + 2 * (1 - ic), 1 - iy + 2 * ic, 1 - iy + 2 * (1 - ic)]
        tables[5].append([h * columns for h in heads])
    widths = [len(t[0]) for t in tables]
    whole = np.concatenate([np.asarray(t, np.int32) for t in tables], axis=1)
    place = lax.dynamic_slice_in_dim(jnp.asarray(whole), x * 16 + node, 1, 0)[0]
    at, places = 0, []
    for w in widths:
        places.append(place[at : at + w])
        at += w

    weight = kv_weight.T
    far_0 = far(lax.dynamic_slice_in_dim(weight, x * part, part, 0))
    near_0 = near(weight)
    hidden_y = to_y(hidden)
    hidden_c = to_core(hidden)

    positions = z * 4 * rows + jnp.arange(4 * rows)
    cosine, sine = rope_tables(positions)
    cos = jnp.concatenate([cosine, cosine], axis=1)
    sin = jnp.concatenate([-sine, sine], axis=1)
    starts = [
        attend_starts(doc_ids, (4 * z + block) * rows, size)
        for block, size in ((2 * (1 - y), 2 * rows), (2 * y + 1 - c, rows), (2 * y + c, rows))
    ]
    q_own, *q_away = [
        lax.dynamic_slice_in_dim(queries, h * columns, columns, 1)
        for h in (y + 2 * c, y + 2 * (1 - c), 1 - y + 2 * c, 1 - y + 2 * (1 - c))
    ]
    far_0, cos, sin, starts, places, q_own, q_away = lax.optimization_barrier(
        (far_0, cos, sin, starts, places, q_own, q_away)
    )
    far_1 = near(far_0)
    far_0x = to_x(far_0)
    far_1, far_0x = lax.optimization_barrier((far_1, far_0x))
    far_1x = to_x(far_1)
    near_c = to_core(jnp.where(c == z % 2, near_0, weight))
    hidden_y, far_1, q_away = lax.optimization_barrier((hidden_y, far_1, q_away))
    hidden_yc = to_core(hidden_y)
    q_core, q_y, q_both = to_core(q_away[0]), to_y(q_away[1]), to_both(q_away[2])

    plane_hidden = [hidden, hidden_c, hidden_y, hidden_yc]
    kv_a = project(places[0], cos, sin, plane_hidden, [weight, near_0, near_c])
    kv_a, places[1] = lax.optimization_barrier((kv_a, places[1]))
    kv_b = project(places[1], cos, sin, plane_hidden, [far_0, far_0x, far_1, far_1x])

    a_up = [kv_a] + [up[k](kv_a) for k in (1, 2, 3)]
    a_up, kv_b = lax.optimization_barrier((a_up, kv_b))
    b_up = [kv_b] + [up[k](kv_b) for k in (1, 2, 3)]
    stored = []
    for k in range(4):
        stored += [a_up[k], b_up[k]]
    across = attend(places[2], starts[0], [q_y, q_both], stored, tokens, chunk)
    back = [to_y(across[0]), to_both(across[1])]
    across, places[3] = lax.optimization_barrier((across, places[3]))
    beside = attend(places[3], starts[1], [q_core], stored, tokens, chunk)
    beside, places[4] = lax.optimization_barrier((beside, places[4]))
    here = attend(places[4], starts[2], [q_own], stored, tokens, chunk)
    parts = [here[0], to_core(beside[0])] + back
    return join(places[5], parts, queries.shape)


def by_gathers(hidden, queries, kv_weight, doc_ids):
    rows = hidden.shape[0]
    tokens = doc_ids.shape[0]
    me = lax.axis_index("node")
    whole = lax.all_gather(kv_weight, "node", axis=1, tiled=True)
    projected = jnp.dot(hidden, whole, preferred_element_type=jnp.float32)
    split = whole.shape[1] // 2
    cosine, sine = rope_tables(me * rows + jnp.arange(rows))
    keys = projected[:, :split].reshape(rows, KVH, HD)
    a, b = keys[..., : HD // 2], keys[..., HD // 2 :]
    cosine, sine = cosine[:, None, :], sine[:, None, :]
    keys = jnp.concatenate([a * cosine - b * sine, b * cosine + a * sine], axis=-1)
    both = jnp.concatenate([keys, projected[:, split:].reshape(rows, KVH, HD)], axis=1)
    both = both.astype(jnp.bfloat16).transpose(1, 0, 2)
    whole = lax.all_gather(both, "node", axis=1, tiled=True)
    chunk = math.gcd(tokens, 512)
    starts = attend_starts(doc_ids, me * rows, rows)
    end = (me * rows + rows + chunk - 1) // chunk
    outs = []
    for g in range(KVH):
        place = scalars(end, me * rows, 0, g * QPK * HD, 1, 0, 0, 1, 1, 0)
        outs += attend(place, starts, [queries], [whole[g], whole[KVH + g]], tokens, chunk)
    return jnp.concatenate(outs, axis=1)


def solution(mesh):
    planes = mesh.shape["groups"] == 2 and mesh.shape["node"] == 16
    in_specs = (P(AXES, None), P(AXES, None), P(None, "node"), P("groups"))
    return jax.shard_map(
        by_planes if planes else by_gathers,
        mesh=mesh,
        in_specs=in_specs,
        out_specs=P(AXES, None),
        check_vma=False,
    )
```

```python
import math

import jax
import jax.numpy as jnp
import numpy as np
from jax import lax
from jax.experimental import pallas as pl
from jax.experimental.pallas import tpu as pltpu
from jax.sharding import PartitionSpec as P

KVH = 4
QPK = 8
HD = 128
AXES = ("groups", "node")
MASKED = -1e30
EXP2_SCALE = HD ** (-0.5) * math.log2(math.e)
VMEM_LIMIT = 32 * 1024 * 1024

ANY = pl.BlockSpec(memory_space=pl.ANY)
IN_SMEM = pl.BlockSpec(memory_space=pltpu.SMEM)
IN_VMEM = pl.BlockSpec(memory_space=pltpu.VMEM)


def scalars(*values):
    return jnp.stack([jnp.asarray(v).astype(jnp.int32) for v in values])


def rope_tables(positions):
    half = HD // 2
    freqs = 500000.0 ** (-(jnp.arange(half).astype(jnp.float32) * 2.0) / HD)
    angle = positions.astype(jnp.float32)[:, None] * freqs[None, :]
    return jnp.cos(angle), jnp.sin(angle)


def attend_kernel(rows, chunk, n_q, n_kv, resumed, last, place_ref, start_ref, starts_ref, *refs):
    queries, refs = refs[:n_q], refs[n_q:]
    arrays, refs = refs[:n_kv], refs[n_kv:]
    state, refs = (refs[:3], refs[3:]) if resumed else ((), refs)
    if last:
        outs, refs = refs[:n_q], refs[n_q:]
        kv, qv, stacked, bias, sem, qsem, ssem, stat_m, stat_l, acc = refs
    else:
        stat_m, stat_l, acc, kv, qv, stacked, bias, sem, qsem, ssem = refs
    part_rows = queries[0].shape[0]
    length = arrays[0].shape[1]
    first_chunk = jnp.maximum(start_ref[0] // chunk, place_ref[0])

    def used(i):
        base = 3 + 2 * n_q + 2 * i
        return (place_ref[base] == 1) & (place_ref[base + 1] + length > first_chunk * chunk)

    def q_copy(i):
        column = pl.multiple_of(place_ref[4 + 2 * i], HD)
        return pltpu.make_async_copy(
            queries[i].at[:, pl.ds(column, QPK * HD)],
            qv.at[pl.ds(pl.multiple_of(place_ref[3 + 2 * i], part_rows), part_rows)],
            qsem.at[i],
        )

    def kv_copy(i):
        at = pl.multiple_of(place_ref[4 + 2 * n_q + 2 * i], length)
        return pltpu.make_async_copy(arrays[i], kv.at[:, pl.ds(at, length)], sem.at[i])

    for i in range(n_q):
        q_copy(i).start()
    for i in range(n_kv):

        @pl.when(used(i))
        def _():
            kv_copy(i).start()

    running = [
        pltpu.make_async_copy(old, new, ssem.at[i])
        for i, (old, new) in enumerate(zip(state, (stat_m, stat_l, acc)))
    ]
    for copy in running:
        copy.start()
    if not resumed:
        stat_m[...] = jnp.full_like(stat_m, MASKED)
        stat_l[...] = jnp.zeros_like(stat_l)
        acc[...] = jnp.zeros_like(acc)
    for i in range(n_q):
        q_copy(i).wait()
    for h in range(QPK):
        stacked[h * rows : (h + 1) * rows, :] = qv[:, h * HD : (h + 1) * HD]
    for i in range(n_kv):

        @pl.when(used(i))
        def _():
            kv_copy(i).wait()

    for copy in running:
        copy.wait()

    lanes = chunk // HD
    starts = jnp.concatenate([starts_ref[...]] * lanes, axis=1)
    q_pos = place_ref[2] + lax.broadcasted_iota(jnp.int32, (rows, chunk), 0)

    @pl.loop(first_chunk, place_ref[1])
    def _(t):
        begin = pl.multiple_of(t * chunk, chunk)
        k_pos = begin + lax.broadcasted_iota(jnp.int32, (rows, chunk), 1)
        bias[...] = jnp.where((k_pos <= q_pos) & (k_pos >= starts), 0.0, MASKED)
        score = lax.dot_general(
            stacked[...],
            kv[0, pl.ds(begin, chunk), :],
            (((1,), (1,)), ((), ())),
            preferred_element_type=jnp.float32,
        )
        score = (score.reshape(QPK, rows, chunk) + bias[...][None]).reshape(QPK * rows, chunk)
        old = stat_m[...]
        top = jnp.maximum(old, jnp.max(score, axis=1, keepdims=True))
        expo = jnp.exp2((score - jnp.concatenate([top] * lanes, axis=1)) * EXP2_SCALE)
        factor = jnp.exp2((old - top) * EXP2_SCALE)
        stat_m[...] = top
        sums = expo[:, :HD]
        for i in range(1, lanes):
            sums = sums + expo[:, i * HD : (i + 1) * HD]
        stat_l[...] = stat_l[...] * factor + sums
        part = jnp.dot(
            expo.astype(jnp.bfloat16),
            kv[1, pl.ds(begin, chunk), :],
            preferred_element_type=jnp.float32,
        )
        acc[...] = acc[...] * factor + part

    if not last:
        return
    for h in range(QPK):
        at = slice(h * rows, (h + 1) * rows)
        done = acc[at, :] / jnp.sum(stat_l[at, :], axis=1, keepdims=True)
        qv[:, h * HD : (h + 1) * HD] = done.astype(jnp.bfloat16)
    for i in range(n_q):
        at = pl.multiple_of(place_ref[3 + 2 * i], part_rows)
        outs[i][...] = qv[pl.ds(at, part_rows), :]


def attend_starts(doc_ids, first_row, rows):
    docs = lax.dynamic_slice_in_dim(doc_ids, first_row, rows)
    starts = jnp.sum((doc_ids[None, :] < docs[:, None]).astype(jnp.int32), axis=1)
    return starts


def attend(place, starts, queries, arrays, tokens, chunk, state=(), last=True):
    rows = starts.shape[0]
    n_q, n_kv = len(queries), len(arrays)
    part_rows = queries[0].shape[0]
    running = (QPK * rows, HD)
    if last:
        out_shape = [jax.ShapeDtypeStruct((part_rows, QPK * HD), jnp.bfloat16)] * n_q
    else:
        out_shape = [jax.ShapeDtypeStruct(running, jnp.float32)] * 3
    return pl.pallas_call(
        lambda *refs: attend_kernel(rows, chunk, n_q, n_kv, bool(state), last, *refs),
        out_shape=out_shape,
        in_specs=[IN_SMEM, IN_SMEM, IN_VMEM] + [ANY] * (n_q + n_kv + len(state)),
        out_specs=[IN_VMEM] * len(out_shape),
        scratch_shapes=[
            pltpu.VMEM((2, tokens, HD), jnp.bfloat16),
            pltpu.VMEM((rows, QPK * HD), jnp.bfloat16),
            pltpu.VMEM((QPK * rows, HD), jnp.bfloat16),
            pltpu.VMEM((rows, chunk), jnp.float32),
            pltpu.SemaphoreType.DMA((n_kv,)),
            pltpu.SemaphoreType.DMA((n_q,)),
            pltpu.SemaphoreType.DMA((3,)),
        ]
        + [pltpu.VMEM(running, jnp.float32)] * (3 if last else 0),
        compiler_params=pltpu.CompilerParams(vmem_limit_bytes=VMEM_LIMIT),
        cost_estimate=pl.CostEstimate(
            flops=rows * tokens * HD,
            bytes_accessed=rows * tokens,
            transcendentals=0,
        ),
        name="attend",
    )(
        place,
        starts[:1],
        jnp.broadcast_to(starts[:, None], (rows, HD)),
        *queries,
        *arrays,
        *state,
    )


def project_kernel(rows, n_hidden, n_pieces, place_ref, cos_ref, sin_ref, *refs):
    hidden = refs[:n_hidden]
    pieces = refs[n_hidden : n_hidden + n_pieces]
    out_ref = refs[n_hidden + n_pieces]
    hbuf, wbuf, hsem, wsem = refs[n_hidden + n_pieces + 1 :]

    def w_copy(i):
        size = pieces[i].shape[0]
        at = pl.multiple_of(place_ref[2 + n_hidden + 2 * i], size)
        return pltpu.make_async_copy(pieces[i], wbuf.at[pl.ds(at, size)], wsem.at[i])

    def h_copy(i):
        at = pl.multiple_of(place_ref[1 + i] * rows, rows)
        return pltpu.make_async_copy(hidden[i], hbuf.at[pl.ds(at, rows)], hsem.at[i])

    for i in range(n_pieces):

        @pl.when(place_ref[1 + n_hidden + 2 * i] == 1)
        def _():
            w_copy(i).start()

    for i in range(n_hidden):
        h_copy(i).start()
    for i in range(n_pieces):

        @pl.when(place_ref[1 + n_hidden + 2 * i] == 1)
        def _():
            w_copy(i).wait()

    for i in range(n_hidden):
        h_copy(i).wait()
    both = lax.dot_general(
        hbuf[...], wbuf[...], (((1,), (1,)), ((), ())), preferred_element_type=jnp.float32
    )
    keys_first = place_ref[0] == 0
    keys = jnp.where(keys_first, both[:, :HD], both[:, HD:])
    values = jnp.where(keys_first, both[:, HD:], both[:, :HD])
    turned = keys * cos_ref[...] + pltpu.roll(keys, HD // 2, 1) * sin_ref[...]
    out_ref[0] = turned.astype(jnp.bfloat16)
    out_ref[1] = values.astype(jnp.bfloat16)


def project(place, cos, sin, hidden, pieces):
    rows, depth = hidden[0].shape
    n = len(hidden)
    return pl.pallas_call(
        lambda *refs: project_kernel(rows, n, len(pieces), *refs),
        out_shape=jax.ShapeDtypeStruct((2, n * rows, HD), jnp.bfloat16),
        in_specs=[IN_SMEM, IN_VMEM, IN_VMEM] + [ANY] * (n + len(pieces)),
        out_specs=IN_VMEM,
        scratch_shapes=[
            pltpu.VMEM((n * rows, depth), jnp.bfloat16),
            pltpu.VMEM((2 * HD, depth), jnp.bfloat16),
            pltpu.SemaphoreType.DMA((n,)),
            pltpu.SemaphoreType.DMA((len(pieces),)),
        ],
        compiler_params=pltpu.CompilerParams(vmem_limit_bytes=VMEM_LIMIT),
        cost_estimate=pl.CostEstimate(
            flops=rows * depth * HD,
            bytes_accessed=rows * depth,
            transcendentals=0,
        ),
        name="project",
    )(place, cos, sin, *hidden, *pieces)


def join_kernel(place_ref, *refs):
    n = len(refs) - 4
    out_ref, whole, sem, out_sem = refs[n:]
    copies = []
    for i in range(n):
        height, width = refs[i].shape
        at = pl.multiple_of(place_ref[2 * i + 1], width)
        row = pl.multiple_of(place_ref[2 * i], height)
        copies.append(
            pltpu.make_async_copy(
                refs[i], whole.at[pl.ds(row, height), pl.ds(at, width)], sem.at[i]
            )
        )
    for c in copies:
        c.start()
    for c in copies:
        c.wait()
    copy = pltpu.make_async_copy(whole, out_ref, out_sem)
    copy.start()
    copy.wait()


def join(place, parts, shape):
    return pl.pallas_call(
        join_kernel,
        out_shape=jax.ShapeDtypeStruct(shape, parts[0].dtype),
        in_specs=[IN_SMEM] + [ANY] * len(parts),
        out_specs=ANY,
        scratch_shapes=[
            pltpu.VMEM(shape, parts[0].dtype),
            pltpu.SemaphoreType.DMA((len(parts),)),
            pltpu.SemaphoreType.DMA,
        ],
        compiler_params=pltpu.CompilerParams(vmem_limit_bytes=VMEM_LIMIT),
        name="join",
    )(place, *parts)


def by_planes(hidden, queries, kv_weight, doc_ids):
    rows = hidden.shape[0]
    tokens = doc_ids.shape[0]
    width = kv_weight.shape[1]
    part = width // 2
    columns = QPK * HD
    x = lax.axis_index("groups")
    node = lax.axis_index("node")
    z, y, c = node // 4, (node // 2) % 2, node % 2

    def hop(fn):
        pairs = []
        for i in range(32):
            to = fn(i // 16, (i // 4) % 4, (i // 2) % 2, i % 2)
            if to is not None:
                pairs.append((i, ((to[0] * 4 + to[1]) * 2 + to[2]) * 2 + to[3]))
        return lambda v: lax.ppermute(v, AXES, pairs)

    to_core = hop(lambda x, z, y, c: (x, z, y, 1 - c))
    to_y = hop(lambda x, z, y, c: (x, z, 1 - y, c))
    to_both = hop(lambda x, z, y, c: (x, z, 1 - y, 1 - c))
    to_x = hop(lambda x, z, y, c: (1 - x, z, y, c))
    near = hop(lambda x, z, y, c: (x, z ^ 1, y, c))
    to_near_x = hop(lambda x, z, y, c: (1 - x, z ^ 1, y, c))
    far = hop(lambda x, z, y, c: (x, z ^ (2 + c), y, z % 2))
    up = {
        k: hop(lambda x, z, y, c, k=k: (x, z + k, y, c) if z + k < 4 else None) for k in (1, 2, 3)
    }

    chunk = math.gcd(tokens, 512)
    tables = [[] for _ in range(8)]
    for i in range(32):
        ix, iz, iy, ic = i // 16, (i // 4) % 4, (i // 2) % 2, i % 2
        blocks = [2 * iy + ic, 2 * iy + 1 - ic, 2 * (1 - iy) + ic, 2 * (1 - iy) + 1 - ic]
        own = int(ic == iz % 2)
        side = HD + (1 - own) * width
        tables[0].append(
            [int(iz >= 2), *blocks]
            + [own, ic * width, 1 - own, ic * width, 1, (1 - ic) * width]
            + [1, side + ix * part, 1, side + (1 - ix) * part]
            + [1, 2 * HD + width - side + ix * part, 1, 2 * HD + width - side + (1 - ix) * part]
        )
        stored = [v for k in range(4) for v in (int(iz >= k), max(iz - k, 0) * 4 * rows)]
        for t, block in enumerate((2 * (1 - iy), 2 * iy + 1 - ic, 2 * iy + ic)):
            first = (4 * iz + block) * rows
            q_rows = [ic * rows, 0, (1 - ic) * rows, 0] if t == 0 else [0, 0]
            tables[1 + t].append([max(iz - 1, 0), iz + 1, first] + q_rows + stored[:4])
            tables[4 + t].append([0, max(iz - 1, 0), first] + q_rows + stored[4:])
        heads = [iy + 2 * ic, iy + 2 * (1 - ic), iy + 2 * (1 - ic)]
        heads += [1 - iy + 2 * ic, 1 - iy + 2 * (1 - ic)]
        tops = [0, 0, rows // 2, 0, 0]
        tables[7].append([v for top, h in zip(tops, heads) for v in (top, h * columns)])
    widths = [len(t[0]) for t in tables]
    whole = np.concatenate([np.asarray(t, np.int32) for t in tables], axis=1)
    place = lax.dynamic_slice_in_dim(jnp.asarray(whole), x * 16 + node, 1, 0)[0]
    at, places = 0, []
    for w in widths:
        places.append(place[at : at + w])
        at += w

    weight = kv_weight.T
    far_0 = far(lax.dynamic_slice_in_dim(weight, x * part, part, 0))
    near_0 = near(weight)
    hidden_y = to_y(hidden)
    hidden_c = to_core(hidden)

    positions = z * 4 * rows + jnp.arange(4 * rows)
    cosine, sine = rope_tables(positions)
    cos = jnp.concatenate([cosine, cosine], axis=1)
    sin = jnp.concatenate([-sine, sine], axis=1)
    starts = [
        attend_starts(doc_ids, (4 * z + block) * rows, size)
        for block, size in ((2 * (1 - y), 2 * rows), (2 * y + 1 - c, rows), (2 * y + c, rows))
    ]
    q_own, *q_away = [
        lax.dynamic_slice_in_dim(queries, h * columns, columns, 1)
        for h in (y + 2 * c, y + 2 * (1 - c), 1 - y + 2 * c, 1 - y + 2 * (1 - c))
    ]
    far_0, cos, sin, starts, places, q_own, q_away = lax.optimization_barrier(
        (far_0, cos, sin, starts, places, q_own, q_away)
    )
    far_1, far_0x, far_1x = near(far_0), to_x(far_0), to_near_x(far_0)
    near_c = to_core(jnp.where(c == z % 2, near_0, weight))
    hidden_y, far_1, far_0x, far_1x, q_away = lax.optimization_barrier(
        (hidden_y, far_1, far_0x, far_1x, q_away)
    )
    hidden_yc = to_core(hidden_y)
    q_core, q_y, q_both = to_core(q_away[0]), to_y(q_away[1]), to_both(q_away[2])

    plane_hidden = [hidden, hidden_c, hidden_y, hidden_yc]
    pieces = [weight, near_0, near_c, far_0, far_0x, far_1, far_1x]
    kv = project(places[0], cos, sin, plane_hidden, pieces)

    stored = [kv] + [up[k](kv) for k in (1, 2, 3)]
    parts_q = [[q_y, q_both], [q_core], [q_own]]
    begun = [
        attend(places[1 + t], starts[t], parts_q[t], stored[:2], tokens, chunk, last=False)
        for t in range(3)
    ]
    begun, places[4] = lax.optimization_barrier((begun, places[4]))

    def finish(t):
        return attend(places[4 + t], starts[t], parts_q[t], stored[2:], tokens, chunk, begun[t])

    across = finish(0)
    back = [to_y(across[0]), to_both(across[1])]
    across, places[5] = lax.optimization_barrier((across, places[5]))
    beside = finish(1)
    beside, places[6] = lax.optimization_barrier((beside, places[6]))
    here = finish(2)
    parts = [here[0], to_core(beside[0][: rows // 2]), to_core(beside[0][rows // 2 :])] + back
    return join(places[7], parts, queries.shape)


def by_gathers(hidden, queries, kv_weight, doc_ids):
    rows = hidden.shape[0]
    tokens = doc_ids.shape[0]
    me = lax.axis_index("node")
    whole = lax.all_gather(kv_weight, "node", axis=1, tiled=True)
    projected = jnp.dot(hidden, whole, preferred_element_type=jnp.float32)
    split = whole.shape[1] // 2
    cosine, sine = rope_tables(me * rows + jnp.arange(rows))
    keys = projected[:, :split].reshape(rows, KVH, HD)
    a, b = keys[..., : HD // 2], keys[..., HD // 2 :]
    cosine, sine = cosine[:, None, :], sine[:, None, :]
    keys = jnp.concatenate([a * cosine - b * sine, b * cosine + a * sine], axis=-1)
    both = jnp.concatenate([keys, projected[:, split:].reshape(rows, KVH, HD)], axis=1)
    both = both.astype(jnp.bfloat16).transpose(1, 0, 2)
    whole = lax.all_gather(both, "node", axis=1, tiled=True)
    chunk = math.gcd(tokens, 512)
    starts = attend_starts(doc_ids, me * rows, rows)
    end = (me * rows + rows + chunk - 1) // chunk
    outs = []
    for g in range(KVH):
        place = scalars(0, end, me * rows, 0, g * QPK * HD, 1, 0)
        pair = jnp.stack([whole[g], whole[KVH + g]])
        outs += attend(place, starts, [queries], [pair], tokens, chunk)
    return jnp.concatenate(outs, axis=1)


def solution(mesh):
    planes = mesh.shape["groups"] == 2 and mesh.shape["node"] == 16
    in_specs = (P(AXES, None), P(AXES, None), P(None, "node"), P("groups"))
    return jax.shard_map(
        by_planes if planes else by_gathers,
        mesh=mesh,
        in_specs=in_specs,
        out_specs=P(AXES, None),
        check_vma=False,
    )
```

```python
import math

import jax
import jax.numpy as jnp
import numpy as np
from jax import lax
from jax.experimental import pallas as pl
from jax.experimental.pallas import tpu as pltpu
from jax.sharding import PartitionSpec as P

KVH = 4
QPK = 8
HD = 128
AXES = ("groups", "node")
MASKED = -1e30
EXP2_SCALE = HD ** (-0.5) * math.log2(math.e)
VMEM_LIMIT = 28 * 1024 * 1024

ANY = pl.BlockSpec(memory_space=pl.ANY)
IN_SMEM = pl.BlockSpec(memory_space=pltpu.SMEM)
IN_VMEM = pl.BlockSpec(memory_space=pltpu.VMEM)


def scalars(*values):
    return jnp.stack([jnp.asarray(v).astype(jnp.int32) for v in values])


def rope_tables(positions):
    half = HD // 2
    freqs = 500000.0 ** (-(jnp.arange(half).astype(jnp.float32) * 2.0) / HD)
    angle = positions.astype(jnp.float32)[:, None] * freqs[None, :]
    return jnp.cos(angle), jnp.sin(angle)


def attend_kernel(rows, chunk, n_q, n_kv, resumed, last, place_ref, start_ref, starts_ref, *refs):
    queries, refs = refs[:n_q], refs[n_q:]
    arrays, refs = refs[: 2 * n_kv], refs[2 * n_kv :]
    state, refs = (refs[:3], refs[3:]) if resumed else ((), refs)
    if last:
        outs, refs = refs[:n_q], refs[n_q:]
        kv, qv, stacked, bias, sem, qsem, ssem, stat_m, stat_l, acc = refs
    else:
        stat_m, stat_l, acc, kv, qv, stacked, bias, sem, qsem, ssem = refs
    part_rows = queries[0].shape[0]
    chunks = arrays[0].shape[0] // chunk

    def q_copy(i):
        column = pl.multiple_of(place_ref[2 + 2 * i], HD)
        return pltpu.make_async_copy(
            queries[i].at[:, pl.ds(column, QPK * HD)],
            qv.at[pl.ds(pl.multiple_of(place_ref[1 + 2 * i], part_rows), part_rows)],
            qsem.at[i],
        )

    def kv_copy(i):
        kind = place_ref[1 + 2 * n_q + n_kv + i // 2]
        kind = kind if i % 2 == 0 else 1 - kind
        return pltpu.make_async_copy(arrays[i], kv.at[i // 2, kind], sem.at[i])

    for i in range(n_q):
        q_copy(i).start()
    running = [
        pltpu.make_async_copy(old, new, ssem.at[i])
        for i, (old, new) in enumerate(zip(state, (stat_m, stat_l, acc)))
    ]
    for copy in running:
        copy.start()
    for i in range(2 * n_kv):
        kv_copy(i).start()
    if not resumed:
        stat_m[...] = jnp.full_like(stat_m, MASKED)
        stat_l[...] = jnp.zeros_like(stat_l)
        acc[...] = jnp.zeros_like(acc)
    for i in range(n_q):
        q_copy(i).wait()
    for h in range(QPK):
        stacked[h * rows : (h + 1) * rows, :] = qv[:, h * HD : (h + 1) * HD]
    for copy in running:
        copy.wait()
    for i in range(2 * n_kv):
        kv_copy(i).wait()

    lanes = chunk // HD
    starts = jnp.concatenate([starts_ref[...]] * lanes, axis=1)
    q_pos = place_ref[0] + lax.broadcasted_iota(jnp.int32, (rows, chunk), 0)
    first_chunk = start_ref[0] // chunk
    end_chunk = (place_ref[0] + rows + chunk - 1) // chunk

    def attend_chunk(i, j, t):
        k_pos = t * chunk + lax.broadcasted_iota(jnp.int32, (rows, chunk), 1)
        bias[...] = jnp.where((k_pos <= q_pos) & (k_pos >= starts), 0.0, MASKED)
        here = pl.ds(pl.multiple_of(j * chunk, chunk), chunk)
        score = lax.dot_general(
            stacked[...],
            kv[i, 0, here, :],
            (((1,), (1,)), ((), ())),
            preferred_element_type=jnp.float32,
        )
        score = (score.reshape(QPK, rows, chunk) + bias[...][None]).reshape(QPK * rows, chunk)
        old = stat_m[...]
        top = jnp.maximum(old, jnp.max(score, axis=1, keepdims=True))
        expo = jnp.exp2((score - jnp.concatenate([top] * lanes, axis=1)) * EXP2_SCALE)
        factor = jnp.exp2((old - top) * EXP2_SCALE)
        stat_m[...] = top
        sums = expo[:, :HD]
        for lane in range(1, lanes):
            sums = sums + expo[:, lane * HD : (lane + 1) * HD]
        stat_l[...] = stat_l[...] * factor + sums
        part = jnp.dot(
            expo.astype(jnp.bfloat16),
            kv[i, 1, here, :],
            preferred_element_type=jnp.float32,
        )
        acc[...] = acc[...] * factor + part

    @pl.loop(0, n_kv * chunks)
    def _(step):
        i, j = step // chunks, step % chunks
        t = place_ref[1 + 2 * n_q + i] * chunks + j

        @pl.when((t >= first_chunk) & (t < end_chunk))
        def _():
            attend_chunk(i, j, t)

    if not last:
        return
    for h in range(QPK):
        at = slice(h * rows, (h + 1) * rows)
        done = acc[at, :] / jnp.sum(stat_l[at, :], axis=1, keepdims=True)
        qv[:, h * HD : (h + 1) * HD] = done.astype(jnp.bfloat16)
    for i in range(n_q):
        at = pl.multiple_of(place_ref[1 + 2 * i], part_rows)
        outs[i][...] = qv[pl.ds(at, part_rows), :]


def attend_starts(doc_ids, first_row, rows):
    docs = lax.dynamic_slice_in_dim(doc_ids, first_row, rows)
    starts = jnp.sum((doc_ids[None, :] < docs[:, None]).astype(jnp.int32), axis=1)
    return starts


def attend(place, starts, queries, arrays, tokens, chunk, state=(), last=True):
    rows = starts.shape[0]
    n_q, n_kv = len(queries), len(arrays) // 2
    part_rows = queries[0].shape[0]
    running = (QPK * rows, HD)
    if last:
        out_shape = [jax.ShapeDtypeStruct((part_rows, QPK * HD), jnp.bfloat16)] * n_q
    else:
        out_shape = [jax.ShapeDtypeStruct(running, jnp.float32)] * 3
    return pl.pallas_call(
        lambda *refs: attend_kernel(rows, chunk, n_q, n_kv, bool(state), last, *refs),
        out_shape=out_shape,
        in_specs=[IN_SMEM, IN_SMEM, IN_VMEM] + [ANY] * (n_q + 2 * n_kv + len(state)),
        out_specs=[IN_VMEM] * len(out_shape),
        scratch_shapes=[
            pltpu.VMEM((n_kv, 2, *arrays[0].shape), jnp.bfloat16),
            pltpu.VMEM((rows, QPK * HD), jnp.bfloat16),
            pltpu.VMEM((QPK * rows, HD), jnp.bfloat16),
            pltpu.VMEM((rows, chunk), jnp.float32),
            pltpu.SemaphoreType.DMA((2 * n_kv,)),
            pltpu.SemaphoreType.DMA((n_q,)),
            pltpu.SemaphoreType.DMA((3,)),
        ]
        + [pltpu.VMEM(running, jnp.float32)] * (3 if last else 0),
        compiler_params=pltpu.CompilerParams(vmem_limit_bytes=VMEM_LIMIT),
        cost_estimate=pl.CostEstimate(
            flops=rows * tokens * HD,
            bytes_accessed=rows * tokens,
            transcendentals=0,
        ),
        name="attend",
    )(
        place,
        starts[:1],
        jnp.broadcast_to(starts[:, None], (rows, HD)),
        *queries,
        *arrays,
        *state,
    )


def project_kernel(rows, n_hidden, n_pieces, place_ref, cos_ref, sin_ref, *refs):
    hidden = refs[:n_hidden]
    pieces = refs[n_hidden : n_hidden + n_pieces]
    out_ref = refs[n_hidden + n_pieces]
    hbuf, wbuf, hsem, wsem = refs[n_hidden + n_pieces + 1 :]

    def w_copy(i):
        size = pieces[i].shape[0]
        at = pl.multiple_of(place_ref[2 + n_hidden + 2 * i], size)
        return pltpu.make_async_copy(pieces[i], wbuf.at[pl.ds(at, size)], wsem.at[i])

    def h_copy(i):
        at = pl.multiple_of(place_ref[1 + i] * rows, rows)
        return pltpu.make_async_copy(hidden[i], hbuf.at[pl.ds(at, rows)], hsem.at[i])

    for i in range(n_pieces):

        @pl.when(place_ref[1 + n_hidden + 2 * i] == 1)
        def _():
            w_copy(i).start()

    for i in range(n_hidden):
        h_copy(i).start()
    for i in range(n_pieces):

        @pl.when(place_ref[1 + n_hidden + 2 * i] == 1)
        def _():
            w_copy(i).wait()

    for i in range(n_hidden):
        h_copy(i).wait()
    head = lax.dot_general(
        hbuf[...], wbuf[...], (((1,), (1,)), ((), ())), preferred_element_type=jnp.float32
    )
    turned = head * cos_ref[...] + pltpu.roll(head, HD // 2, 1) * sin_ref[...]
    out_ref[...] = jnp.where(place_ref[0] == 1, turned, head).astype(jnp.bfloat16)


def project(place, cos, sin, hidden, pieces):
    rows, depth = hidden[0].shape
    n = len(hidden)
    return pl.pallas_call(
        lambda *refs: project_kernel(rows, n, len(pieces), *refs),
        out_shape=jax.ShapeDtypeStruct((n * rows, HD), jnp.bfloat16),
        in_specs=[IN_SMEM, IN_VMEM, IN_VMEM] + [ANY] * (n + len(pieces)),
        out_specs=IN_VMEM,
        scratch_shapes=[
            pltpu.VMEM((n * rows, depth), jnp.bfloat16),
            pltpu.VMEM((HD, depth), jnp.bfloat16),
            pltpu.SemaphoreType.DMA((n,)),
            pltpu.SemaphoreType.DMA((len(pieces),)),
        ],
        compiler_params=pltpu.CompilerParams(vmem_limit_bytes=VMEM_LIMIT),
        cost_estimate=pl.CostEstimate(
            flops=rows * depth * HD,
            bytes_accessed=rows * depth,
            transcendentals=0,
        ),
        name="project",
    )(place, cos, sin, *hidden, *pieces)


def join_kernel(place_ref, *refs):
    n = len(refs) - 4
    out_ref, whole, sem, out_sem = refs[n:]
    copies = []
    for i in range(n):
        height, width = refs[i].shape
        at = pl.multiple_of(place_ref[2 * i + 1], width)
        row = pl.multiple_of(place_ref[2 * i], height)
        copies.append(
            pltpu.make_async_copy(
                refs[i], whole.at[pl.ds(row, height), pl.ds(at, width)], sem.at[i]
            )
        )
    for c in copies:
        c.start()
    for c in copies:
        c.wait()
    copy = pltpu.make_async_copy(whole, out_ref, out_sem)
    copy.start()
    copy.wait()


def join(place, parts, shape):
    return pl.pallas_call(
        join_kernel,
        out_shape=jax.ShapeDtypeStruct(shape, parts[0].dtype),
        in_specs=[IN_SMEM] + [ANY] * len(parts),
        out_specs=ANY,
        scratch_shapes=[
            pltpu.VMEM(shape, parts[0].dtype),
            pltpu.SemaphoreType.DMA((len(parts),)),
            pltpu.SemaphoreType.DMA,
        ],
        compiler_params=pltpu.CompilerParams(vmem_limit_bytes=VMEM_LIMIT),
        name="join",
    )(place, *parts)


def by_planes(hidden, queries, kv_weight, doc_ids):
    rows = hidden.shape[0]
    tokens = doc_ids.shape[0]
    width = kv_weight.shape[1]
    part = width // 2
    columns = QPK * HD
    x = lax.axis_index("groups")
    node = lax.axis_index("node")
    z, y, c = node // 4, (node // 2) % 2, node % 2

    def hop(fn):
        pairs = []
        for i in range(32):
            to = fn(i // 16, (i // 4) % 4, (i // 2) % 2, i % 2)
            if to is not None:
                pairs.append((i, ((to[0] * 4 + to[1]) * 2 + to[2]) * 2 + to[3]))
        return lambda v: lax.ppermute(v, AXES, pairs)

    to_core = hop(lambda x, z, y, c: (x, z, y, 1 - c))
    to_y = hop(lambda x, z, y, c: (x, z, 1 - y, c))
    to_both = hop(lambda x, z, y, c: (x, z, 1 - y, 1 - c))
    to_x = hop(lambda x, z, y, c: (1 - x, z, y, c))
    near = hop(lambda x, z, y, c: (x, z ^ 1, y, c))
    far = hop(lambda x, z, y, c: (x, z ^ (2 + c), y, z % 2))
    up_near = hop(lambda x, z, y, c: (x, z + 1, y, c) if z % 2 == 0 else None)
    up_far = hop(lambda x, z, y, c: (x, z + 2, y, c) if z < 2 else None)
    swap_high = hop(lambda x, z, y, c: (x, z ^ 1, y, c) if z >= 2 else None)

    chunk = math.gcd(tokens, 512)
    tables = [[] for _ in range(9)]
    for i in range(32):
        ix, iz, iy, ic = i // 16, (i // 4) % 4, (i // 2) % 2, i % 2
        blocks = [2 * iy + ic, 2 * iy + 1 - ic, 2 * (1 - iy) + ic, 2 * (1 - iy) + 1 - ic]
        own = int(ic == iz % 2)
        tables[0].append(
            [int(iz < 2), *blocks]
            + [own, ic * width, 1 - own, ic * width, 1, (1 - ic) * width]
        )
        side = (1 - own) * width
        tables[6].append(
            [int(iz >= 2), *blocks]
            + [1, side + ix * part, 1, side + (1 - ix) * part]
            + [1, width - side + ix * part, 1, width - side + (1 - ix) * part]
        )
        planes = [iz, iz - 1 if iz % 2 else -1, iz - 2, (iz ^ 1) - 2 if iz >= 2 else -1]
        for t, block in enumerate((2 * (1 - iy), 2 * iy + 1 - ic, 2 * iy + ic)):
            first = (4 * iz + block) * rows
            q_rows = [ic * rows, 0, (1 - ic) * rows, 0] if t == 0 else [0, 0]
            calls = (
                [(1, planes[:1]), (4, planes[1:3]), (2, planes[3:])],
                [(3, planes[:1]), (7, planes[1:])],
                [(8, planes)],
            )[t]
            for at, some in calls:
                kinds = [max(plane, 0) // 2 for plane in some]
                tables[at].append([first] + q_rows + some + kinds)
        heads = [iy + 2 * ic, iy + 2 * (1 - ic), iy + 2 * (1 - ic)]
        heads += [1 - iy + 2 * ic, 1 - iy + 2 * (1 - ic)]
        tops = [0, 0, rows // 2, 0, 0]
        tables[5].append([v for top, h in zip(tops, heads) for v in (top, h * columns)])
    widths = [len(t[0]) for t in tables]
    whole = np.concatenate([np.asarray(t, np.int32) for t in tables], axis=1)
    place = lax.dynamic_slice_in_dim(jnp.asarray(whole), x * 16 + node, 1, 0)[0]
    at, places = 0, []
    for w in widths:
        places.append(place[at : at + w])
        at += w

    weight = kv_weight.T
    far_0 = far(lax.dynamic_slice_in_dim(weight, x * part, part, 0))
    near_0 = near(weight)
    hidden_y = to_y(hidden)
    hidden_c = to_core(hidden)

    positions = z * 4 * rows + jnp.arange(4 * rows)
    cosine, sine = rope_tables(positions)
    cos = jnp.concatenate([cosine, cosine], axis=1)
    sin = jnp.concatenate([-sine, sine], axis=1)
    starts = [
        attend_starts(doc_ids, (4 * z + block) * rows, size)
        for block, size in ((2 * (1 - y), 2 * rows), (2 * y + 1 - c, rows), (2 * y + c, rows))
    ]
    q_own, *q_away = [
        lax.dynamic_slice_in_dim(queries, h * columns, columns, 1)
        for h in (y + 2 * c, y + 2 * (1 - c), 1 - y + 2 * c, 1 - y + 2 * (1 - c))
    ]
    far_0, cos, sin, starts, places, q_own, q_away = lax.optimization_barrier(
        (far_0, cos, sin, starts, places, q_own, q_away)
    )
    far_1, far_0x = near(far_0), to_x(far_0)
    far_1, far_0x = lax.optimization_barrier((far_1, far_0x))
    far_1x = to_x(far_1)
    near_c = to_core(jnp.where(c == z % 2, near_0, weight))
    q_core = to_core(q_away[0])
    hidden_y, far_1, q_away, q_core = lax.optimization_barrier((hidden_y, far_1, q_away, q_core))
    hidden_yc = to_core(hidden_y)
    q_y, q_both = to_y(q_away[1]), to_both(q_away[2])

    plane_hidden = [hidden, hidden_c, hidden_y, hidden_yc]
    kv_a = project(places[0], cos, sin, plane_hidden, [weight, near_0, near_c])
    kv_a, places[6] = lax.optimization_barrier((kv_a, places[6]))
    kv_b = project(places[6], cos, sin, plane_hidden, [far_0, far_0x, far_1, far_1x])

    a_near, a_far = up_near(kv_a), up_far(kv_a)
    b_near, b_far = up_near(kv_b), up_far(kv_b)
    own, near_below = [kv_a, kv_b], [a_near, b_near]
    q_partner = [q_y, q_both]
    begun = attend(places[1], starts[0], q_partner, own, tokens, chunk, last=False)
    begun_beside = attend(places[3], starts[1], [q_core], own, tokens, chunk, last=False)
    begun, begun_beside, a_far = lax.optimization_barrier((begun, begun_beside, a_far))
    other = [swap_high(a_far), swap_high(b_far)]
    below = near_below + [a_far, b_far]
    begun = attend(places[4], starts[0], q_partner, below, tokens, chunk, begun, last=False)
    across = attend(places[2], starts[0], q_partner, other, tokens, chunk, begun)
    back = [to_y(across[0]), to_both(across[1])]
    below += other
    across, places[7] = lax.optimization_barrier((across, places[7]))
    beside = attend(places[7], starts[1], [q_core], below, tokens, chunk, begun_beside)
    beside, places[8] = lax.optimization_barrier((beside, places[8]))
    here = attend(places[8], starts[2], [q_own], own + below, tokens, chunk)
    parts = [here[0], to_core(beside[0][: rows // 2]), to_core(beside[0][rows // 2 :])] + back
    return join(places[5], parts, queries.shape)


def by_gathers(hidden, queries, kv_weight, doc_ids):
    rows = hidden.shape[0]
    tokens = doc_ids.shape[0]
    me = lax.axis_index("node")
    whole = lax.all_gather(kv_weight, "node", axis=1, tiled=True)
    projected = jnp.dot(hidden, whole, preferred_element_type=jnp.float32)
    split = whole.shape[1] // 2
    cosine, sine = rope_tables(me * rows + jnp.arange(rows))
    keys = projected[:, :split].reshape(rows, KVH, HD)
    a, b = keys[..., : HD // 2], keys[..., HD // 2 :]
    cosine, sine = cosine[:, None, :], sine[:, None, :]
    keys = jnp.concatenate([a * cosine - b * sine, b * cosine + a * sine], axis=-1)
    both = jnp.concatenate([keys, projected[:, split:].reshape(rows, KVH, HD)], axis=1)
    both = both.astype(jnp.bfloat16).transpose(1, 0, 2)
    whole = lax.all_gather(both, "node", axis=1, tiled=True)
    chunk = math.gcd(tokens, 512)
    starts = attend_starts(doc_ids, me * rows, rows)
    outs = []
    for g in range(KVH):
        place = scalars(me * rows, 0, g * QPK * HD, 0, 0)
        pair = [whole[g], whole[KVH + g]]
        outs += attend(place, starts, [queries], pair, tokens, chunk)
    return jnp.concatenate(outs, axis=1)


def solution(mesh):
    planes = mesh.shape["groups"] == 2 and mesh.shape["node"] == 16
    in_specs = (P(AXES, None), P(AXES, None), P(None, "node"), P("groups"))
    return jax.shard_map(
        by_planes if planes else by_gathers,
        mesh=mesh,
        in_specs=in_specs,
        out_specs=P(AXES, None),
        check_vma=False,
    )
```

```python
import math

import jax
import jax.numpy as jnp
import numpy as np
from jax import lax
from jax.experimental import pallas as pl
from jax.experimental.pallas import tpu as pltpu
from jax.sharding import PartitionSpec as P

KVH = 4
QPK = 8
HD = 128
AXES = ("groups", "node")
MASKED = -1e30
EXP2_SCALE = HD ** (-0.5) * math.log2(math.e)
VMEM_LIMIT = 28 * 1024 * 1024

ANY = pl.BlockSpec(memory_space=pl.ANY)
IN_SMEM = pl.BlockSpec(memory_space=pltpu.SMEM)
IN_VMEM = pl.BlockSpec(memory_space=pltpu.VMEM)


def scalars(*values):
    return jnp.stack([jnp.asarray(v).astype(jnp.int32) for v in values])


def rope_tables(positions):
    half = HD // 2
    freqs = 500000.0 ** (-(jnp.arange(half).astype(jnp.float32) * 2.0) / HD)
    angle = positions.astype(jnp.float32)[:, None] * freqs[None, :]
    return jnp.cos(angle), jnp.sin(angle)


def attend_kernel(rows, chunk, n_q, n_kv, resumed, last, place_ref, starts_ref, *refs):
    queries, refs = refs[:n_q], refs[n_q:]
    arrays, refs = refs[: 2 * n_kv], refs[2 * n_kv :]
    state, refs = (refs[:3], refs[3:]) if resumed else ((), refs)
    if last:
        outs, refs = refs[:n_q], refs[n_q:]
        kv, stacked, bias, stat_m, stat_l, acc = refs
    else:
        stat_m, stat_l, acc, kv, stacked, bias = refs
    part_rows = rows // n_q
    chunks = arrays[0].shape[0] // chunk

    if resumed:
        for old, new in zip(state, (stat_m, stat_l, acc)):
            new[...] = old[...]
    else:
        stat_m[...] = jnp.full_like(stat_m, MASKED)
        stat_l[...] = jnp.zeros_like(stat_l)
        acc[...] = jnp.zeros_like(acc)
    for h in range(QPK):
        for i in range(n_q):
            at = h * rows + i * part_rows
            stacked[at : at + part_rows, :] = queries[i][:, h * HD : (h + 1) * HD]
    for i in range(n_kv):
        kind = place_ref[n_q + n_kv + i]
        kv[i, kind] = arrays[2 * i][...]
        kv[i, 1 - kind] = arrays[2 * i + 1][...]

    lanes = chunk // HD
    starts = jnp.concatenate([starts_ref[...]] * lanes, axis=1)
    q_pos = jnp.concatenate(
        [
            place_ref[i] + lax.broadcasted_iota(jnp.int32, (part_rows, chunk), 0)
            for i in range(n_q)
        ],
        axis=0,
    )
    first_chunk = place_ref[n_q + 2 * n_kv] // chunk
    last_row = place_ref[0]
    for i in range(1, n_q):
        last_row = jnp.maximum(last_row, place_ref[i])
    end_chunk = (last_row + part_rows + chunk - 1) // chunk

    def attend_chunk(i, j, t):
        k_pos = t * chunk + lax.broadcasted_iota(jnp.int32, (rows, chunk), 1)
        bias[...] = jnp.where((k_pos <= q_pos) & (k_pos >= starts), 0.0, MASKED)
        here = pl.ds(pl.multiple_of(j * chunk, chunk), chunk)
        score = lax.dot_general(
            stacked[...],
            kv[i, 0, here, :],
            (((1,), (1,)), ((), ())),
            preferred_element_type=jnp.float32,
        )
        score = (score.reshape(QPK, rows, chunk) + bias[...][None]).reshape(QPK * rows, chunk)
        old = stat_m[...]
        top = jnp.maximum(old, jnp.max(score, axis=1, keepdims=True))
        expo = jnp.exp2((score - jnp.concatenate([top] * lanes, axis=1)) * EXP2_SCALE)
        factor = jnp.exp2((old - top) * EXP2_SCALE)
        stat_m[...] = top
        sums = expo[:, :HD]
        for lane in range(1, lanes):
            sums = sums + expo[:, lane * HD : (lane + 1) * HD]
        stat_l[...] = stat_l[...] * factor + sums
        part = jnp.dot(
            expo.astype(jnp.bfloat16),
            kv[i, 1, here, :],
            preferred_element_type=jnp.float32,
        )
        acc[...] = acc[...] * factor + part

    @pl.loop(0, n_kv * chunks)
    def _(step):
        i, j = step // chunks, step % chunks
        t = place_ref[n_q + i] * chunks + j

        @pl.when((t >= first_chunk) & (t < end_chunk))
        def _():
            attend_chunk(i, j, t)

    if not last:
        return
    for h in range(QPK):
        at = slice(h * rows, (h + 1) * rows)
        done = acc[at, :] / jnp.sum(stat_l[at, :], axis=1, keepdims=True)
        for i in range(n_q):
            outs[i][:, h * HD : (h + 1) * HD] = done[
                i * part_rows : (i + 1) * part_rows
            ].astype(jnp.bfloat16)


def attend_starts(doc_ids, first_rows, rows):
    docs = [lax.dynamic_slice_in_dim(doc_ids, first, rows) for first in first_rows]
    docs = jnp.concatenate(docs)
    starts = jnp.sum((doc_ids[None, :] < docs[:, None]).astype(jnp.int32), axis=1)
    return jnp.broadcast_to(starts[:, None], (starts.shape[0], HD)), jnp.min(starts)[None]


def attend(place, starts, queries, arrays, tokens, chunk, state=(), last=True):
    rows = starts.shape[0]
    n_q, n_kv = len(queries), len(arrays) // 2
    part_rows = queries[0].shape[0]
    running = (QPK * rows, HD)
    if last:
        out_shape = [jax.ShapeDtypeStruct((part_rows, QPK * HD), jnp.bfloat16)] * n_q
    else:
        out_shape = [jax.ShapeDtypeStruct(running, jnp.float32)] * 3
    return pl.pallas_call(
        lambda *refs: attend_kernel(rows, chunk, n_q, n_kv, bool(state), last, *refs),
        out_shape=out_shape,
        in_specs=[IN_SMEM] + [IN_VMEM] * (1 + n_q + 2 * n_kv + len(state)),
        out_specs=[IN_VMEM] * len(out_shape),
        scratch_shapes=[
            pltpu.VMEM((n_kv, 2, *arrays[0].shape), jnp.bfloat16),
            pltpu.VMEM((QPK * rows, HD), jnp.bfloat16),
            pltpu.VMEM((rows, chunk), jnp.float32),
        ]
        + [pltpu.VMEM(running, jnp.float32)] * (3 if last else 0),
        compiler_params=pltpu.CompilerParams(vmem_limit_bytes=VMEM_LIMIT),
        cost_estimate=pl.CostEstimate(
            flops=rows * tokens * HD,
            bytes_accessed=rows * tokens,
            transcendentals=0,
        ),
        name="attend",
    )(place, starts, *queries, *arrays, *state)


def project_kernel(rows, n_hidden, n_pieces, place_ref, cos_ref, sin_ref, *refs):
    hidden = refs[:n_hidden]
    pieces = refs[n_hidden : n_hidden + n_pieces]
    out_ref = refs[n_hidden + n_pieces]
    hbuf, wbuf, hsem, wsem = refs[n_hidden + n_pieces + 1 :]

    def w_copy(i):
        size = pieces[i].shape[0]
        at = pl.multiple_of(place_ref[2 + n_hidden + 2 * i], size)
        return pltpu.make_async_copy(pieces[i], wbuf.at[pl.ds(at, size)], wsem.at[i])

    def h_copy(i):
        at = pl.multiple_of(place_ref[1 + i] * rows, rows)
        return pltpu.make_async_copy(hidden[i], hbuf.at[pl.ds(at, rows)], hsem.at[i])

    for i in range(n_pieces):

        @pl.when(place_ref[1 + n_hidden + 2 * i] == 1)
        def _():
            w_copy(i).start()

    for i in range(n_hidden):
        h_copy(i).start()
    for i in range(n_pieces):

        @pl.when(place_ref[1 + n_hidden + 2 * i] == 1)
        def _():
            w_copy(i).wait()

    for i in range(n_hidden):
        h_copy(i).wait()
    head = lax.dot_general(
        hbuf[...], wbuf[...], (((1,), (1,)), ((), ())), preferred_element_type=jnp.float32
    )
    turned = head * cos_ref[...] + pltpu.roll(head, HD // 2, 1) * sin_ref[...]
    out_ref[...] = jnp.where(place_ref[0] == 1, turned, head).astype(jnp.bfloat16)


def project(place, cos, sin, hidden, pieces):
    rows, depth = hidden[0].shape
    n = len(hidden)
    return pl.pallas_call(
        lambda *refs: project_kernel(rows, n, len(pieces), *refs),
        out_shape=jax.ShapeDtypeStruct((n * rows, HD), jnp.bfloat16),
        in_specs=[IN_SMEM, IN_VMEM, IN_VMEM] + [ANY] * (n + len(pieces)),
        out_specs=IN_VMEM,
        scratch_shapes=[
            pltpu.VMEM((n * rows, depth), jnp.bfloat16),
            pltpu.VMEM((HD, depth), jnp.bfloat16),
            pltpu.SemaphoreType.DMA((n,)),
            pltpu.SemaphoreType.DMA((len(pieces),)),
        ],
        compiler_params=pltpu.CompilerParams(vmem_limit_bytes=VMEM_LIMIT),
        cost_estimate=pl.CostEstimate(
            flops=rows * depth * HD,
            bytes_accessed=rows * depth,
            transcendentals=0,
        ),
        name="project",
    )(place, cos, sin, *hidden, *pieces)


def join_kernel(place_ref, *refs):
    n = len(refs) - 4
    out_ref, whole, sem, out_sem = refs[n:]
    copies = []
    for i in range(n):
        height, width = refs[i].shape
        at = pl.multiple_of(place_ref[2 * i + 1], width)
        row = pl.multiple_of(place_ref[2 * i], height)
        copies.append(
            pltpu.make_async_copy(
                refs[i], whole.at[pl.ds(row, height), pl.ds(at, width)], sem.at[i]
            )
        )
    for c in copies:
        c.start()
    for c in copies:
        c.wait()
    copy = pltpu.make_async_copy(whole, out_ref, out_sem)
    copy.start()
    copy.wait()


def join(place, parts, shape):
    return pl.pallas_call(
        join_kernel,
        out_shape=jax.ShapeDtypeStruct(shape, parts[0].dtype),
        in_specs=[IN_SMEM] + [ANY] * len(parts),
        out_specs=ANY,
        scratch_shapes=[
            pltpu.VMEM(shape, parts[0].dtype),
            pltpu.SemaphoreType.DMA((len(parts),)),
            pltpu.SemaphoreType.DMA,
        ],
        compiler_params=pltpu.CompilerParams(vmem_limit_bytes=VMEM_LIMIT),
        name="join",
    )(place, *parts)


def by_planes(hidden, queries, kv_weight, doc_ids):
    rows = hidden.shape[0]
    tokens = doc_ids.shape[0]
    width = kv_weight.shape[1]
    part = width // 2
    columns = QPK * HD
    x = lax.axis_index("groups")
    node = lax.axis_index("node")
    z, y, c = node // 4, (node // 2) % 2, node % 2

    def hop(fn):
        pairs = []
        for i in range(32):
            to = fn(i // 16, (i // 4) % 4, (i // 2) % 2, i % 2)
            if to is not None:
                pairs.append((i, ((to[0] * 4 + to[1]) * 2 + to[2]) * 2 + to[3]))
        return lambda v: lax.ppermute(v, AXES, pairs)

    to_core = hop(lambda x, z, y, c: (x, z, y, 1 - c))
    to_y = hop(lambda x, z, y, c: (x, z, 1 - y, c))
    to_both = hop(lambda x, z, y, c: (x, z, 1 - y, 1 - c))
    to_x = hop(lambda x, z, y, c: (1 - x, z, y, c))
    near = hop(lambda x, z, y, c: (x, z ^ 1, y, c))
    far = hop(lambda x, z, y, c: (x, z ^ (2 + c), y, z % 2))
    up_near = hop(lambda x, z, y, c: (x, z + 1, y, c) if z % 2 == 0 else None)
    up_far = hop(lambda x, z, y, c: (x, z + 2, y, c) if z < 2 else None)
    swap_high = hop(lambda x, z, y, c: (x, z ^ 1, y, c) if z >= 2 else None)

    chunk = math.gcd(tokens, 512)
    tables = [[] for _ in range(7)]
    for i in range(32):
        ix, iz, iy, ic = i // 16, (i // 4) % 4, (i // 2) % 2, i % 2
        blocks = [2 * iy + ic, 2 * iy + 1 - ic, 2 * (1 - iy) + ic, 2 * (1 - iy) + 1 - ic]
        own = int(ic == iz % 2)
        tables[0].append(
            [int(iz < 2), *blocks]
            + [own, ic * width, 1 - own, ic * width, 1, (1 - ic) * width]
        )
        side = (1 - own) * width
        tables[6].append(
            [int(iz >= 2), *blocks]
            + [1, side + ix * part, 1, side + (1 - ix) * part]
            + [1, width - side + ix * part, 1, width - side + (1 - ix) * part]
        )
        planes = [iz, iz - 1 if iz % 2 else -1, iz - 2, (iz ^ 1) - 2 if iz >= 2 else -1]
        calls = [(1, 1 - iy, planes[:1]), (2, 1 - iy, planes[3:])]
        calls += [(3, iy, planes), (4, 1 - iy, planes[1:3])]
        for at, iy_rows, some in calls:
            first = [(4 * iz + 2 * iy_rows + core) * rows for core in (ic, 1 - ic)]
            kinds = [max(plane, 0) // 2 for plane in some]
            tables[at].append(first + some + kinds)
        heads = [iy + 2 * ic, iy + 2 * (1 - ic), iy + 2 * (1 - ic)]
        heads += [1 - iy + 2 * ic, 1 - iy + 2 * (1 - ic)]
        tops = [0, 0, rows // 2, 0, 0]
        tables[5].append([v for top, h in zip(tops, heads) for v in (top, h * columns)])
    widths = [len(t[0]) for t in tables]
    whole = np.concatenate([np.asarray(t, np.int32) for t in tables], axis=1)
    place = lax.dynamic_slice_in_dim(jnp.asarray(whole), x * 16 + node, 1, 0)[0]
    at, places = 0, []
    for w in widths:
        places.append(place[at : at + w])
        at += w

    weight = kv_weight.T
    far_0 = far(lax.dynamic_slice_in_dim(weight, x * part, part, 0))
    near_0 = near(weight)
    hidden_y = to_y(hidden)
    hidden_c = to_core(hidden)

    positions = z * 4 * rows + jnp.arange(4 * rows)
    cosine, sine = rope_tables(positions)
    cos = jnp.concatenate([cosine, cosine], axis=1)
    sin = jnp.concatenate([-sine, sine], axis=1)
    firsts = [
        [(4 * z + 2 * (1 - y) + c) * rows, (4 * z + 2 * (1 - y) + 1 - c) * rows],
        [(4 * z + 2 * y + c) * rows, (4 * z + 2 * y + 1 - c) * rows],
    ]
    starts, lowest = zip(*[attend_starts(doc_ids, first, rows) for first in firsts])
    for at, low in ((1, 0), (2, 0), (3, 1), (4, 0)):
        places[at] = jnp.concatenate([places[at], lowest[low]])
    q_own, *q_away = [
        lax.dynamic_slice_in_dim(queries, h * columns, columns, 1)
        for h in (y + 2 * c, y + 2 * (1 - c), 1 - y + 2 * c, 1 - y + 2 * (1 - c))
    ]
    far_0, cos, sin, starts, places, q_own, q_away = lax.optimization_barrier(
        (far_0, cos, sin, starts, places, q_own, q_away)
    )
    far_1, far_0x = near(far_0), to_x(far_0)
    far_1, far_0x = lax.optimization_barrier((far_1, far_0x))
    far_1x = to_x(far_1)
    near_c = to_core(jnp.where(c == z % 2, near_0, weight))
    q_core = to_core(q_away[0])
    hidden_y, far_1, q_away, q_core = lax.optimization_barrier((hidden_y, far_1, q_away, q_core))
    hidden_yc = to_core(hidden_y)
    q_y, q_both = to_y(q_away[1]), to_both(q_away[2])

    plane_hidden = [hidden, hidden_c, hidden_y, hidden_yc]
    kv_a = project(places[0], cos, sin, plane_hidden, [weight, near_0, near_c])
    kv_a, places[6] = lax.optimization_barrier((kv_a, places[6]))
    kv_b = project(places[6], cos, sin, plane_hidden, [far_0, far_0x, far_1, far_1x])

    a_near, a_far = up_near(kv_a), up_far(kv_a)
    b_near, b_far = up_near(kv_b), up_far(kv_b)
    own, near_below = [kv_a, kv_b], [a_near, b_near]
    q_partner = [q_y, q_both]
    begun = attend(places[1], starts[0], q_partner, own, tokens, chunk, last=False)
    begun, a_far = lax.optimization_barrier((begun, a_far))
    other = [swap_high(a_far), swap_high(b_far)]
    below = near_below + [a_far, b_far]
    begun = attend(places[4], starts[0], q_partner, below, tokens, chunk, begun, last=False)
    across = attend(places[2], starts[0], q_partner, other, tokens, chunk, begun)
    back = [to_y(across[0]), to_both(across[1])]
    stored = own + below + other
    across, places[3] = lax.optimization_barrier((across, places[3]))
    here, beside = attend(places[3], starts[1], [q_own, q_core], stored, tokens, chunk)
    parts = [here, to_core(beside[: rows // 2]), to_core(beside[rows // 2 :])] + back
    return join(places[5], parts, queries.shape)


def by_gathers(hidden, queries, kv_weight, doc_ids):
    rows = hidden.shape[0]
    tokens = doc_ids.shape[0]
    me = lax.axis_index("node")
    whole = lax.all_gather(kv_weight, "node", axis=1, tiled=True)
    projected = jnp.dot(hidden, whole, preferred_element_type=jnp.float32)
    split = whole.shape[1] // 2
    cosine, sine = rope_tables(me * rows + jnp.arange(rows))
    keys = projected[:, :split].reshape(rows, KVH, HD)
    a, b = keys[..., : HD // 2], keys[..., HD // 2 :]
    cosine, sine = cosine[:, None, :], sine[:, None, :]
    keys = jnp.concatenate([a * cosine - b * sine, b * cosine + a * sine], axis=-1)
    both = jnp.concatenate([keys, projected[:, split:].reshape(rows, KVH, HD)], axis=1)
    both = both.astype(jnp.bfloat16).transpose(1, 0, 2)
    whole = lax.all_gather(both, "node", axis=1, tiled=True)
    chunk = math.gcd(tokens, 512)
    starts, lowest = attend_starts(doc_ids, [me * rows], rows)
    place = jnp.concatenate([scalars(me * rows, 0, 0), lowest])
    outs = []
    for g in range(KVH):
        pair = [whole[g], whole[KVH + g]]
        mine = queries[:, g * QPK * HD : (g + 1) * QPK * HD]
        outs += attend(place, starts, [mine], pair, tokens, chunk)
    return jnp.concatenate(outs, axis=1)


def solution(mesh):
    planes = mesh.shape["groups"] == 2 and mesh.shape["node"] == 16
    in_specs = (P(AXES, None), P(AXES, None), P(None, "node"), P("groups"))
    return jax.shard_map(
        by_planes if planes else by_gathers,
        mesh=mesh,
        in_specs=in_specs,
        out_specs=P(AXES, None),
        check_vma=False,
    )
```

```python
import math

import jax
import jax.numpy as jnp
import numpy as np
from jax import lax
from jax.experimental import pallas as pl
from jax.experimental.pallas import tpu as pltpu
from jax.sharding import PartitionSpec as P

KVH = 4
QPK = 8
HD = 128
AXES = ("groups", "node")
MASKED = -1e30
EXP2_SCALE = HD ** (-0.5) * math.log2(math.e)
VMEM_LIMIT = 28 * 1024 * 1024

ANY = pl.BlockSpec(memory_space=pl.ANY)
IN_SMEM = pl.BlockSpec(memory_space=pltpu.SMEM)
IN_VMEM = pl.BlockSpec(memory_space=pltpu.VMEM)


def scalars(*values):
    return jnp.stack([jnp.asarray(v).astype(jnp.int32) for v in values])


def rope_tables(positions):
    half = HD // 2
    freqs = 500000.0 ** (-(jnp.arange(half).astype(jnp.float32) * 2.0) / HD)
    angle = positions.astype(jnp.float32)[:, None] * freqs[None, :]
    return jnp.cos(angle), jnp.sin(angle)


def attend_kernel(rows, chunk, n_q, n_kv, resumed, last, place_ref, starts_ref, *refs):
    queries, refs = refs[:n_q], refs[n_q:]
    arrays, refs = refs[: 2 * n_kv], refs[2 * n_kv :]
    state, refs = (refs[:3], refs[3:]) if resumed else ((), refs)
    if last:
        outs, refs = refs[:n_q], refs[n_q:]
        kv, stacked, bias, stat_m, stat_l, acc = refs
    else:
        stat_m, stat_l, acc, kv, stacked, bias = refs
    part_rows = rows // n_q
    chunks = arrays[0].shape[0] // chunk

    if resumed:
        for old, new in zip(state, (stat_m, stat_l, acc)):
            new[...] = old[...]
    else:
        stat_m[...] = jnp.full_like(stat_m, MASKED)
        stat_l[...] = jnp.zeros_like(stat_l)
        acc[...] = jnp.zeros_like(acc)
    for h in range(QPK):
        for i in range(n_q):
            at = h * rows + i * part_rows
            stacked[at : at + part_rows, :] = queries[i][:, h * HD : (h + 1) * HD]
    for i in range(n_kv):
        kind = place_ref[n_q + n_kv + i]
        kv[i, kind] = arrays[2 * i][...]
        kv[i, 1 - kind] = arrays[2 * i + 1][...]

    first_key = place_ref[n_q + 2 * n_kv]
    last_row = place_ref[0]
    for i in range(1, n_q):
        last_row = jnp.maximum(last_row, place_ref[i])
    end_key = last_row + part_rows

    def attend_keys(i, at, begin, size):
        lanes = size // HD
        starts = jnp.concatenate([starts_ref[...]] * lanes, axis=1)
        q_pos = jnp.concatenate(
            [
                place_ref[part] + lax.broadcasted_iota(jnp.int32, (part_rows, size), 0)
                for part in range(n_q)
            ],
            axis=0,
        )
        k_pos = begin + lax.broadcasted_iota(jnp.int32, (rows, size), 1)
        bias[:, :size] = jnp.where((k_pos <= q_pos) & (k_pos >= starts), 0.0, MASKED)
        here = pl.ds(pl.multiple_of(at, size), size)
        score = lax.dot_general(
            stacked[...],
            kv[i, 0, here, :],
            (((1,), (1,)), ((), ())),
            preferred_element_type=jnp.float32,
        )
        score = (score.reshape(QPK, rows, size) + bias[:, :size][None]).reshape(QPK * rows, size)
        old = stat_m[...]
        top = jnp.maximum(old, jnp.max(score, axis=1, keepdims=True))
        expo = jnp.exp2((score - jnp.concatenate([top] * lanes, axis=1)) * EXP2_SCALE)
        factor = jnp.exp2((old - top) * EXP2_SCALE)
        stat_m[...] = top
        sums = expo[:, :HD]
        for lane in range(1, lanes):
            sums = sums + expo[:, lane * HD : (lane + 1) * HD]
        stat_l[...] = stat_l[...] * factor + sums
        part = jnp.dot(
            expo.astype(jnp.bfloat16),
            kv[i, 1, here, :],
            preferred_element_type=jnp.float32,
        )
        acc[...] = acc[...] * factor + part

    @pl.loop(0, n_kv * chunks)
    def _(step):
        i, j = step // chunks, step % chunks
        begin = (place_ref[n_q + i] * chunks + j) * chunk
        middle = begin + chunk // 2
        low = (begin >= 0) & (first_key < middle) & (end_key > begin)
        high = (begin >= 0) & (first_key < begin + chunk) & (end_key > middle)

        @pl.when(low & high)
        def _():
            attend_keys(i, j * chunk, begin, chunk)

        @pl.when(low != high)
        def _():
            half = jnp.where(high, chunk // 2, 0)
            attend_keys(i, j * chunk + half, begin + half, chunk // 2)

    if not last:
        return
    for h in range(QPK):
        at = slice(h * rows, (h + 1) * rows)
        done = acc[at, :] / jnp.sum(stat_l[at, :], axis=1, keepdims=True)
        for i in range(n_q):
            outs[i][:, h * HD : (h + 1) * HD] = done[
                i * part_rows : (i + 1) * part_rows
            ].astype(jnp.bfloat16)


def attend_starts(doc_ids, first_rows, rows):
    docs = [lax.dynamic_slice_in_dim(doc_ids, first, rows) for first in first_rows]
    docs = jnp.concatenate(docs)
    starts = jnp.sum((doc_ids[None, :] < docs[:, None]).astype(jnp.int32), axis=1)
    return jnp.broadcast_to(starts[:, None], (starts.shape[0], HD)), jnp.min(starts)[None]


def attend(place, starts, queries, arrays, tokens, chunk, state=(), last=True):
    rows = starts.shape[0]
    n_q, n_kv = len(queries), len(arrays) // 2
    part_rows = queries[0].shape[0]
    running = (QPK * rows, HD)
    if last:
        out_shape = [jax.ShapeDtypeStruct((part_rows, QPK * HD), jnp.bfloat16)] * n_q
    else:
        out_shape = [jax.ShapeDtypeStruct(running, jnp.float32)] * 3
    return pl.pallas_call(
        lambda *refs: attend_kernel(rows, chunk, n_q, n_kv, bool(state), last, *refs),
        out_shape=out_shape,
        in_specs=[IN_SMEM] + [IN_VMEM] * (1 + n_q + 2 * n_kv + len(state)),
        out_specs=[IN_VMEM] * len(out_shape),
        scratch_shapes=[
            pltpu.VMEM((n_kv, 2, *arrays[0].shape), jnp.bfloat16),
            pltpu.VMEM((QPK * rows, HD), jnp.bfloat16),
            pltpu.VMEM((rows, chunk), jnp.float32),
        ]
        + [pltpu.VMEM(running, jnp.float32)] * (3 if last else 0),
        compiler_params=pltpu.CompilerParams(vmem_limit_bytes=VMEM_LIMIT),
        cost_estimate=pl.CostEstimate(
            flops=rows * tokens * HD,
            bytes_accessed=rows * tokens,
            transcendentals=0,
        ),
        name="attend",
    )(place, starts, *queries, *arrays, *state)


def project_kernel(rows, n_hidden, n_pieces, place_ref, cos_ref, sin_ref, *refs):
    hidden = refs[:n_hidden]
    pieces = refs[n_hidden : n_hidden + n_pieces]
    out_ref, wbuf = refs[n_hidden + n_pieces :]

    for i in range(n_pieces):
        size = pieces[i].shape[0]

        @pl.when(place_ref[1 + n_hidden + 2 * i] == 1)
        def _():
            at = pl.multiple_of(place_ref[2 + n_hidden + 2 * i], size)
            wbuf[pl.ds(at, size), :] = pieces[i][...]

    heads = lax.dot_general(
        jnp.concatenate([block[...] for block in hidden], axis=0),
        wbuf[...],
        (((1,), (1,)), ((), ())),
        preferred_element_type=jnp.float32,
    )
    for i in range(n_hidden):
        at = pl.ds(pl.multiple_of(place_ref[1 + i] * rows, rows), rows)
        head = heads[i * rows : (i + 1) * rows]
        turned = head * cos_ref[at, :] + pltpu.roll(head, HD // 2, 1) * sin_ref[at, :]
        out_ref[at, :] = jnp.where(place_ref[0] == 1, turned, head).astype(jnp.bfloat16)


def project(place, cos, sin, hidden, pieces):
    rows, depth = hidden[0].shape
    n = len(hidden)
    return pl.pallas_call(
        lambda *refs: project_kernel(rows, n, len(pieces), *refs),
        out_shape=jax.ShapeDtypeStruct((n * rows, HD), jnp.bfloat16),
        in_specs=[IN_SMEM] + [IN_VMEM] * (2 + n + len(pieces)),
        out_specs=IN_VMEM,
        scratch_shapes=[pltpu.VMEM((HD, depth), jnp.bfloat16)],
        compiler_params=pltpu.CompilerParams(vmem_limit_bytes=VMEM_LIMIT),
        cost_estimate=pl.CostEstimate(
            flops=rows * depth * HD,
            bytes_accessed=rows * depth,
            transcendentals=0,
        ),
        name="project",
    )(place, cos, sin, *hidden, *pieces)


def join_kernel(place_ref, *refs):
    *parts, out_ref = refs
    for i, part in enumerate(parts):
        height, width = part.shape
        row = pl.multiple_of(place_ref[2 * i], height)
        at = pl.multiple_of(place_ref[2 * i + 1], width)
        out_ref[pl.ds(row, height), pl.ds(at, width)] = part[...]


def join(place, parts, shape):
    return pl.pallas_call(
        join_kernel,
        out_shape=jax.ShapeDtypeStruct(shape, parts[0].dtype),
        in_specs=[IN_SMEM] + [IN_VMEM] * len(parts),
        out_specs=IN_VMEM,
        compiler_params=pltpu.CompilerParams(vmem_limit_bytes=VMEM_LIMIT),
        name="join",
    )(place, *parts)


def by_planes(hidden, queries, kv_weight, doc_ids):
    rows = hidden.shape[0]
    tokens = doc_ids.shape[0]
    width = kv_weight.shape[1]
    part = width // 2
    columns = QPK * HD
    x = lax.axis_index("groups")
    node = lax.axis_index("node")
    z, y, c = node // 4, (node // 2) % 2, node % 2

    def hop(fn):
        pairs = []
        for i in range(32):
            to = fn(i // 16, (i // 4) % 4, (i // 2) % 2, i % 2)
            if to is not None:
                pairs.append((i, ((to[0] * 4 + to[1]) * 2 + to[2]) * 2 + to[3]))
        return lambda v: lax.ppermute(v, AXES, pairs)

    to_core = hop(lambda x, z, y, c: (x, z, y, 1 - c))
    to_y = hop(lambda x, z, y, c: (x, z, 1 - y, c))
    to_both = hop(lambda x, z, y, c: (x, z, 1 - y, 1 - c))
    to_x = hop(lambda x, z, y, c: (1 - x, z, y, c))
    near = hop(lambda x, z, y, c: (x, z ^ 1, y, c))
    far = hop(lambda x, z, y, c: (x, z ^ (2 + c), y, z % 2))
    up_near = hop(lambda x, z, y, c: (x, z + 1, y, c) if z % 2 == 0 else None)
    up_far = hop(lambda x, z, y, c: (x, z + 2, y, c) if z < 2 else None)
    swap_high = hop(lambda x, z, y, c: (x, z ^ 1, y, c) if z >= 2 else None)

    chunk = math.gcd(tokens, 512)
    tables = [[] for _ in range(7)]
    for i in range(32):
        ix, iz, iy, ic = i // 16, (i // 4) % 4, (i // 2) % 2, i % 2
        blocks = [2 * iy + ic, 2 * iy + 1 - ic, 2 * (1 - iy) + ic, 2 * (1 - iy) + 1 - ic]
        own = int(ic == iz % 2)
        tables[0].append(
            [int(iz < 2), *blocks]
            + [own, ic * width, 1 - own, ic * width, 1, (1 - ic) * width]
        )
        side = (1 - own) * width
        tables[6].append(
            [int(iz >= 2), *blocks]
            + [1, side + ix * part, 1, side + (1 - ix) * part]
            + [1, width - side + ix * part, 1, width - side + (1 - ix) * part]
        )
        planes = [iz, iz - 1 if iz % 2 else -1, iz - 2, (iz ^ 1) - 2 if iz >= 2 else -1]
        calls = [(1, 1 - iy, planes[:1]), (2, 1 - iy, planes[3:])]
        calls += [(3, iy, planes), (4, 1 - iy, planes[1:3])]
        for at, iy_rows, some in calls:
            first = [(4 * iz + 2 * iy_rows + core) * rows for core in (ic, 1 - ic)]
            kinds = [max(plane, 0) // 2 for plane in some]
            tables[at].append(first + some + kinds)
        heads = [iy + 2 * ic, iy + 2 * (1 - ic), iy + 2 * (1 - ic)]
        heads += [1 - iy + 2 * ic, 1 - iy + 2 * (1 - ic)]
        tops = [0, 0, rows // 2, 0, 0]
        tables[5].append([v for top, h in zip(tops, heads) for v in (top, h * columns)])
    widths = [len(t[0]) for t in tables]
    whole = np.concatenate([np.asarray(t, np.int32) for t in tables], axis=1)
    place = lax.dynamic_slice_in_dim(jnp.asarray(whole), x * 16 + node, 1, 0)[0]
    at, places = 0, []
    for w in widths:
        places.append(place[at : at + w])
        at += w

    weight = kv_weight.T
    far_0 = far(lax.dynamic_slice_in_dim(weight, x * part, part, 0))
    near_0 = near(weight)
    hidden_y = to_y(hidden)
    hidden_c = to_core(hidden)

    positions = z * 4 * rows + jnp.arange(4 * rows)
    cosine, sine = rope_tables(positions)
    cos = jnp.concatenate([cosine, cosine], axis=1)
    sin = jnp.concatenate([-sine, sine], axis=1)
    firsts = [
        [(4 * z + 2 * (1 - y) + c) * rows, (4 * z + 2 * (1 - y) + 1 - c) * rows],
        [(4 * z + 2 * y + c) * rows, (4 * z + 2 * y + 1 - c) * rows],
    ]
    starts, lowest = zip(*[attend_starts(doc_ids, first, rows) for first in firsts])
    for at, low in ((1, 0), (2, 0), (3, 1), (4, 0)):
        places[at] = jnp.concatenate([places[at], lowest[low]])
    q_own, *q_away = [
        lax.dynamic_slice_in_dim(queries, h * columns, columns, 1)
        for h in (y + 2 * c, y + 2 * (1 - c), 1 - y + 2 * c, 1 - y + 2 * (1 - c))
    ]
    far_0, cos, sin, starts, places, q_own, q_away = lax.optimization_barrier(
        (far_0, cos, sin, starts, places, q_own, q_away)
    )
    far_1, far_0x = near(far_0), to_x(far_0)
    far_1, far_0x = lax.optimization_barrier((far_1, far_0x))
    far_1x = to_x(far_1)
    near_c = to_core(jnp.where(c == z % 2, near_0, weight))
    q_core = to_core(q_away[0])
    hidden_y, far_1, q_away, q_core = lax.optimization_barrier((hidden_y, far_1, q_away, q_core))
    hidden_yc = to_core(hidden_y)
    q_y, q_both = to_y(q_away[1]), to_both(q_away[2])

    plane_hidden = [hidden, hidden_c, hidden_y, hidden_yc]
    kv_a = project(places[0], cos, sin, plane_hidden, [weight, near_0, near_c])
    kv_a, places[6] = lax.optimization_barrier((kv_a, places[6]))
    kv_b = project(places[6], cos, sin, plane_hidden, [far_0, far_0x, far_1, far_1x])

    a_near, a_far = up_near(kv_a), up_far(kv_a)
    b_near, b_far = up_near(kv_b), up_far(kv_b)
    own, near_below = [kv_a, kv_b], [a_near, b_near]
    q_partner = [q_y, q_both]
    begun = attend(places[1], starts[0], q_partner, own, tokens, chunk, last=False)
    begun, a_far = lax.optimization_barrier((begun, a_far))
    other = [swap_high(a_far), swap_high(b_far)]
    below = near_below + [a_far, b_far]
    begun = attend(places[4], starts[0], q_partner, below, tokens, chunk, begun, last=False)
    across = attend(places[2], starts[0], q_partner, other, tokens, chunk, begun)
    back = [to_y(across[0]), to_both(across[1])]
    stored = own + below + other
    across, places[3] = lax.optimization_barrier((across, places[3]))
    here, beside = attend(places[3], starts[1], [q_own, q_core], stored, tokens, chunk)
    parts = [here, to_core(beside[: rows // 2]), to_core(beside[rows // 2 :])] + back
    return join(places[5], parts, queries.shape)


def by_gathers(hidden, queries, kv_weight, doc_ids):
    rows = hidden.shape[0]
    tokens = doc_ids.shape[0]
    me = lax.axis_index("node")
    whole = lax.all_gather(kv_weight, "node", axis=1, tiled=True)
    projected = jnp.dot(hidden, whole, preferred_element_type=jnp.float32)
    split = whole.shape[1] // 2
    cosine, sine = rope_tables(me * rows + jnp.arange(rows))
    keys = projected[:, :split].reshape(rows, KVH, HD)
    a, b = keys[..., : HD // 2], keys[..., HD // 2 :]
    cosine, sine = cosine[:, None, :], sine[:, None, :]
    keys = jnp.concatenate([a * cosine - b * sine, b * cosine + a * sine], axis=-1)
    both = jnp.concatenate([keys, projected[:, split:].reshape(rows, KVH, HD)], axis=1)
    both = both.astype(jnp.bfloat16).transpose(1, 0, 2)
    whole = lax.all_gather(both, "node", axis=1, tiled=True)
    chunk = math.gcd(tokens, 512)
    starts, lowest = attend_starts(doc_ids, [me * rows], rows)
    place = jnp.concatenate([scalars(me * rows, 0, 0), lowest])
    outs = []
    for g in range(KVH):
        pair = [whole[g], whole[KVH + g]]
        mine = queries[:, g * QPK * HD : (g + 1) * QPK * HD]
        outs += attend(place, starts, [mine], pair, tokens, chunk)
    return jnp.concatenate(outs, axis=1)


def solution(mesh):
    planes = mesh.shape["groups"] == 2 and mesh.shape["node"] == 16
    in_specs = (P(AXES, None), P(AXES, None), P(None, "node"), P("groups"))
    return jax.shard_map(
        by_planes if planes else by_gathers,
        mesh=mesh,
        in_specs=in_specs,
        out_specs=P(AXES, None),
        check_vma=False,
    )
```

```python
import math

import jax
import jax.numpy as jnp
import numpy as np
from jax import lax
from jax.experimental import pallas as pl
from jax.experimental.pallas import tpu as pltpu
from jax.sharding import PartitionSpec as P

KVH = 4
QPK = 8
HD = 128
AXES = ("groups", "node")
MASKED = -1e30
EXP2_SCALE = HD ** (-0.5) * math.log2(math.e)
VMEM_LIMIT = 28 * 1024 * 1024

ANY = pl.BlockSpec(memory_space=pl.ANY)
IN_SMEM = pl.BlockSpec(memory_space=pltpu.SMEM)
IN_VMEM = pl.BlockSpec(memory_space=pltpu.VMEM)


def scalars(*values):
    return jnp.stack([jnp.asarray(v).astype(jnp.int32) for v in values])


def rope_tables(positions):
    half = HD // 2
    freqs = 500000.0 ** (-(jnp.arange(half).astype(jnp.float32) * 2.0) / HD)
    angle = positions.astype(jnp.float32)[:, None] * freqs[None, :]
    return jnp.cos(angle), jnp.sin(angle)


def attend_kernel(rows, chunk, n_q, n_kv, resumed, last, place_ref, starts_ref, *refs):
    queries, refs = refs[:n_q], refs[n_q:]
    arrays, refs = refs[: 2 * n_kv], refs[2 * n_kv :]
    state, refs = (refs[:3], refs[3:]) if resumed else ((), refs)
    if last:
        outs, refs = refs[:n_q], refs[n_q:]
        kv, stacked, bias, stat_m, stat_l, acc = refs
    else:
        stat_m, stat_l, acc, kv, stacked, bias = refs
    part_rows = rows // n_q
    chunks = arrays[0].shape[0] // chunk

    if resumed:
        for old, new in zip(state, (stat_m, stat_l, acc)):
            new[...] = old[...]
    else:
        stat_m[...] = jnp.full_like(stat_m, MASKED)
        stat_l[...] = jnp.zeros_like(stat_l)
        acc[...] = jnp.zeros_like(acc)
    for h in range(QPK):
        for i in range(n_q):
            at = h * rows + i * part_rows
            stacked[at : at + part_rows, :] = queries[i][:, h * HD : (h + 1) * HD]
    for i in range(n_kv):
        kind = place_ref[n_q + n_kv + i]
        kv[i, kind] = arrays[2 * i][...]
        kv[i, 1 - kind] = arrays[2 * i + 1][...]

    first_key = place_ref[n_q + 2 * n_kv]
    last_row = place_ref[0]
    for i in range(1, n_q):
        last_row = jnp.maximum(last_row, place_ref[i])
    end_key = last_row + part_rows

    def attend_keys(i, at, begin, size):
        lanes = size // HD
        starts = jnp.concatenate([starts_ref[...]] * lanes, axis=1)
        q_pos = jnp.concatenate(
            [
                place_ref[part] + lax.broadcasted_iota(jnp.int32, (part_rows, size), 0)
                for part in range(n_q)
            ],
            axis=0,
        )
        k_pos = begin + lax.broadcasted_iota(jnp.int32, (rows, size), 1)
        bias[:, :size] = jnp.where((k_pos <= q_pos) & (k_pos >= starts), 0.0, MASKED)
        here = pl.ds(pl.multiple_of(at, size), size)
        score = lax.dot_general(
            stacked[...],
            kv[i, 0, here, :],
            (((1,), (1,)), ((), ())),
            preferred_element_type=jnp.float32,
        )
        score = (score.reshape(QPK, rows, size) + bias[:, :size][None]).reshape(QPK * rows, size)
        old = stat_m[...]
        top = jnp.maximum(old, jnp.max(score, axis=1, keepdims=True))
        expo = jnp.exp2((score - jnp.concatenate([top] * lanes, axis=1)) * EXP2_SCALE)
        factor = jnp.exp2((old - top) * EXP2_SCALE)
        stat_m[...] = top
        sums = expo[:, :HD]
        for lane in range(1, lanes):
            sums = sums + expo[:, lane * HD : (lane + 1) * HD]
        stat_l[...] = stat_l[...] * factor + sums
        part = jnp.dot(
            expo.astype(jnp.bfloat16),
            kv[i, 1, here, :],
            preferred_element_type=jnp.float32,
        )
        acc[...] = acc[...] * factor + part

    @pl.loop(0, n_kv * chunks)
    def _(step):
        i, j = step // chunks, step % chunks
        begin = (place_ref[n_q + i] * chunks + j) * chunk
        middle = begin + chunk // 2
        low = (begin >= 0) & (first_key < middle) & (end_key > begin)
        high = (begin >= 0) & (first_key < begin + chunk) & (end_key > middle)

        @pl.when(low & high)
        def _():
            attend_keys(i, j * chunk, begin, chunk)

        @pl.when(low != high)
        def _():
            half = jnp.where(high, chunk // 2, 0)
            attend_keys(i, j * chunk + half, begin + half, chunk // 2)

    if not last:
        return
    for h in range(QPK):
        at = slice(h * rows, (h + 1) * rows)
        done = acc[at, :] / jnp.sum(stat_l[at, :], axis=1, keepdims=True)
        for i in range(n_q):
            outs[i][:, h * HD : (h + 1) * HD] = done[
                i * part_rows : (i + 1) * part_rows
            ].astype(jnp.bfloat16)


def attend_starts(doc_ids, first_rows, rows):
    docs = [lax.dynamic_slice_in_dim(doc_ids, first, rows) for first in first_rows]
    docs = jnp.concatenate(docs)
    starts = jnp.sum((doc_ids[None, :] < docs[:, None]).astype(jnp.int32), axis=1)
    return jnp.broadcast_to(starts[:, None], (starts.shape[0], HD)), jnp.min(starts)[None]


def attend(place, starts, queries, arrays, tokens, chunk, state=(), last=True):
    rows = starts.shape[0]
    n_q, n_kv = len(queries), len(arrays) // 2
    part_rows = queries[0].shape[0]
    running = (QPK * rows, HD)
    if last:
        out_shape = [jax.ShapeDtypeStruct((part_rows, QPK * HD), jnp.bfloat16)] * n_q
    else:
        out_shape = [jax.ShapeDtypeStruct(running, jnp.float32)] * 3
    return pl.pallas_call(
        lambda *refs: attend_kernel(rows, chunk, n_q, n_kv, bool(state), last, *refs),
        out_shape=out_shape,
        in_specs=[IN_SMEM] + [IN_VMEM] * (1 + n_q + 2 * n_kv + len(state)),
        out_specs=[IN_VMEM] * len(out_shape),
        scratch_shapes=[
            pltpu.VMEM((n_kv, 2, *arrays[0].shape), jnp.bfloat16),
            pltpu.VMEM((QPK * rows, HD), jnp.bfloat16),
            pltpu.VMEM((rows, chunk), jnp.float32),
        ]
        + [pltpu.VMEM(running, jnp.float32)] * (3 if last else 0),
        compiler_params=pltpu.CompilerParams(vmem_limit_bytes=VMEM_LIMIT),
        cost_estimate=pl.CostEstimate(
            flops=rows * tokens * HD,
            bytes_accessed=rows * tokens,
            transcendentals=0,
        ),
        name="attend",
    )(place, starts, *queries, *arrays, *state)


def project_kernel(rows, n_hidden, n_pieces, place_ref, cos_ref, sin_ref, *refs):
    hidden = refs[:n_hidden]
    pieces = refs[n_hidden : n_hidden + n_pieces]
    out_ref, wbuf = refs[n_hidden + n_pieces :]

    for i in range(n_pieces):
        size = pieces[i].shape[0]

        @pl.when(place_ref[1 + n_hidden + 2 * i] == 1)
        def _():
            at = pl.multiple_of(place_ref[2 + n_hidden + 2 * i], size)
            wbuf[pl.ds(at, size), :] = pieces[i][...]

    heads = lax.dot_general(
        jnp.concatenate([block[...] for block in hidden], axis=0),
        wbuf[...],
        (((1,), (1,)), ((), ())),
        preferred_element_type=jnp.float32,
    )
    for i in range(n_hidden):
        at = pl.ds(pl.multiple_of(place_ref[1 + i] * rows, rows), rows)
        head = heads[i * rows : (i + 1) * rows]
        turned = head * cos_ref[at, :] + pltpu.roll(head, HD // 2, 1) * sin_ref[at, :]
        out_ref[at, :] = jnp.where(place_ref[0] == 1, turned, head).astype(jnp.bfloat16)


def project(place, cos, sin, hidden, pieces):
    rows, depth = hidden[0].shape
    n = len(hidden)
    return pl.pallas_call(
        lambda *refs: project_kernel(rows, n, len(pieces), *refs),
        out_shape=jax.ShapeDtypeStruct((n * rows, HD), jnp.bfloat16),
        in_specs=[IN_SMEM] + [IN_VMEM] * (2 + n + len(pieces)),
        out_specs=IN_VMEM,
        scratch_shapes=[pltpu.VMEM((HD, depth), jnp.bfloat16)],
        compiler_params=pltpu.CompilerParams(vmem_limit_bytes=VMEM_LIMIT),
        cost_estimate=pl.CostEstimate(
            flops=rows * depth * HD,
            bytes_accessed=rows * depth,
            transcendentals=0,
        ),
        name="project",
    )(place, cos, sin, *hidden, *pieces)


def by_planes(hidden, queries, kv_weight, doc_ids):
    rows = hidden.shape[0]
    tokens = doc_ids.shape[0]
    width = kv_weight.shape[1]
    part = width // 2
    columns = QPK * HD
    x = lax.axis_index("groups")
    node = lax.axis_index("node")
    z, y, c = node // 4, (node // 2) % 2, node % 2

    def hop(fn):
        pairs = []
        for i in range(32):
            to = fn(i // 16, (i // 4) % 4, (i // 2) % 2, i % 2)
            if to is not None:
                pairs.append((i, ((to[0] * 4 + to[1]) * 2 + to[2]) * 2 + to[3]))
        return lambda v: lax.ppermute(v, AXES, pairs)

    to_core = hop(lambda x, z, y, c: (x, z, y, 1 - c))
    to_y = hop(lambda x, z, y, c: (x, z, 1 - y, c))
    to_both = hop(lambda x, z, y, c: (x, z, 1 - y, 1 - c))
    to_x = hop(lambda x, z, y, c: (1 - x, z, y, c))
    near = hop(lambda x, z, y, c: (x, z ^ 1, y, c))
    far = hop(lambda x, z, y, c: (x, z ^ (2 + c), y, z % 2))
    up_near = hop(lambda x, z, y, c: (x, z + 1, y, c) if z % 2 == 0 else None)
    up_far = hop(lambda x, z, y, c: (x, z + 2, y, c) if z < 2 else None)
    swap_high = hop(lambda x, z, y, c: (x, z ^ 1, y, c) if z >= 2 else None)

    chunk = math.gcd(tokens, 512)
    tables = [[] for _ in range(6)]
    for i in range(32):
        ix, iz, iy, ic = i // 16, (i // 4) % 4, (i // 2) % 2, i % 2
        blocks = [2 * iy + ic, 2 * iy + 1 - ic, 2 * (1 - iy) + ic, 2 * (1 - iy) + 1 - ic]
        own = int(ic == iz % 2)
        tables[0].append(
            [int(iz < 2), *blocks]
            + [own, ic * width, 1 - own, ic * width, 1, (1 - ic) * width]
        )
        side = (1 - own) * width
        tables[5].append(
            [int(iz >= 2), *blocks]
            + [1, side + ix * part, 1, side + (1 - ix) * part]
            + [1, width - side + ix * part, 1, width - side + (1 - ix) * part]
        )
        planes = [iz, iz - 1 if iz % 2 else -1, iz - 2, (iz ^ 1) - 2 if iz >= 2 else -1]
        calls = [(1, 1 - iy, planes[:1]), (2, 1 - iy, planes[3:])]
        calls += [(3, iy, planes), (4, 1 - iy, planes[1:3])]
        for at, iy_rows, some in calls:
            first = [(4 * iz + 2 * iy_rows + core) * rows for core in (ic, 1 - ic)]
            kinds = [max(plane, 0) // 2 for plane in some]
            tables[at].append(first + some + kinds)
    widths = [len(t[0]) for t in tables]
    whole = np.concatenate([np.asarray(t, np.int32) for t in tables], axis=1)
    place = lax.dynamic_slice_in_dim(jnp.asarray(whole), x * 16 + node, 1, 0)[0]
    at, places = 0, []
    for w in widths:
        places.append(place[at : at + w])
        at += w

    weight = kv_weight.T
    far_0 = far(lax.dynamic_slice_in_dim(weight, x * part, part, 0))
    near_0 = near(weight)
    hidden_y = to_y(hidden)
    hidden_c = to_core(hidden)

    positions = z * 4 * rows + jnp.arange(4 * rows)
    cosine, sine = rope_tables(positions)
    cos = jnp.concatenate([cosine, cosine], axis=1)
    sin = jnp.concatenate([-sine, sine], axis=1)
    firsts = [
        [(4 * z + 2 * (1 - y) + c) * rows, (4 * z + 2 * (1 - y) + 1 - c) * rows],
        [(4 * z + 2 * y + c) * rows, (4 * z + 2 * y + 1 - c) * rows],
    ]
    starts, lowest = zip(*[attend_starts(doc_ids, first, rows) for first in firsts])
    for at, low in ((1, 0), (2, 0), (3, 1), (4, 0)):
        places[at] = jnp.concatenate([places[at], lowest[low]])
    q_own, *q_away = [
        lax.dynamic_slice_in_dim(queries, h * columns, columns, 1)
        for h in (y + 2 * c, y + 2 * (1 - c), 1 - y + 2 * c, 1 - y + 2 * (1 - c))
    ]
    far_0, cos, sin, starts, places, q_own, q_away = lax.optimization_barrier(
        (far_0, cos, sin, starts, places, q_own, q_away)
    )
    far_1, far_0x = near(far_0), to_x(far_0)
    far_1, far_0x = lax.optimization_barrier((far_1, far_0x))
    far_1x = to_x(far_1)
    near_c = to_core(jnp.where(c == z % 2, near_0, weight))
    q_core = to_core(q_away[0])
    hidden_y, far_1, q_away, q_core = lax.optimization_barrier((hidden_y, far_1, q_away, q_core))
    hidden_yc = to_core(hidden_y)
    q_y, q_both = to_y(q_away[1]), to_both(q_away[2])

    plane_hidden = [hidden, hidden_c, hidden_y, hidden_yc]
    kv_a = project(places[0], cos, sin, plane_hidden, [weight, near_0, near_c])
    kv_a, places[5] = lax.optimization_barrier((kv_a, places[5]))
    kv_b = project(places[5], cos, sin, plane_hidden, [far_0, far_0x, far_1, far_1x])

    a_near, a_far = up_near(kv_a), up_far(kv_a)
    b_near, b_far = up_near(kv_b), up_far(kv_b)
    own, near_below = [kv_a, kv_b], [a_near, b_near]
    q_partner = [q_y, q_both]
    begun = attend(places[1], starts[0], q_partner, own, tokens, chunk, last=False)
    begun, a_far = lax.optimization_barrier((begun, a_far))
    other = [swap_high(a_far), swap_high(b_far)]
    below = near_below + [a_far, b_far]
    begun = attend(places[4], starts[0], q_partner, below, tokens, chunk, begun, last=False)
    across = attend(places[2], starts[0], q_partner, other, tokens, chunk, begun)
    back = [to_y(across[0]), to_both(across[1])]
    stored = own + below + other
    across, places[3] = lax.optimization_barrier((across, places[3]))
    here, beside = attend(places[3], starts[1], [q_own, q_core], stored, tokens, chunk)
    halves = [to_core(beside[: rows // 2]), to_core(beside[rows // 2 :])]
    here, halves, back = lax.optimization_barrier((here, halves, back))
    same_y = [here, jnp.concatenate(halves, axis=0)]
    heads = []
    for h in range(KVH):
        mine = jnp.where(h // 2 == c, same_y[0], same_y[1])
        other_y = jnp.where(h // 2 == c, back[0], back[1])
        heads.append(jnp.where(h % 2 == y, mine, other_y))
    return jnp.concatenate(heads, axis=1)


def by_gathers(hidden, queries, kv_weight, doc_ids):
    rows = hidden.shape[0]
    tokens = doc_ids.shape[0]
    me = lax.axis_index("node")
    whole = lax.all_gather(kv_weight, "node", axis=1, tiled=True)
    projected = jnp.dot(hidden, whole, preferred_element_type=jnp.float32)
    split = whole.shape[1] // 2
    cosine, sine = rope_tables(me * rows + jnp.arange(rows))
    keys = projected[:, :split].reshape(rows, KVH, HD)
    a, b = keys[..., : HD // 2], keys[..., HD // 2 :]
    cosine, sine = cosine[:, None, :], sine[:, None, :]
    keys = jnp.concatenate([a * cosine - b * sine, b * cosine + a * sine], axis=-1)
    both = jnp.concatenate([keys, projected[:, split:].reshape(rows, KVH, HD)], axis=1)
    both = both.astype(jnp.bfloat16).transpose(1, 0, 2)
    whole = lax.all_gather(both, "node", axis=1, tiled=True)
    chunk = math.gcd(tokens, 512)
    starts, lowest = attend_starts(doc_ids, [me * rows], rows)
    place = jnp.concatenate([scalars(me * rows, 0, 0), lowest])
    outs = []
    for g in range(KVH):
        pair = [whole[g], whole[KVH + g]]
        mine = queries[:, g * QPK * HD : (g + 1) * QPK * HD]
        outs += attend(place, starts, [mine], pair, tokens, chunk)
    return jnp.concatenate(outs, axis=1)


def solution(mesh):
    planes = mesh.shape["groups"] == 2 and mesh.shape["node"] == 16
    in_specs = (P(AXES, None), P(AXES, None), P(None, "node"), P("groups"))
    return jax.shard_map(
        by_planes if planes else by_gathers,
        mesh=mesh,
        in_specs=in_specs,
        out_specs=P(AXES, None),
        check_vma=False,
    )
```

```python
import math

import jax
import jax.numpy as jnp
import numpy as np
from jax import lax
from jax.experimental import pallas as pl
from jax.experimental.pallas import tpu as pltpu
from jax.sharding import PartitionSpec as P

KVH = 4
QPK = 8
HD = 128
AXES = ("groups", "node")
MASKED = -1e30
EXP2_SCALE = HD ** (-0.5) * math.log2(math.e)
VMEM_LIMIT = 28 * 1024 * 1024

ANY = pl.BlockSpec(memory_space=pl.ANY)
IN_SMEM = pl.BlockSpec(memory_space=pltpu.SMEM)
IN_VMEM = pl.BlockSpec(memory_space=pltpu.VMEM)


def scalars(*values):
    return jnp.stack([jnp.asarray(v).astype(jnp.int32) for v in values])


def rope_tables(positions):
    half = HD // 2
    freqs = 500000.0 ** (-(jnp.arange(half).astype(jnp.float32) * 2.0) / HD)
    angle = positions.astype(jnp.float32)[:, None] * freqs[None, :]
    return jnp.cos(angle), jnp.sin(angle)


def attend_kernel(rows, chunk, n_q, n_kv, resumed, last, place_ref, starts_ref, *refs):
    queries, refs = refs[:n_q], refs[n_q:]
    arrays, refs = refs[: 2 * n_kv], refs[2 * n_kv :]
    state, refs = (refs[:3], refs[3:]) if resumed else ((), refs)
    if last:
        outs, refs = refs[:n_q], refs[n_q:]
        kv, stacked, bias, stat_m, stat_l, acc = refs
    else:
        stat_m, stat_l, acc, kv, stacked, bias = refs
    part_rows = rows // n_q
    chunks = arrays[0].shape[0] // chunk

    if resumed:
        for old, new in zip(state, (stat_m, stat_l, acc)):
            new[...] = old[...]
    else:
        stat_m[...] = jnp.full_like(stat_m, MASKED)
        stat_l[...] = jnp.zeros_like(stat_l)
        acc[...] = jnp.zeros_like(acc)
    for h in range(QPK):
        for i in range(n_q):
            at = h * rows + i * part_rows
            stacked[at : at + part_rows, :] = queries[i][:, h * HD : (h + 1) * HD]
    for i in range(n_kv):
        kind = place_ref[n_q + n_kv + i]
        kv[i, kind] = arrays[2 * i][...]
        kv[i, 1 - kind] = arrays[2 * i + 1][...]

    first_key = place_ref[n_q + 2 * n_kv]
    last_row = place_ref[0]
    for i in range(1, n_q):
        last_row = jnp.maximum(last_row, place_ref[i])
    end_key = last_row + part_rows

    def attend_keys(i, at, begin, size):
        lanes = size // HD
        starts = jnp.concatenate([starts_ref[...]] * lanes, axis=1)
        q_pos = jnp.concatenate(
            [
                place_ref[part] + lax.broadcasted_iota(jnp.int32, (part_rows, size), 0)
                for part in range(n_q)
            ],
            axis=0,
        )
        k_pos = begin + lax.broadcasted_iota(jnp.int32, (rows, size), 1)
        bias[:, :size] = jnp.where((k_pos <= q_pos) & (k_pos >= starts), 0.0, MASKED)
        here = pl.ds(pl.multiple_of(at, size), size)
        score = lax.dot_general(
            stacked[...],
            kv[i, 0, here, :],
            (((1,), (1,)), ((), ())),
            preferred_element_type=jnp.float32,
        )
        score = (score.reshape(QPK, rows, size) + bias[:, :size][None]).reshape(QPK * rows, size)
        old = stat_m[...]
        top = jnp.maximum(old, jnp.max(score, axis=1, keepdims=True))
        expo = jnp.exp2((score - jnp.concatenate([top] * lanes, axis=1)) * EXP2_SCALE)
        factor = jnp.exp2((old - top) * EXP2_SCALE)
        stat_m[...] = top
        sums = expo[:, :HD]
        for lane in range(1, lanes):
            sums = sums + expo[:, lane * HD : (lane + 1) * HD]
        stat_l[...] = stat_l[...] * factor + sums
        part = jnp.dot(
            expo.astype(jnp.bfloat16),
            kv[i, 1, here, :],
            preferred_element_type=jnp.float32,
        )
        acc[...] = acc[...] * factor + part

    @pl.loop(0, n_kv * chunks)
    def _(step):
        i, j = step // chunks, step % chunks
        begin = (place_ref[n_q + i] * chunks + j) * chunk
        middle = begin + chunk // 2
        low = (begin >= 0) & (first_key < middle) & (end_key > begin)
        high = (begin >= 0) & (first_key < begin + chunk) & (end_key > middle)

        @pl.when(low & high)
        def _():
            attend_keys(i, j * chunk, begin, chunk)

        @pl.when(low != high)
        def _():
            half = jnp.where(high, chunk // 2, 0)
            attend_keys(i, j * chunk + half, begin + half, chunk // 2)

    if not last:
        return
    for h in range(QPK):
        at = slice(h * rows, (h + 1) * rows)
        done = acc[at, :] / jnp.sum(stat_l[at, :], axis=1, keepdims=True)
        for i in range(n_q):
            outs[i][:, h * HD : (h + 1) * HD] = done[
                i * part_rows : (i + 1) * part_rows
            ].astype(jnp.bfloat16)


def attend_starts(doc_ids, first_rows, rows):
    docs = [lax.dynamic_slice_in_dim(doc_ids, first, rows) for first in first_rows]
    docs = jnp.concatenate(docs)
    starts = jnp.sum((doc_ids[None, :] < docs[:, None]).astype(jnp.int32), axis=1)
    return jnp.broadcast_to(starts[:, None], (starts.shape[0], HD)), jnp.min(starts)[None]


def attend(place, starts, queries, arrays, tokens, chunk, state=(), last=True):
    rows = starts.shape[0]
    n_q, n_kv = len(queries), len(arrays) // 2
    part_rows = queries[0].shape[0]
    running = (QPK * rows, HD)
    if last:
        out_shape = [jax.ShapeDtypeStruct((part_rows, QPK * HD), jnp.bfloat16)] * n_q
    else:
        out_shape = [jax.ShapeDtypeStruct(running, jnp.float32)] * 3
    return pl.pallas_call(
        lambda *refs: attend_kernel(rows, chunk, n_q, n_kv, bool(state), last, *refs),
        out_shape=out_shape,
        in_specs=[IN_SMEM] + [IN_VMEM] * (1 + n_q + 2 * n_kv + len(state)),
        out_specs=[IN_VMEM] * len(out_shape),
        scratch_shapes=[
            pltpu.VMEM((n_kv, 2, *arrays[0].shape), jnp.bfloat16),
            pltpu.VMEM((QPK * rows, HD), jnp.bfloat16),
            pltpu.VMEM((rows, chunk), jnp.float32),
        ]
        + [pltpu.VMEM(running, jnp.float32)] * (3 if last else 0),
        compiler_params=pltpu.CompilerParams(vmem_limit_bytes=VMEM_LIMIT),
        cost_estimate=pl.CostEstimate(
            flops=rows * tokens * HD,
            bytes_accessed=rows * tokens,
            transcendentals=0,
        ),
        name="attend",
    )(place, starts, *queries, *arrays, *state)


def project_kernel(rows, n_hidden, n_pieces, place_ref, cos_ref, sin_ref, *refs):
    hidden = refs[:n_hidden]
    pieces = refs[n_hidden : n_hidden + n_pieces]
    out_ref, wbuf = refs[n_hidden + n_pieces :]

    for i in range(n_pieces):
        size = pieces[i].shape[0]

        @pl.when(place_ref[1 + n_hidden + 2 * i] == 1)
        def _():
            at = pl.multiple_of(place_ref[2 + n_hidden + 2 * i], size)
            wbuf[pl.ds(at, size), :] = pieces[i][...]

    heads = lax.dot_general(
        jnp.concatenate([block[...] for block in hidden], axis=0),
        wbuf[...],
        (((1,), (1,)), ((), ())),
        preferred_element_type=jnp.float32,
    )
    for i in range(n_hidden):
        at = pl.ds(pl.multiple_of(place_ref[1 + i] * rows, rows), rows)
        head = heads[i * rows : (i + 1) * rows]
        turned = head * cos_ref[at, :] + pltpu.roll(head, HD // 2, 1) * sin_ref[at, :]
        out_ref[at, :] = jnp.where(place_ref[0] == 1, turned, head).astype(jnp.bfloat16)


def project(place, cos, sin, hidden, pieces):
    rows, depth = hidden[0].shape
    n = len(hidden)
    return pl.pallas_call(
        lambda *refs: project_kernel(rows, n, len(pieces), *refs),
        out_shape=jax.ShapeDtypeStruct((n * rows, HD), jnp.bfloat16),
        in_specs=[IN_SMEM] + [IN_VMEM] * (2 + n + len(pieces)),
        out_specs=IN_VMEM,
        scratch_shapes=[pltpu.VMEM((HD, depth), jnp.bfloat16)],
        compiler_params=pltpu.CompilerParams(vmem_limit_bytes=VMEM_LIMIT),
        cost_estimate=pl.CostEstimate(
            flops=rows * depth * HD,
            bytes_accessed=rows * depth,
            transcendentals=0,
        ),
        name="project",
    )(place, cos, sin, *hidden, *pieces)


def by_planes(hidden, queries, kv_weight, doc_ids):
    rows = hidden.shape[0]
    tokens = doc_ids.shape[0]
    width = kv_weight.shape[1]
    part = width // 2
    columns = QPK * HD
    x = lax.axis_index("groups")
    node = lax.axis_index("node")
    z, y, c = node // 4, (node // 2) % 2, node % 2

    def hop(fn):
        pairs = []
        for i in range(32):
            to = fn(i // 16, (i // 4) % 4, (i // 2) % 2, i % 2)
            if to is not None:
                pairs.append((i, ((to[0] * 4 + to[1]) * 2 + to[2]) * 2 + to[3]))
        return lambda v: lax.ppermute(v, AXES, pairs)

    to_core = hop(lambda x, z, y, c: (x, z, y, 1 - c))
    to_y = hop(lambda x, z, y, c: (x, z, 1 - y, c))
    to_both = hop(lambda x, z, y, c: (x, z, 1 - y, 1 - c))
    to_x = hop(lambda x, z, y, c: (1 - x, z, y, c))
    near = hop(lambda x, z, y, c: (x, z ^ 1, y, c))
    far = hop(lambda x, z, y, c: (x, z ^ (2 + c), y, z % 2))
    up_near = hop(lambda x, z, y, c: (x, z + 1, y, c) if z % 2 == 0 else None)
    up_far = hop(lambda x, z, y, c: (x, z + 2, y, c) if z < 2 else None)
    swap_high = hop(lambda x, z, y, c: (x, z ^ 1, y, c) if z >= 2 else None)

    chunk = math.gcd(tokens, 512)
    tables = [[] for _ in range(7)]
    for i in range(32):
        ix, iz, iy, ic = i // 16, (i // 4) % 4, (i // 2) % 2, i % 2
        blocks = [2 * iy + ic, 2 * iy + 1 - ic, 2 * (1 - iy) + ic, 2 * (1 - iy) + 1 - ic]
        own = int(ic == iz % 2)
        tables[0].append(
            [int(iz < 2), *blocks]
            + [own, ic * width, 1 - own, ic * width, 1, (1 - ic) * width]
        )
        side = (1 - own) * width
        tables[5].append(
            [int(iz >= 2), *blocks]
            + [1, side + ix * part, 1, side + (1 - ix) * part]
            + [1, width - side + ix * part, 1, width - side + (1 - ix) * part]
        )
        planes = [iz, iz - 1 if iz % 2 else -1, iz - 2, (iz ^ 1) - 2 if iz >= 2 else -1]
        calls = [(1, 1 - iy, planes[:1]), (2, 1 - iy, planes[3:])]
        calls += [(3, iy, planes), (4, 1 - iy, planes[1:3]), (6, iy, planes)]
        for at, iy_rows, some in calls:
            cores = {3: [1 - ic], 6: [ic]}.get(at, [ic, 1 - ic])
            first = [(4 * iz + 2 * iy_rows + core) * rows for core in cores]
            kinds = [max(plane, 0) // 2 for plane in some]
            tables[at].append(first + some + kinds)
    widths = [len(t[0]) for t in tables]
    whole = np.concatenate([np.asarray(t, np.int32) for t in tables], axis=1)
    place = lax.dynamic_slice_in_dim(jnp.asarray(whole), x * 16 + node, 1, 0)[0]
    at, places = 0, []
    for w in widths:
        places.append(place[at : at + w])
        at += w

    weight = kv_weight.T
    far_0 = far(lax.dynamic_slice_in_dim(weight, x * part, part, 0))
    near_0 = near(weight)
    hidden_y = to_y(hidden)
    hidden_c = to_core(hidden)

    positions = z * 4 * rows + jnp.arange(4 * rows)
    cosine, sine = rope_tables(positions)
    cos = jnp.concatenate([cosine, cosine], axis=1)
    sin = jnp.concatenate([-sine, sine], axis=1)
    firsts = [
        [(4 * z + 2 * (1 - y) + c) * rows, (4 * z + 2 * (1 - y) + 1 - c) * rows],
        [(4 * z + 2 * y + c) * rows, (4 * z + 2 * y + 1 - c) * rows],
    ]
    starts, lowest = zip(*[attend_starts(doc_ids, first, rows) for first in firsts])
    starts = [starts[0], starts[1][:rows], starts[1][rows:]]
    for at, low in ((1, 0), (2, 0), (3, 1), (4, 0), (6, 1)):
        places[at] = jnp.concatenate([places[at], lowest[low]])
    q_own, *q_away = [
        lax.dynamic_slice_in_dim(queries, h * columns, columns, 1)
        for h in (y + 2 * c, y + 2 * (1 - c), 1 - y + 2 * c, 1 - y + 2 * (1 - c))
    ]
    far_0, cos, sin, starts, places, q_own, q_away = lax.optimization_barrier(
        (far_0, cos, sin, starts, places, q_own, q_away)
    )
    far_1, far_0x = near(far_0), to_x(far_0)
    far_1, far_0x = lax.optimization_barrier((far_1, far_0x))
    far_1x = to_x(far_1)
    near_c = to_core(jnp.where(c == z % 2, near_0, weight))
    q_core = to_core(q_away[0])
    hidden_y, far_1, q_away, q_core = lax.optimization_barrier((hidden_y, far_1, q_away, q_core))
    hidden_yc = to_core(hidden_y)
    q_y, q_both = to_y(q_away[1]), to_both(q_away[2])

    plane_hidden = [hidden, hidden_c, hidden_y, hidden_yc]
    kv_a = project(places[0], cos, sin, plane_hidden, [weight, near_0, near_c])
    kv_a, places[5] = lax.optimization_barrier((kv_a, places[5]))
    kv_b = project(places[5], cos, sin, plane_hidden, [far_0, far_0x, far_1, far_1x])

    a_near, a_far = up_near(kv_a), up_far(kv_a)
    b_near, b_far = up_near(kv_b), up_far(kv_b)
    own, near_below = [kv_a, kv_b], [a_near, b_near]
    q_partner = [q_y, q_both]
    begun = attend(places[1], starts[0], q_partner, own, tokens, chunk, last=False)
    begun, a_far = lax.optimization_barrier((begun, a_far))
    other = [swap_high(a_far), swap_high(b_far)]
    below = near_below + [a_far, b_far]
    begun = attend(places[4], starts[0], q_partner, below, tokens, chunk, begun, last=False)
    across = attend(places[2], starts[0], q_partner, other, tokens, chunk, begun)
    back = [to_y(across[0]), to_both(across[1])]
    stored = own + below + other
    across, places[3] = lax.optimization_barrier((across, places[3]))
    (beside,) = attend(places[3], starts[2], [q_core], stored, tokens, chunk)
    beside, places[6] = lax.optimization_barrier((beside, places[6]))
    (here,) = attend(places[6], starts[1], [q_own], stored, tokens, chunk)
    halves = [to_core(beside[: rows // 2]), to_core(beside[rows // 2 :])]
    here, halves, back = lax.optimization_barrier((here, halves, back))
    same_y = [here, jnp.concatenate(halves, axis=0)]
    heads = []
    for h in range(KVH):
        mine = jnp.where(h // 2 == c, same_y[0], same_y[1])
        other_y = jnp.where(h // 2 == c, back[0], back[1])
        heads.append(jnp.where(h % 2 == y, mine, other_y))
    return jnp.concatenate(heads, axis=1)


def by_gathers(hidden, queries, kv_weight, doc_ids):
    rows = hidden.shape[0]
    tokens = doc_ids.shape[0]
    me = lax.axis_index("node")
    whole = lax.all_gather(kv_weight, "node", axis=1, tiled=True)
    projected = jnp.dot(hidden, whole, preferred_element_type=jnp.float32)
    split = whole.shape[1] // 2
    cosine, sine = rope_tables(me * rows + jnp.arange(rows))
    keys = projected[:, :split].reshape(rows, KVH, HD)
    a, b = keys[..., : HD // 2], keys[..., HD // 2 :]
    cosine, sine = cosine[:, None, :], sine[:, None, :]
    keys = jnp.concatenate([a * cosine - b * sine, b * cosine + a * sine], axis=-1)
    both = jnp.concatenate([keys, projected[:, split:].reshape(rows, KVH, HD)], axis=1)
    both = both.astype(jnp.bfloat16).transpose(1, 0, 2)
    whole = lax.all_gather(both, "node", axis=1, tiled=True)
    chunk = math.gcd(tokens, 512)
    starts, lowest = attend_starts(doc_ids, [me * rows], rows)
    place = jnp.concatenate([scalars(me * rows, 0, 0), lowest])
    outs = []
    for g in range(KVH):
        pair = [whole[g], whole[KVH + g]]
        mine = queries[:, g * QPK * HD : (g + 1) * QPK * HD]
        outs += attend(place, starts, [mine], pair, tokens, chunk)
    return jnp.concatenate(outs, axis=1)


def solution(mesh):
    planes = mesh.shape["groups"] == 2 and mesh.shape["node"] == 16
    in_specs = (P(AXES, None), P(AXES, None), P(None, "node"), P("groups"))
    return jax.shard_map(
        by_planes if planes else by_gathers,
        mesh=mesh,
        in_specs=in_specs,
        out_specs=P(AXES, None),
        check_vma=False,
    )
```

```python
import math

import jax
import jax.numpy as jnp
import numpy as np
from jax import lax
from jax.experimental import pallas as pl
from jax.experimental.pallas import tpu as pltpu
from jax.sharding import PartitionSpec as P

KVH = 4
QPK = 8
HD = 128
AXES = ("groups", "node")
MASKED = -1e30
EXP2_SCALE = HD ** (-0.5) * math.log2(math.e)
VMEM_LIMIT = 28 * 1024 * 1024

ANY = pl.BlockSpec(memory_space=pl.ANY)
IN_SMEM = pl.BlockSpec(memory_space=pltpu.SMEM)
IN_VMEM = pl.BlockSpec(memory_space=pltpu.VMEM)


def scalars(*values):
    return jnp.stack([jnp.asarray(v).astype(jnp.int32) for v in values])


def rope_tables(positions):
    half = HD // 2
    freqs = 500000.0 ** (-(jnp.arange(half).astype(jnp.float32) * 2.0) / HD)
    angle = positions.astype(jnp.float32)[:, None] * freqs[None, :]
    return jnp.cos(angle), jnp.sin(angle)


def attend_kernel(rows, chunk, n_q, n_kv, resumed, last, place_ref, starts_ref, *refs):
    queries, refs = refs[:n_q], refs[n_q:]
    arrays, refs = refs[: 2 * n_kv], refs[2 * n_kv :]
    state, refs = (refs[:3], refs[3:]) if resumed else ((), refs)
    if last:
        outs, refs = refs[:n_q], refs[n_q:]
        kv, stacked, bias, stat_m, stat_l, acc = refs
    else:
        stat_m, stat_l, acc, kv, stacked, bias = refs
    part_rows = rows // n_q
    chunks = arrays[0].shape[0] // chunk

    if resumed:
        for old, new in zip(state, (stat_m, stat_l, acc)):
            new[...] = old[...]
    else:
        stat_m[...] = jnp.full_like(stat_m, MASKED)
        stat_l[...] = jnp.zeros_like(stat_l)
        acc[...] = jnp.zeros_like(acc)
    for h in range(QPK):
        for i in range(n_q):
            at = h * rows + i * part_rows
            stacked[at : at + part_rows, :] = queries[i][:, h * HD : (h + 1) * HD]
    for i in range(n_kv):
        kind = place_ref[n_q + n_kv + i]
        kv[i, kind] = arrays[2 * i][...]
        kv[i, 1 - kind] = arrays[2 * i + 1][...]

    first_key = place_ref[n_q + 2 * n_kv]
    last_row = place_ref[0]
    for i in range(1, n_q):
        last_row = jnp.maximum(last_row, place_ref[i])
    end_key = last_row + part_rows

    def attend_keys(i, at, begin, size):
        lanes = size // HD
        starts = jnp.concatenate([starts_ref[...]] * lanes, axis=1)
        q_pos = jnp.concatenate(
            [
                place_ref[part] + lax.broadcasted_iota(jnp.int32, (part_rows, size), 0)
                for part in range(n_q)
            ],
            axis=0,
        )
        k_pos = begin + lax.broadcasted_iota(jnp.int32, (rows, size), 1)
        bias[:, :size] = jnp.where((k_pos <= q_pos) & (k_pos >= starts), 0.0, MASKED)
        here = pl.ds(pl.multiple_of(at, size), size)
        score = lax.dot_general(
            stacked[...],
            kv[i, 0, here, :],
            (((1,), (1,)), ((), ())),
            preferred_element_type=jnp.float32,
        )
        score = (score.reshape(QPK, rows, size) + bias[:, :size][None]).reshape(QPK * rows, size)
        old = stat_m[...]
        top = jnp.maximum(old, jnp.max(score, axis=1, keepdims=True))
        expo = jnp.exp2((score - jnp.concatenate([top] * lanes, axis=1)) * EXP2_SCALE)
        factor = jnp.exp2((old - top) * EXP2_SCALE)
        stat_m[...] = top
        sums = expo[:, :HD]
        for lane in range(1, lanes):
            sums = sums + expo[:, lane * HD : (lane + 1) * HD]
        stat_l[...] = stat_l[...] * factor + sums
        part = jnp.dot(
            expo.astype(jnp.bfloat16),
            kv[i, 1, here, :],
            preferred_element_type=jnp.float32,
        )
        acc[...] = acc[...] * factor + part

    @pl.loop(0, n_kv * chunks)
    def _(step):
        i, j = step // chunks, step % chunks
        begin = (place_ref[n_q + i] * chunks + j) * chunk
        middle = begin + chunk // 2
        low = (begin >= 0) & (first_key < middle) & (end_key > begin)
        high = (begin >= 0) & (first_key < begin + chunk) & (end_key > middle)

        @pl.when(low & high)
        def _():
            attend_keys(i, j * chunk, begin, chunk)

        @pl.when(low != high)
        def _():
            half = jnp.where(high, chunk // 2, 0)
            attend_keys(i, j * chunk + half, begin + half, chunk // 2)

    if not last:
        return
    for h in range(QPK):
        at = slice(h * rows, (h + 1) * rows)
        done = acc[at, :] / jnp.sum(stat_l[at, :], axis=1, keepdims=True)
        for i in range(n_q):
            outs[i][:, h * HD : (h + 1) * HD] = done[
                i * part_rows : (i + 1) * part_rows
            ].astype(jnp.bfloat16)


def attend_starts(doc_ids, first_rows, rows):
    docs = [lax.dynamic_slice_in_dim(doc_ids, first, rows) for first in first_rows]
    docs = jnp.concatenate(docs)
    starts = jnp.sum((doc_ids[None, :] < docs[:, None]).astype(jnp.int32), axis=1)
    return jnp.broadcast_to(starts[:, None], (starts.shape[0], HD)), starts[::rows]


def attend(place, starts, queries, arrays, tokens, chunk, state=(), last=True):
    rows = starts.shape[0]
    n_q, n_kv = len(queries), len(arrays) // 2
    part_rows = queries[0].shape[0]
    running = (QPK * rows, HD)
    if last:
        out_shape = [jax.ShapeDtypeStruct((part_rows, QPK * HD), jnp.bfloat16)] * n_q
    else:
        out_shape = [jax.ShapeDtypeStruct(running, jnp.float32)] * 3
    return pl.pallas_call(
        lambda *refs: attend_kernel(rows, chunk, n_q, n_kv, bool(state), last, *refs),
        out_shape=out_shape,
        in_specs=[IN_SMEM] + [IN_VMEM] * (1 + n_q + 2 * n_kv + len(state)),
        out_specs=[IN_VMEM] * len(out_shape),
        scratch_shapes=[
            pltpu.VMEM((n_kv, 2, *arrays[0].shape), jnp.bfloat16),
            pltpu.VMEM((QPK * rows, HD), jnp.bfloat16),
            pltpu.VMEM((rows, chunk), jnp.float32),
        ]
        + [pltpu.VMEM(running, jnp.float32)] * (3 if last else 0),
        compiler_params=pltpu.CompilerParams(vmem_limit_bytes=VMEM_LIMIT),
        cost_estimate=pl.CostEstimate(
            flops=rows * tokens * HD,
            bytes_accessed=rows * tokens,
            transcendentals=0,
        ),
        name="attend",
    )(place, starts, *queries, *arrays, *state)


def project_kernel(rows, n_hidden, n_pieces, place_ref, cos_ref, sin_ref, *refs):
    hidden = refs[:n_hidden]
    pieces = refs[n_hidden : n_hidden + n_pieces]
    out_ref, wbuf = refs[n_hidden + n_pieces :]

    for i in range(n_pieces):
        size = pieces[i].shape[0]

        @pl.when(place_ref[1 + n_hidden + 2 * i] == 1)
        def _():
            at = pl.multiple_of(place_ref[2 + n_hidden + 2 * i], size)
            wbuf[pl.ds(at, size), :] = pieces[i][...]

    heads = lax.dot_general(
        jnp.concatenate([block[...] for block in hidden], axis=0),
        wbuf[...],
        (((1,), (1,)), ((), ())),
        preferred_element_type=jnp.float32,
    )
    for i in range(n_hidden):
        at = pl.ds(pl.multiple_of(place_ref[1 + i] * rows, rows), rows)
        head = heads[i * rows : (i + 1) * rows]
        turned = head * cos_ref[at, :] + pltpu.roll(head, HD // 2, 1) * sin_ref[at, :]
        out_ref[at, :] = jnp.where(place_ref[0] == 1, turned, head).astype(jnp.bfloat16)


def project(place, cos, sin, hidden, pieces):
    rows, depth = hidden[0].shape
    n = len(hidden)
    return pl.pallas_call(
        lambda *refs: project_kernel(rows, n, len(pieces), *refs),
        out_shape=jax.ShapeDtypeStruct((n * rows, HD), jnp.bfloat16),
        in_specs=[IN_SMEM] + [IN_VMEM] * (2 + n + len(pieces)),
        out_specs=IN_VMEM,
        scratch_shapes=[pltpu.VMEM((HD, depth), jnp.bfloat16)],
        compiler_params=pltpu.CompilerParams(vmem_limit_bytes=VMEM_LIMIT),
        cost_estimate=pl.CostEstimate(
            flops=rows * depth * HD,
            bytes_accessed=rows * depth,
            transcendentals=0,
        ),
        name="project",
    )(place, cos, sin, *hidden, *pieces)


def by_planes(hidden, queries, kv_weight, doc_ids):
    rows = hidden.shape[0]
    tokens = doc_ids.shape[0]
    width = kv_weight.shape[1]
    part = width // 2
    columns = QPK * HD
    x = lax.axis_index("groups")
    node = lax.axis_index("node")
    z, y, c = node // 4, (node // 2) % 2, node % 2

    def hop(fn):
        pairs = []
        for i in range(32):
            to = fn(i // 16, (i // 4) % 4, (i // 2) % 2, i % 2)
            if to is not None:
                pairs.append((i, ((to[0] * 4 + to[1]) * 2 + to[2]) * 2 + to[3]))
        return lambda v: lax.ppermute(v, AXES, pairs)

    to_core = hop(lambda x, z, y, c: (x, z, y, 1 - c))
    to_y = hop(lambda x, z, y, c: (x, z, 1 - y, c))
    to_both = hop(lambda x, z, y, c: (x, z, 1 - y, 1 - c))
    to_x = hop(lambda x, z, y, c: (1 - x, z, y, c))
    near = hop(lambda x, z, y, c: (x, z ^ 1, y, c))
    far = hop(lambda x, z, y, c: (x, z ^ (2 + c), y, z % 2))
    up_near = hop(lambda x, z, y, c: (x, z + 1, y, c) if z % 2 == 0 else None)
    up_far = hop(lambda x, z, y, c: (x, z + 2, y, c) if z < 2 else None)
    swap_high = hop(lambda x, z, y, c: (x, z ^ 1, y, c) if z >= 2 else None)

    chunk = math.gcd(tokens, 512)
    tables = [[] for _ in range(7)]
    for i in range(32):
        ix, iz, iy, ic = i // 16, (i // 4) % 4, (i // 2) % 2, i % 2
        blocks = [2 * iy + ic, 2 * iy + 1 - ic, 2 * (1 - iy) + ic, 2 * (1 - iy) + 1 - ic]
        own = int(ic == iz % 2)
        tables[0].append(
            [int(iz < 2), *blocks]
            + [own, ic * width, 1 - own, ic * width, 1, (1 - ic) * width]
        )
        side = (1 - own) * width
        tables[5].append(
            [int(iz >= 2), *blocks]
            + [1, side + ix * part, 1, side + (1 - ix) * part]
            + [1, width - side + ix * part, 1, width - side + (1 - ix) * part]
        )
        planes = [iz, iz - 1 if iz % 2 else -1, iz - 2, (iz ^ 1) - 2 if iz >= 2 else -1]
        calls = [(1, 1 - iy, planes[:1]), (2, 1 - iy, planes[3:])]
        calls += [(3, iy, planes), (4, 1 - iy, planes[1:3]), (6, iy, planes)]
        for at, iy_rows, some in calls:
            cores = {3: [1 - ic], 6: [ic]}.get(at, [ic, 1 - ic])
            first = [(4 * iz + 2 * iy_rows + core) * rows for core in cores]
            kinds = [max(plane, 0) // 2 for plane in some]
            tables[at].append(first + some + kinds)
    widths = [len(t[0]) for t in tables]
    whole = np.concatenate([np.asarray(t, np.int32) for t in tables], axis=1)
    place = lax.dynamic_slice_in_dim(jnp.asarray(whole), x * 16 + node, 1, 0)[0]
    at, places = 0, []
    for w in widths:
        places.append(place[at : at + w])
        at += w

    weight = kv_weight.T
    far_0 = far(lax.dynamic_slice_in_dim(weight, x * part, part, 0))
    near_0 = near(weight)
    hidden_y = to_y(hidden)
    hidden_c = to_core(hidden)

    positions = z * 4 * rows + jnp.arange(4 * rows)
    cosine, sine = rope_tables(positions)
    cos = jnp.concatenate([cosine, cosine], axis=1)
    sin = jnp.concatenate([-sine, sine], axis=1)
    firsts = [
        [(4 * z + 2 * (1 - y) + c) * rows, (4 * z + 2 * (1 - y) + 1 - c) * rows],
        [(4 * z + 2 * y + c) * rows, (4 * z + 2 * y + 1 - c) * rows],
    ]
    starts, lowest = zip(*[attend_starts(doc_ids, first, rows) for first in firsts])
    starts = [starts[0], starts[1][:rows], starts[1][rows:]]
    both = jnp.minimum(lowest[0][:1], lowest[0][1:])
    lows = ((1, both), (2, both), (3, lowest[1][1:]), (4, both), (6, lowest[1][:1]))
    for at, low in lows:
        places[at] = jnp.concatenate([places[at], low])
    q_own, *q_away = [
        lax.dynamic_slice_in_dim(queries, h * columns, columns, 1)
        for h in (y + 2 * c, y + 2 * (1 - c), 1 - y + 2 * c, 1 - y + 2 * (1 - c))
    ]
    far_0, cos, sin, starts, places, q_own, q_away = lax.optimization_barrier(
        (far_0, cos, sin, starts, places, q_own, q_away)
    )
    far_1, far_0x = near(far_0), to_x(far_0)
    far_1, far_0x = lax.optimization_barrier((far_1, far_0x))
    far_1x = to_x(far_1)
    near_c = to_core(jnp.where(c == z % 2, near_0, weight))
    q_core = to_core(q_away[0])
    hidden_y, far_1, q_away, q_core = lax.optimization_barrier((hidden_y, far_1, q_away, q_core))
    hidden_yc = to_core(hidden_y)
    q_y, q_both = to_y(q_away[1]), to_both(q_away[2])

    plane_hidden = [hidden, hidden_c, hidden_y, hidden_yc]
    kv_a = project(places[0], cos, sin, plane_hidden, [weight, near_0, near_c])
    kv_a, places[5] = lax.optimization_barrier((kv_a, places[5]))
    kv_b = project(places[5], cos, sin, plane_hidden, [far_0, far_0x, far_1, far_1x])

    a_near, a_far = up_near(kv_a), up_far(kv_a)
    b_near, b_far = up_near(kv_b), up_far(kv_b)
    own, near_below = [kv_a, kv_b], [a_near, b_near]
    q_partner = [q_y, q_both]
    begun = attend(places[1], starts[0], q_partner, own, tokens, chunk, last=False)
    begun, a_far = lax.optimization_barrier((begun, a_far))
    other = [swap_high(a_far), swap_high(b_far)]
    below = near_below + [a_far, b_far]
    begun = attend(places[4], starts[0], q_partner, below, tokens, chunk, begun, last=False)
    across = attend(places[2], starts[0], q_partner, other, tokens, chunk, begun)
    back = [to_y(across[0]), to_both(across[1])]
    stored = own + below + other
    across, places[3] = lax.optimization_barrier((across, places[3]))
    (beside,) = attend(places[3], starts[2], [q_core], stored, tokens, chunk)
    beside, places[6] = lax.optimization_barrier((beside, places[6]))
    (here,) = attend(places[6], starts[1], [q_own], stored, tokens, chunk)
    halves = [to_core(beside[: rows // 2]), to_core(beside[rows // 2 :])]
    here, halves, back = lax.optimization_barrier((here, halves, back))
    same_y = [here, jnp.concatenate(halves, axis=0)]
    heads = []
    for h in range(KVH):
        mine = jnp.where(h // 2 == c, same_y[0], same_y[1])
        other_y = jnp.where(h // 2 == c, back[0], back[1])
        heads.append(jnp.where(h % 2 == y, mine, other_y))
    return jnp.concatenate(heads, axis=1)


def by_gathers(hidden, queries, kv_weight, doc_ids):
    rows = hidden.shape[0]
    tokens = doc_ids.shape[0]
    me = lax.axis_index("node")
    whole = lax.all_gather(kv_weight, "node", axis=1, tiled=True)
    projected = jnp.dot(hidden, whole, preferred_element_type=jnp.float32)
    split = whole.shape[1] // 2
    cosine, sine = rope_tables(me * rows + jnp.arange(rows))
    keys = projected[:, :split].reshape(rows, KVH, HD)
    a, b = keys[..., : HD // 2], keys[..., HD // 2 :]
    cosine, sine = cosine[:, None, :], sine[:, None, :]
    keys = jnp.concatenate([a * cosine - b * sine, b * cosine + a * sine], axis=-1)
    both = jnp.concatenate([keys, projected[:, split:].reshape(rows, KVH, HD)], axis=1)
    both = both.astype(jnp.bfloat16).transpose(1, 0, 2)
    whole = lax.all_gather(both, "node", axis=1, tiled=True)
    chunk = math.gcd(tokens, 512)
    starts, lowest = attend_starts(doc_ids, [me * rows], rows)
    place = jnp.concatenate([scalars(me * rows, 0, 0), lowest])
    outs = []
    for g in range(KVH):
        pair = [whole[g], whole[KVH + g]]
        mine = queries[:, g * QPK * HD : (g + 1) * QPK * HD]
        outs += attend(place, starts, [mine], pair, tokens, chunk)
    return jnp.concatenate(outs, axis=1)


def solution(mesh):
    planes = mesh.shape["groups"] == 2 and mesh.shape["node"] == 16
    in_specs = (P(AXES, None), P(AXES, None), P(None, "node"), P("groups"))
    return jax.shard_map(
        by_planes if planes else by_gathers,
        mesh=mesh,
        in_specs=in_specs,
        out_specs=P(AXES, None),
        check_vma=False,
    )
```
